32 devices in a mesh: fsdp: 8 (over y, x, core), ctx: 4 (over z).
Axes of the slice: x: 2, y: 2, z: 4, core: 2. Of those that a mesh axis runs over, the one named last changes fastest.
Arguments:
- inputs: bfloat16 [8, 2, 1024, 896], P('fsdp', None, 'ctx'), may hold values from -40 to 40
- cotangent: bfloat16 [8, 2, 1024, 896], P('fsdp', None, 'ctx'), may hold values from -6 to 6
- lengths: int32 [8, 2, 4], P('fsdp'), may hold values from 1 to 960, 1024 in all within a row
- order: int32 [8, 2, 8], P('fsdp'), may hold values from 0 to 7, each once within a row
- w_qkv: bfloat16 [896, 1152], P('fsdp'), may hold values from -0.1875 to 0.1875
- b_qkv: bfloat16 [1152], P('fsdp'), may hold values from -3 to 3
- w_out: bfloat16 [896, 896], P('fsdp'), may hold values from -3 to 3
- norm_attn: bfloat16 [896], P('fsdp'), may hold values from 0.25 to 1.75
- norm_mlp: bfloat16 [896], P('fsdp'), may hold values from 0.25 to 1.75
- w_gate_up: bfloat16 [896, 9728], P('fsdp'), may hold values from -0.1875 to 0.1875
- w_down: bfloat16 [4864, 896], P('fsdp'), may hold values from -0.078125 to 0.078125
Outputs:
- outputs: bfloat16 [8, 2, 1024, 896], P('fsdp', None, 'ctx')
- d_inputs: float32 [8, 2, 1024, 896], P('fsdp', None, 'ctx')
- grad_w_qkv: float32 [896, 1152], P('fsdp')
- grad_b_qkv: float32 [1024], P('fsdp')
- grad_b_v: float32 [128], P('fsdp')
- grad_w_out: float32 [896, 896], P('fsdp')
- grad_norm_attn: float32 [896], P('fsdp')
- grad_norm_mlp: float32 [896], P('fsdp')
- grad_w_gate_up: float32 [896, 9728], P('fsdp')
- grad_w_down: float32 [4864, 896], P('fsdp')
The draws below stay inside these ranges and needn't reach their ends.
Inputs may be any that keep to these rules, and one draw needn't show every extreme that they name: Each row of 4 lengths sums to 1024. `order`: each row holds every block number once.
All inputs are finite; a program needn't handle non-finite values.
Results may differ from the reference program's by a relative error of at most 0.02.
Values may be sent and summed in bfloat16 or wider, within the bound.
A program may use at most 320 MiB of HBM per device.

```python
import math
import jax
import jax.numpy as jnp
import numpy as np
from jax import lax

D = 896
HQ = 14
KVH = 2
HD = 64
FF = 4864
TOK_DEV = 256
MICRO = 2
NSEQ = 4
GROUP = 7
QW = 896
KW = 128
FW = 1152
BLOCK = 128
MB = 1024
NBLK = 8
QBLOCK = 512
N_FSDP = 8


def draw_inputs(key, part):
    key = jax.random.fold_in(key, 11)
    row_key, col_key, base_key = jax.random.split(key, 3)
    full_shape = (N_FSDP, MICRO, MB, D)
    row_scale = jnp.exp(jax.random.uniform(row_key, (N_FSDP, MICRO, MB, 1), jnp.float32, minval=math.log(0.3), maxval=math.log(3.0)))
    col_scale = jnp.exp(jax.random.uniform(col_key, (1, 1, 1, D), jnp.float32, minval=math.log(0.5), maxval=math.log(2.0)))
    base_draw = jax.random.normal(base_key, full_shape, jnp.float32)
    return jnp.clip(base_draw * row_scale * col_scale, -40.0, 40.0).astype(jnp.bfloat16)


def block_scale(key, dims, cuts, smallest, largest):
    factor_of, own = 1.0, jax.random.fold_in(key, 6)
    for axis_at, blocks in cuts:
        draws = jnp.exp(jax.random.uniform(jax.random.fold_in(own, axis_at), (blocks,), jnp.float32, smallest / len(cuts), largest / len(cuts)))
        factor_of = factor_of * jnp.repeat(draws, dims[axis_at] // blocks).reshape([-1 if axis == axis_at else 1 for axis in range(len(dims))])
    return factor_of


def split_up(number_of, total, limit, lean):
    weights = [(1 << 20) // math.isqrt(standing ** lean) + 1 for standing in range(2, number_of + 1)]
    spare, holding = total - limit - (number_of - 1), [1] * (number_of - 1)
    while spare > 0:
        free = [i for i in range(number_of - 1) if holding[i] < limit]
        whole, budget = sum([weights[i] for i in free]), spare
        for i in free:
            extra = min(limit - holding[i], max(1, budget * weights[i] // whole), spare)
            holding[i] = holding[i] + extra
            spare = spare - extra
    return np.array([limit] + holding)


def uneven_parts(rng, amount, total, reach, skew):
    if amount == 2:
        one = jax.random.randint(rng, (), max(1, total - reach), min(reach, total - 1) + 1)
        return jnp.stack([one, total - one])
    tallies = jnp.asarray(split_up(amount, total, reach, skew), jnp.int32)
    pairs = (amount - 1) // 2
    giver, taker = tallies[1:1 + 2 * pairs:2], tallies[2:2 + 2 * pairs:2]
    room = jnp.minimum(giver - 1, reach - taker)
    moved = jax.random.randint(jax.random.fold_in(rng, 1), (pairs,), 0, 1 << 20) % (room + 1)
    tallies = tallies.at[1:1 + 2 * pairs:2].set(giver - moved).at[2:2 + 2 * pairs:2].set(taker + moved)
    return tallies[jax.random.permutation(jax.random.fold_in(rng, 2), amount)]


def bell_draw(own_key, shape, spread, limit, pieces=(), held_as=jnp.bfloat16):
    drawn = jax.random.normal(own_key, shape, jnp.float32) * spread
    if len(pieces) > 0:
        drawn = block_scale(own_key, shape, pieces, -0.22, 0.18) * drawn
    return jnp.clip(drawn, min=-limit, max=limit).astype(held_as)


def setup_inputs(seed: int = 0) -> dict:
    seeds = jax.random.split(jax.random.key(seed), 12)
    return {
        "inputs": draw_inputs(jax.random.fold_in(seeds[11], 71), 0),
        "cotangent": bell_draw(seeds[1], (N_FSDP, MICRO, MB, D), 1.0, 6.0, ((0, 8), (2, 4))),
        "lengths": jax.vmap(lambda own: uneven_parts(own, NSEQ, MB, MB - TOK_DEV // 4, 2))(jax.random.split(seeds[2], N_FSDP * MICRO)).reshape((N_FSDP, MICRO, NSEQ)).astype(jnp.int32),
        "order": jax.vmap(lambda own: jax.random.permutation(own, NBLK))(jax.random.split(seeds[3], N_FSDP * MICRO)).reshape((N_FSDP, MICRO, NBLK)).astype(jnp.int32),
        "w_qkv": bell_draw(seeds[4], (D, FW), D ** -0.5, 0.1875, ((0, 8),)),
        "b_qkv": bell_draw(seeds[5], (FW,), 0.5, 3.0, ((0, 8),)),
        "w_out": bell_draw(seeds[6], (QW, D), 4 ** -0.5, 3.0, ((0, 8),)),
        "norm_attn": jnp.clip(1.0 + 0.15 * jax.random.normal(seeds[7], (D,), jnp.float32), 0.25, 1.75).astype(jnp.bfloat16),
        "norm_mlp": jnp.clip(1.0 + 0.15 * jax.random.normal(seeds[8], (D,), jnp.float32), 0.25, 1.75).astype(jnp.bfloat16),
        "w_gate_up": bell_draw(seeds[9], (D, 2 * FF), D ** -0.5, 0.1875, ((0, 8),)),
        "w_down": bell_draw(seeds[10], (FF, D), FF ** -0.5, 0.078125, ((0, 8),)),
    }


@jax.custom_vjp
def low(v):
    return lax.optimization_barrier(v.astype(jnp.bfloat16)).astype(jnp.float32)

@jax.custom_vjp
def low_back(v):
    return v

def low_keep(v):
    return (low(v), None)

def low_pass(kept, grad):
    return (grad,)

def back_keep(v):
    return (v, None)

def back_low(kept, grad):
    return (low(grad),)
low.defvjp(low_keep, low_pass)
low_back.defvjp(back_keep, back_low)
EPSILON = 1e-06
ROPE_BASE = 1000000.0
NEGATIVE = -1e+30
PRECISE = lax.Precision.HIGHEST

def token_places(order_one, lengths_one, first_row, row_count, block_rows):
    stored = first_row + jnp.arange(row_count, dtype=jnp.int32)
    block_ids = (stored // block_rows).astype(jnp.int32)
    numbers = jnp.arange(order_one.shape[0], dtype=jnp.int32)
    chosen = lax.optimization_barrier(jnp.sum(jnp.where(block_ids[:, None] == numbers[None, :], order_one[None, :], 0), axis=1)).astype(jnp.int32)
    natural = (chosen * block_rows + stored % block_rows).astype(jnp.int32)
    ends = jnp.cumsum(lengths_one).astype(jnp.int32)
    passed = (ends[None, :] <= natural[:, None]).astype(jnp.int32)
    segment = lax.optimization_barrier(jnp.sum(passed, axis=1)).astype(jnp.int32)
    begin = lax.optimization_barrier(jnp.sum(passed * lengths_one[None, :], axis=1)).astype(jnp.int32)
    return (natural, segment, (natural - begin).astype(jnp.int32))

def rope_tables(position, head_dim):
    half_dim = head_dim // 2
    freqs = jnp.power(jnp.float32(ROPE_BASE), -(jnp.arange(half_dim, dtype=jnp.float32) * (2.0 / head_dim)))
    angle = position.astype(jnp.float32)[:, None] * freqs[None, :]
    cosine_table = jnp.cos(angle)
    sine_table = jnp.sin(angle)
    cosine_full = jnp.concatenate([cosine_table, cosine_table], axis=1)[:, None, :]
    sine_full = jnp.concatenate([sine_table, sine_table], axis=1)[:, None, :]
    return (cosine_full, sine_full)

def rotate_forward(vectors, cosine_full, sine_full):
    half_dim = vectors.shape[-1] // 2
    swapped = jnp.concatenate([-vectors[..., half_dim:], vectors[..., :half_dim]], axis=-1)
    return vectors * cosine_full + swapped * sine_full

def attend(query_block, query_nat, query_seg, key_heads, value_heads, key_nat, key_seg):
    rows_here = query_block.shape[0]
    grouped = query_block.reshape(rows_here, KVH, GROUP, HD)
    raw_scores = jnp.einsum('tgjd,kgd->gjtk', grouped, key_heads, precision=PRECISE) * (1.0 / math.sqrt(HD))
    scores = low_back(raw_scores)
    allowed = (query_seg[:, None] == key_seg[None, :]) & (key_nat[None, :] <= query_nat[:, None])
    masked = jnp.where(allowed[None, None], scores, NEGATIVE)
    row_top = lax.optimization_barrier(jnp.max(masked, axis=-1, keepdims=True))
    log_total = row_top + jnp.log(lax.optimization_barrier(jnp.sum(jnp.exp(masked - row_top), axis=-1, keepdims=True)))
    probs_low = low(jnp.exp(masked - log_total))
    mixed = jnp.einsum('gjtk,kgd->tgjd', probs_low, value_heads, precision=PRECISE)
    return mixed.reshape(rows_here, QW)

def block_forward(stream, params, lengths_one, order_one):
    w_qkv, b_qkv, w_out, gain_attn, gain_mlp, w_gate_up, w_down = params
    natural, segment, position = token_places(order_one, lengths_one, 0, MB, BLOCK)
    cosine_full, sine_full = rope_tables(position, HD)
    inv_attn = lax.rsqrt(lax.optimization_barrier(jnp.mean(stream * stream, axis=1, keepdims=True)) + EPSILON)
    hn_attn = low(stream * inv_attn * gain_attn)
    project = low_back(jnp.dot(hn_attn, w_qkv, precision=PRECISE) + b_qkv)
    queries = low(rotate_forward(project[:, :QW].reshape(MB, HQ, HD), cosine_full, sine_full))
    key_heads = low(rotate_forward(project[:, QW:QW + KW].reshape(MB, KVH, HD), cosine_full, sine_full))
    value_heads = low(project[:, QW + KW:].reshape(MB, KVH, HD))
    saved_attend = jax.checkpoint(attend)
    blocks = MB // QBLOCK
    mixed = lax.map(lambda element: saved_attend(element[0], element[1], element[2], key_heads, value_heads, natural, segment), (queries.reshape(blocks, QBLOCK, HQ, HD), natural.reshape(blocks, QBLOCK), segment.reshape(blocks, QBLOCK)))
    attended = low(low_back(mixed.reshape(MB, QW)))
    stream_mid = stream + low_back(jnp.dot(attended, w_out, precision=PRECISE))
    inv_mlp = lax.rsqrt(lax.optimization_barrier(jnp.mean(stream_mid * stream_mid, axis=1, keepdims=True)) + EPSILON)
    hn_mlp = low(stream_mid * inv_mlp * gain_mlp)
    gate_up = low_back(jnp.dot(hn_mlp, w_gate_up, precision=PRECISE))
    hidden = low(jax.nn.silu(gate_up[:, :FF]) * gate_up[:, FF:])
    return stream_mid + low_back(jnp.dot(hidden, w_down, precision=PRECISE))

def reference(inputs, cotangent, lengths, order, w_qkv, b_qkv, w_out, norm_attn, norm_mlp, w_gate_up, w_down):
    batches = N_FSDP * MICRO
    streams = inputs.reshape(batches, MB, D).astype(jnp.float32)
    lengths_all = lengths.reshape(batches, NSEQ).astype(jnp.int32)
    order_all = order.reshape(batches, NBLK).astype(jnp.int32)
    params = tuple((weight_one.astype(jnp.float32) for weight_one in (w_qkv, b_qkv, w_out, norm_attn, norm_mlp, w_gate_up, w_down)))
    saved_layer = jax.checkpoint(block_forward)

    def forward(stream_all, param_all):

        def advance(carried, element):
            return (carried, saved_layer(element[0], param_all, element[1], element[2]))
        carried_end, results = lax.scan(advance, jnp.zeros((), jnp.float32), (stream_all, lengths_all, order_all))
        return results
    results, pullback = jax.vjp(forward, streams, params)
    grad_streams, grad_params = pullback(cotangent.reshape(batches, MB, D).astype(jnp.float32))
    outputs = results.reshape(N_FSDP, MICRO, MB, D).astype(jnp.bfloat16)
    d_inputs = grad_streams.reshape(N_FSDP, MICRO, MB, D).astype(jnp.float32)
    bias_grad = grad_params[1].astype(jnp.float32)
    return (outputs, d_inputs, grad_params[0].astype(jnp.float32), bias_grad[:QW + KW], bias_grad[QW + KW:], grad_params[2].astype(jnp.float32), grad_params[3].astype(jnp.float32), grad_params[4].astype(jnp.float32), grad_params[5].astype(jnp.float32), grad_params[6].astype(jnp.float32))
```

```python
import functools
import math

import jax
import jax.numpy as jnp
import numpy as np
from jax import lax
from jax.experimental import pallas as pl
from jax.experimental.pallas import tpu as pltpu
from jax.sharding import PartitionSpec as P

HQ = 14
KVH = 2
HD = 64
EPSILON = 1e-06
ROPE_BASE = 1000000.0
NEGATIVE = -1e30
TP = 4
LANES = 128
CHUNK = 256
BF = jnp.bfloat16
F32 = jnp.float32
MESH = pl.DeviceIdType.MESH
VMEM_LIMIT = 60 * 1024 * 1024


def flip1(v):
    return v + 1 - 2 * (v % 2)


def flip2(v):
    return v + 2 - 4 * ((v // 2) % 2)


def dot(a, b):
    return jnp.dot(a, b, preferred_element_type=F32)


def dot_nt(a, b):
    return lax.dot_general(a, b, (((1,), (1,)), ((), ())), preferred_element_type=F32)


class Links:
    def __init__(self, send_sems, recv_sems):
        self.send_sems, self.recv_sems = send_sems, recv_sems
        self.started = []

    def put(self, src, dst, device):
        at = len(self.started)
        copy = pltpu.make_async_remote_copy(
            src_ref=src,
            dst_ref=dst,
            send_sem=self.send_sems.at[at],
            recv_sem=self.recv_sems.at[at],
            device_id=device,
            device_id_type=MESH,
        )
        copy.start()
        self.started.append((copy, device))
        return at

    def arrive(self, at, slot):
        pltpu.make_async_remote_copy(
            src_ref=slot,
            dst_ref=slot,
            send_sem=self.send_sems.at[at],
            recv_sem=self.recv_sems.at[at],
            device_id=self.started[at][1],
            device_id_type=MESH,
        ).wait_recv()

    def drain(self):
        for copy, _ in self.started:
            copy.wait_send()


def enter(devices):
    barrier = pltpu.get_barrier_semaphore()
    for device in devices:
        pl.semaphore_signal(barrier, inc=1, device_id=device, device_id_type=MESH)
    pl.semaphore_wait(barrier, len(devices))


def gather_kernel(
    n, wq, wo, sm, wgu, wd, gd, wq_all, wo_all, sm_all, wgu_t, wd_t, gd_all, send, recv, here
):
    replicas = n // TP
    f, c = lax.axis_index("fsdp"), lax.axis_index("ctx")
    t, r = f % TP, f // TP
    sib, par, cross = (flip1(f), c), (flip2(f), c), (flip2(flip1(f)), c)
    peers = [((f + TP * j) % n, c) for j in range(1, replicas)]
    back = [(f - TP * j + n) % n for j in range(1, replicas)]
    rback = [(r - j + replicas) % replicas for j in range(1, replicas)]
    enter([sib, par, cross] + peers)
    links = Links(send, recv)
    local = []

    def keep(src, dst):
        copy = pltpu.make_async_copy(src, dst, here.at[len(local)])
        copy.start()
        local.append(copy)

    pending = []
    both = []
    for own, every in ((wq, wq_all), (wo, wo_all), (sm, sm_all)):
        ys = [links.put(own, every.at[f], peer) for peer in peers]
        x = links.put(own, every.at[f], par)
        s = links.put(own, every.at[f], sib)
        keep(own, every.at[f])
        both.append((every, ys, x, s))
    gd_x = links.put(gd, gd_all.at[t], par)
    gd_s = links.put(gd, gd_all.at[t], sib)
    keep(gd, gd_all.at[t])
    gu_s = links.put(wgu.at[flip1(t)], wgu_t.at[r, t], sib)
    gu_x = links.put(wgu.at[flip2(t)], wgu_t.at[r, t], par)
    gu_c = links.put(wgu.at[flip2(flip1(t))], wgu_t.at[r, t], cross)
    keep(wgu.at[t], wgu_t.at[r, t])
    for j, peer in enumerate(peers):
        at = links.put(wgu.at[t], wgu_t.at[r, t], peer)
        pending.append((at, wgu_t.at[rback[j], t]))
        at = links.put(wd, wd_t.at[r], peer)
        pending.append((at, wd_t.at[rback[j]]))
    keep(wd, wd_t.at[r])
    later = []
    for every, ys, x, s in both:
        pending.append((s, every.at[flip1(f)]))
        for j, at in enumerate(ys):
            links.arrive(at, every.at[back[j]])
            at_x = links.put(every.at[back[j]], every.at[back[j]], par)
            later.append((every, at_x, flip2(back[j])))
            at_s = links.put(every.at[back[j]], every.at[back[j]], sib)
            pending.append((at_s, every.at[flip1(back[j])]))
        links.arrive(x, every.at[flip2(f)])
        at_s = links.put(every.at[flip2(f)], every.at[flip2(f)], sib)
        pending.append((at_s, every.at[flip2(flip1(f))]))
    for at, other in ((gu_s, flip1(t)), (gu_x, flip2(t)), (gu_c, flip2(flip1(t)))):
        links.arrive(at, wgu_t.at[r, other])
        for j, peer in enumerate(peers):
            at_y = links.put(wgu_t.at[r, other], wgu_t.at[r, other], peer)
            pending.append((at_y, wgu_t.at[rback[j], other]))
    for every, at, slot in later:
        links.arrive(at, every.at[slot])
        at_s = links.put(every.at[slot], every.at[slot], sib)
        pending.append((at_s, every.at[flip1(slot)]))
    links.arrive(gd_x, gd_all.at[flip2(t)])
    at_s = links.put(gd_all.at[flip2(t)], gd_all.at[flip2(t)], sib)
    pending.append((at_s, gd_all.at[flip2(flip1(t))]))
    pending.append((gd_s, gd_all.at[flip1(t)]))
    for at, slot in pending:
        links.arrive(at, slot)
    links.drain()
    for copy in local:
        copy.wait()


def gather_weights(n, wq, wo, sm, wgu, wd, gd):
    replicas = n // TP
    copies = 3 * ((replicas - 1) * 4 + 3) + 3 + (replicas - 1) * 5 + 3
    anywhere = pl.BlockSpec(memory_space=pl.ANY)
    shapes = (
        jax.ShapeDtypeStruct((n,) + wq.shape, BF),
        jax.ShapeDtypeStruct((n,) + wo.shape, BF),
        jax.ShapeDtypeStruct((n,) + sm.shape, BF),
        jax.ShapeDtypeStruct((replicas,) + wgu.shape, BF),
        jax.ShapeDtypeStruct((replicas,) + wd.shape, BF),
        jax.ShapeDtypeStruct((TP,) + gd.shape, BF),
    )
    return pl.pallas_call(
        functools.partial(gather_kernel, n),
        out_shape=shapes,
        in_specs=[anywhere] * 6,
        out_specs=[anywhere] * 6,
        scratch_shapes=[
            pltpu.SemaphoreType.DMA((copies,)),
            pltpu.SemaphoreType.DMA((copies,)),
            pltpu.SemaphoreType.DMA((6,)),
        ],
        compiler_params=pltpu.CompilerParams(collective_id=0, has_side_effects=True),
        name="gather_weights",
    )(wq, wo, sm, wgu, wd, gd)


def begin_of(natural, lens, m, count):
    begin = jnp.zeros_like(natural)
    end = jnp.int32(0)
    for j in range(count):
        piece = lens[m, j]
        end = end + piece
        begin = begin + jnp.where(end <= natural, piece, 0)
    return begin


def fill_tables(m, rows, c, freq, order, lens, cos_ref, sin_ref):
    block = rows // 2
    lane = lax.broadcasted_iota(jnp.int32, (block, LANES), 1)
    low = (lane % HD) < (HD // 2)
    for b in range(2):
        natural = order[m, c * 2 + b] * block + lax.broadcasted_iota(
            jnp.int32, (block, LANES), 0
        )
        position = natural - begin_of(natural, lens, m, lens.shape[1])
        angle = position.astype(F32) * freq[0:1, :]
        at = m * rows + b * block
        cos_ref[at : at + block, :] = jnp.cos(angle)
        sine = jnp.sin(angle)
        sin_ref[at : at + block, :] = jnp.where(low, -sine, sine)


def swap_halves(u):
    lane = lax.broadcasted_iota(jnp.int32, u.shape, 1)
    low = (lane % HD) < (HD // 2)
    return jnp.where(low, pltpu.roll(u, LANES - HD // 2, 1), pltpu.roll(u, HD // 2, 1))


def fill_bias(m, rows, c, order, lens, bias_ref):
    block = rows // 2
    lane = lax.broadcasted_iota(jnp.int32, (1, rows), 1)
    query = jnp.where(
        lane < block,
        order[m, c * 2] * block + lane,
        order[m, c * 2 + 1] * block + lane - block,
    )
    begin = begin_of(query, lens, m, lens.shape[1])

    def body(k, carry):
        key = order[m, k] * block + lax.broadcasted_iota(jnp.int32, (block, rows), 0)
        allowed = (key <= query) & (key >= begin)
        at = pl.multiple_of(k * block, block)
        bias_ref[pl.ds(at, block), :] = jnp.where(allowed, 0.0, NEGATIVE)
        return carry

    lax.fori_loop(0, order.shape[1], body, 0)


def fill_heads(whole, var_ref):
    rolled = pltpu.roll(whole, HD, 1)
    low = lax.broadcasted_iota(jnp.int32, whole.shape, 1) < HD
    var_ref[0, 0] = jnp.where(low, whole, 0.0).astype(BF)
    var_ref[0, 1] = jnp.where(low, 0.0, rolled).astype(BF)
    var_ref[1, 0] = jnp.where(low, rolled, 0.0).astype(BF)
    var_ref[1, 1] = jnp.where(low, 0.0, whole).astype(BF)


def fill_heads_turned(whole, var_ref):
    turned = whole.T
    rolled = jnp.concatenate([turned[HD:], turned[:HD]], axis=0)
    low = lax.broadcasted_iota(jnp.int32, turned.shape, 0) < HD
    var_ref[0, 0] = jnp.where(low, turned, 0.0).astype(BF)
    var_ref[0, 1] = jnp.where(low, 0.0, rolled).astype(BF)
    var_ref[1, 0] = jnp.where(low, rolled, 0.0).astype(BF)
    var_ref[1, 1] = jnp.where(low, 0.0, turned).astype(BF)


def inverse_norm(v):
    return lax.rsqrt(jnp.mean(v * v, axis=1, keepdims=True) + EPSILON)


def forward_kernel(
    size, order, lens, x, wq, wo, bias_qkv, gain_attn, gain_mlp, freq,
    h2, x2, qs, kv, lse, obt,
    cos_ref, sin_ref, bias_ref, kvar, vvar, ob, land, send, recv, out_sem,
):
    micro, rows, ctx = size
    group = HQ // KVH
    pairs = HQ // 2
    width = HQ * HD
    f, c = lax.axis_index("fsdp"), lax.axis_index("ctx")
    others = [(f, (c + j) % ctx) for j in range(1, ctx)]
    back = [(c - j + ctx) % ctx for j in range(1, ctx)]
    enter(others)
    links = Links(send, recv)
    arrivals = []
    for m in range(micro):
        fill_tables(m, rows, c, freq, order, lens, cos_ref, sin_ref)
    for m in range(micro):
        stream = x[m].astype(F32)
        h1 = (stream * inverse_norm(stream) * gain_attn[...]).astype(BF)
        project = dot(h1, wq[...]) + bias_qkv[...]
        cosine = cos_ref[m * rows : (m + 1) * rows, :]
        sine = sin_ref[m * rows : (m + 1) * rows, :]
        keys = project[:, width : width + LANES]
        keys = keys * cosine + swap_halves(keys) * sine
        land[m, c, :, :LANES] = keys.astype(BF)
        land[m, c, :, LANES:] = project[:, width + LANES :].astype(BF)
        arrivals.append([links.put(land.at[m, c], land.at[m, c], other) for other in others])
        for p in range(pairs):
            query = project[:, p * LANES : (p + 1) * LANES]
            query = query * cosine + swap_halves(query) * sine
            qs[m, p] = (query.astype(BF).astype(F32) * (1.0 / math.sqrt(HD))).astype(BF)
    out_copies = []
    for m in range(micro):
        fill_bias(m, rows, c, order, lens, bias_ref)
        for at, source in zip(arrivals[m], back):
            links.arrive(at, land.at[m, source])
        copy = pltpu.make_async_copy(land.at[m], kv.at[m], out_sem.at[m])
        copy.start()
        out_copies.append(copy)
        both = land[m].reshape(ctx * rows, 2 * LANES).astype(F32)
        fill_heads(both[:, :LANES], kvar)
        fill_heads_turned(both[:, LANES:], vvar)

        def pair(p, carry):
            query = qs[m, p]
            mixed = jnp.zeros((LANES, rows), F32)
            for parity in range(2):
                head = 2 * p + parity
                g = head // group
                scores = dot_nt(kvar[g, parity], query) + bias_ref[...]
                top = jnp.max(scores, axis=0, keepdims=True)
                probs = jnp.exp(scores - top)
                total = jnp.sum(probs, axis=0, keepdims=True)
                mixed = mixed + dot(vvar[g, parity], probs.astype(BF)) / total
                lse[m, pl.ds(head, 1), :] = top + jnp.log(total)
            at = pl.multiple_of(p * LANES, LANES)
            obt[m, pl.ds(at, LANES), :] = mixed.astype(BF)
            ob[:, pl.ds(at, LANES)] = mixed.T.astype(BF)
            return carry

        lax.fori_loop(0, pairs, pair, 0)
        middle = x[m].astype(F32) + dot(ob[...], wo[...])
        x2[m] = middle
        h2[m] = (middle * inverse_norm(middle) * gain_mlp[...]).astype(BF)
    links.drain()
    for copy in out_copies:
        copy.wait()


def attention_forward(ctx, order, lens, x, wq, wo, bias_qkv, gain_attn, gain_mlp, freq):
    micro, rows, width = x.shape
    keys = rows * ctx
    vmem = pl.BlockSpec(memory_space=pltpu.VMEM)
    smem = pl.BlockSpec(memory_space=pltpu.SMEM)
    copies = micro * (ctx - 1)
    return pl.pallas_call(
        functools.partial(forward_kernel, (micro, rows, ctx)),
        out_shape=(
            jax.ShapeDtypeStruct((micro, rows, width), BF),
            jax.ShapeDtypeStruct((micro, rows, width), F32),
            jax.ShapeDtypeStruct((micro, HQ // 2, rows, LANES), BF),
            jax.ShapeDtypeStruct((micro, ctx, rows, 2 * LANES), BF),
            jax.ShapeDtypeStruct((micro, HQ, rows), F32),
            jax.ShapeDtypeStruct((micro, HQ * HD, rows), BF),
        ),
        in_specs=[smem, smem] + [vmem] * 7,
        out_specs=[vmem, vmem, vmem, pl.BlockSpec(memory_space=pl.ANY), vmem, vmem],
        scratch_shapes=[
            pltpu.VMEM((micro * rows, LANES), F32),
            pltpu.VMEM((micro * rows, LANES), F32),
            pltpu.VMEM((keys, rows), F32),
            pltpu.VMEM((KVH, 2, keys, LANES), BF),
            pltpu.VMEM((KVH, 2, LANES, keys), BF),
            pltpu.VMEM((rows, HQ * HD), BF),
            pltpu.VMEM((micro, ctx, rows, 2 * LANES), BF),
            pltpu.SemaphoreType.DMA((copies,)),
            pltpu.SemaphoreType.DMA((copies,)),
            pltpu.SemaphoreType.DMA((micro,)),
        ],
        compiler_params=pltpu.CompilerParams(
            collective_id=1, has_side_effects=True, vmem_limit_bytes=VMEM_LIMIT
        ),
        name="attention_forward",
    )(order, lens, x, wq, wo, bias_qkv, gain_attn, gain_mlp, freq)


def mlp_kernel(
    size, h2, gd, wgu, wd,
    out, gh2, grads,
    hbuf, turned_h, turned_g, acc_out, acc_gh, dgate, dup, ddown,
    sib_out, sib_in, par_out, par_in, keep_sum, stage, send, recv, out_sem,
):
    micro, rows, width, replicas, padded = size
    quarter = replicas * padded
    both = 2 * rows
    f, c = lax.axis_index("fsdp"), lax.axis_index("ctx")
    t = f % TP
    core = t % 2
    mine, theirs = t - core, flip2(t) - core
    sib, par = (flip1(f), c), (flip2(f), c)
    enter([sib, par])
    links = Links(send, recv)
    from_sib, from_par = [], []
    for m in range(micro):
        hbuf[m, t] = h2[m]
        from_sib.append(links.put(hbuf.at[m, t], hbuf.at[m, t], sib))
        from_par.append(links.put(hbuf.at[m, t], hbuf.at[m, t], par))
    from_cross = [None] * micro

    def forward_on(m):
        links.arrive(from_par[m], hbuf.at[m, flip2(t)])
        from_cross[m] = links.put(hbuf.at[m, flip2(t)], hbuf.at[m, flip2(t)], sib)

    def chunk(m, side, first, j):
        at = pl.multiple_of(j * CHUNK, CHUNK)
        up_at = pl.multiple_of(quarter + j * CHUNK, CHUNK)
        hidden_in = hbuf[m, pl.ds(side, 2)].reshape(both, width)
        grad_in = gd[m, pl.ds(side, 2)].reshape(both, width)
        w_gate = wgu[:, pl.ds(at, CHUNK)]
        w_up = wgu[:, pl.ds(up_at, CHUNK)]
        w_down = wd[pl.ds(at, CHUNK), :]
        gate = dot(hidden_in, w_gate)
        up = dot(hidden_in, w_up)
        gm = dot_nt(grad_in, w_down)
        sg = 0.5 * jnp.tanh(0.5 * gate) + 0.5
        silu = gate * sg
        mb = (silu * up).astype(BF)
        ggate = (gm * up * (sg + silu * (1.0 - sg))).astype(BF)
        gup = (gm * silu).astype(BF)
        acc_out[...] += dot(mb, w_down)
        acc_gh[...] += dot_nt(ggate, w_gate) + dot_nt(gup, w_up)
        if first:
            dgate[:, pl.ds(at, CHUNK)] = dot(turned_h[...], ggate)
            dup[:, pl.ds(at, CHUNK)] = dot(turned_h[...], gup)
            ddown[:, pl.ds(at, CHUNK)] = dot(turned_g[...], mb)
        else:
            dgate[:, pl.ds(at, CHUNK)] += dot(turned_h[...], ggate)
            dup[:, pl.ds(at, CHUNK)] += dot(turned_h[...], gup)
            ddown[:, pl.ds(at, CHUNK)] += dot(turned_g[...], mb)

    def compute(m, side, first, middle):
        turned_h[...] = hbuf[m, pl.ds(side, 2)].reshape(both, width).T
        turned_g[...] = gd[m, pl.ds(side, 2)].reshape(both, width).T
        acc_out[...] = jnp.zeros_like(acc_out)
        acc_gh[...] = jnp.zeros_like(acc_gh)
        chunks = quarter // CHUNK

        def body(j, carry):
            chunk(m, side, first, j)
            return carry

        lax.fori_loop(0, 1, body, 0)
        middle()
        lax.fori_loop(1, chunks, body, 0)

    def share(step):
        here = pl.multiple_of(core * rows, rows)
        there = pl.multiple_of(rows - core * rows, rows)
        ats = []
        for k, acc in enumerate((acc_gh, acc_out)):
            sib_out[step, k] = acc[pl.ds(there, rows), :].astype(BF)
            ats.append(links.put(sib_out.at[step, k], sib_in.at[step, k], sib))
            keep_sum[k] = acc[pl.ds(here, rows), :]
        return ats

    def pass_on(step, m, ats):
        got = []
        for k, at in enumerate(ats):
            links.arrive(at, sib_in.at[step, k])
            par_out[m, k] = (keep_sum[k] + sib_in[step, k].astype(F32)).astype(BF)
            got.append(links.put(par_out.at[m, k], par_in.at[m, k], par))
        return got

    def stay(step, m, ats):
        for k, at in enumerate(ats):
            links.arrive(at, sib_in.at[step, k])
            (gh2, out)[k][m] = keep_sum[k] + sib_in[step, k].astype(F32)

    def finish(m, ats):
        for k, (at, ref) in enumerate(zip(ats, (gh2, out))):
            links.arrive(at, par_in.at[m, k])
            ref[m] = ref[m] + par_in[m, k].astype(F32)

    plan = [(0, True)] + [(m, False) for m in range(micro)] + [(m, True) for m in range(1, micro)]
    waiting = None
    sums = [None] * micro
    ready_own = [False] * micro
    for step, (m, own) in enumerate(plan):
        if own:
            links.arrive(from_sib[m], hbuf.at[m, flip1(t)])
        else:
            links.arrive(from_cross[m], hbuf.at[m, flip2(flip1(t))])

        def middle(step=step):
            if step < micro:
                forward_on(step)
            if step > 0:
                last_m, last_own = plan[step - 1]
                if last_own:
                    stay(step - 1, last_m, waiting)
                else:
                    sums[last_m] = pass_on(step - 1, last_m, waiting)

        compute(m, mine if own else theirs, step == 0, middle)
        waiting = share(step)
    high = width // (replicas * TP)
    copies = []
    for replica in range(replicas):
        for k in range(TP + 2):
            slot = len(copies) % 2
            if len(copies) >= 2:
                copies[-2].wait()
            if k < TP:
                piece = slice((replica * TP + k) * high, (replica * TP + k + 1) * high)
                stage[slot, :, :quarter] = dgate[piece, :].astype(BF)
                stage[slot, :, quarter:] = dup[piece, :].astype(BF)
            else:
                for q in range(2 * replicas):
                    at = (k - TP) * 2 * replicas + q
                    stage[slot, :, q * padded : (q + 1) * padded] = ddown[
                        at * high : (at + 1) * high, replica * padded : (replica + 1) * padded
                    ].astype(BF)
            copy = pltpu.make_async_copy(stage.at[slot], grads.at[replica, k], out_sem.at[slot])
            copy.start()
            copies.append(copy)
    last_m, last_own = plan[-1]
    if last_own:
        stay(len(plan) - 1, last_m, waiting)
    else:
        sums[last_m] = pass_on(len(plan) - 1, last_m, waiting)
    for m in range(micro):
        finish(m, sums[m])
    for copy in copies[-2:]:
        copy.wait()
    links.drain()


def mlp(n, h2, gd, wgu, wd):
    micro, rows, width = h2.shape
    replicas = n // TP
    padded = wd.shape[0] // replicas
    quarter = replicas * padded
    vmem = pl.BlockSpec(memory_space=pltpu.VMEM)
    steps = 2 * micro
    copies = micro * 3 + steps * 2 + micro * 2
    return pl.pallas_call(
        functools.partial(mlp_kernel, (micro, rows, width, replicas, padded)),
        out_shape=(
            jax.ShapeDtypeStruct((micro, rows, width), F32),
            jax.ShapeDtypeStruct((micro, rows, width), F32),
            jax.ShapeDtypeStruct((replicas, TP + 2, width // n, 2 * quarter), BF),
        ),
        in_specs=[vmem] * 4,
        out_specs=[vmem, vmem, pl.BlockSpec(memory_space=pl.ANY)],
        scratch_shapes=[
            pltpu.VMEM((micro, TP, rows, width), BF),
            pltpu.VMEM((width, 2 * rows), BF),
            pltpu.VMEM((width, 2 * rows), BF),
            pltpu.VMEM((2 * rows, width), F32),
            pltpu.VMEM((2 * rows, width), F32),
            pltpu.VMEM((width, quarter), F32),
            pltpu.VMEM((width, quarter), F32),
            pltpu.VMEM((width, quarter), F32),
            pltpu.VMEM((steps, 2, rows, width), BF),
            pltpu.VMEM((steps, 2, rows, width), BF),
            pltpu.VMEM((micro, 2, rows, width), BF),
            pltpu.VMEM((micro, 2, rows, width), BF),
            pltpu.VMEM((2, rows, width), F32),
            pltpu.VMEM((2, width // n, 2 * quarter), BF),
            pltpu.SemaphoreType.DMA((copies,)),
            pltpu.SemaphoreType.DMA((copies,)),
            pltpu.SemaphoreType.DMA((2,)),
        ],
        compiler_params=pltpu.CompilerParams(
            collective_id=2, has_side_effects=True, vmem_limit_bytes=VMEM_LIMIT
        ),
        name="mlp",
    )(h2, gd, wgu, wd)


def backward_kernel(
    size, order, lens, gh2, x2, gy, x, wq, wo, gain_attn, gain_mlp, freq, qs, kv, lse, obt,
    dx, dwq, dwo, dbias, dgain_attn, dgain_mlp,
    cos_ref, sin_ref, bias_ref, kvar, kvar_turned, vvar, gx2, go_ref, gp, gk, gv, part, land,
    send, recv,
):
    micro, rows, ctx = size
    group = HQ // KVH
    pairs = HQ // 2
    width = HQ * HD
    scale = 1.0 / math.sqrt(HD)
    f, c = lax.axis_index("fsdp"), lax.axis_index("ctx")
    others = [(f, (c + j) % ctx) for j in range(1, ctx)]
    back = [(c - j + ctx) % ctx for j in range(1, ctx)]
    enter(others)
    links = Links(send, recv)
    arrivals = []
    for m in range(micro):
        fill_tables(m, rows, c, freq, order, lens, cos_ref, sin_ref)
        stream = x2[m]
        inverse = inverse_norm(stream)
        normed = stream * inverse
        grad = gh2[m]
        term = jnp.sum(grad * normed, axis=0, keepdims=True)
        dgain_mlp[...] = term if m == 0 else dgain_mlp[...] + term
        grad = grad * gain_mlp[...]
        grad = gy[m].astype(F32) + inverse * (
            grad - normed * jnp.mean(grad * normed, axis=1, keepdims=True)
        )
        gx2[m] = grad
        low = grad.astype(BF)
        term = dot(obt[m], low)
        dwo[...] = term if m == 0 else dwo[...] + term
        spread = dot_nt(low, wo[...]).astype(BF)
        for p in range(pairs):
            go_ref[m, p] = spread[:, p * LANES : (p + 1) * LANES]
    for m in range(micro):
        fill_bias(m, rows, c, order, lens, bias_ref)
        both = kv[m].reshape(ctx * rows, 2 * LANES).astype(F32)
        fill_heads(both[:, :LANES], kvar)
        fill_heads_turned(both[:, :LANES], kvar_turned)
        fill_heads(both[:, LANES:], vvar)
        gk[...] = jnp.zeros_like(gk)
        gv[...] = jnp.zeros_like(gv)
        cosine = cos_ref[m * rows : (m + 1) * rows, :]
        sine = sin_ref[m * rows : (m + 1) * rows, :]

        def pair(p, carry):
            query = qs[m, p]
            go = go_ref[m, p]
            grad_query = jnp.zeros((LANES, rows), F32)
            for parity in range(2):
                head = 2 * p + parity
                g = head // group
                scores = dot_nt(kvar[g, parity], query) + bias_ref[...]
                probs = jnp.exp(scores - lse[m, pl.ds(head, 1), :])
                grad_probs = dot_nt(vvar[g, parity], go)
                delta = jnp.sum(probs * grad_probs, axis=0, keepdims=True)
                grad_scores = (probs * (grad_probs - delta)).astype(BF)
                grad_query = grad_query + dot(kvar_turned[g, parity], grad_scores)
                gk[g, parity] += dot(grad_scores, query)
                gv[g, parity] += dot(probs.astype(BF), go)
            turned = grad_query.T * scale
            turned = turned * cosine - swap_halves(turned) * sine
            at = pl.multiple_of(p * LANES, LANES)
            gp[m * rows : (m + 1) * rows, pl.ds(at, LANES)] = turned.astype(BF)
            return carry

        lax.fori_loop(0, pairs, pair, 0)
        low = lax.broadcasted_iota(jnp.int32, (ctx * rows, LANES), 1) < HD
        for k, acc in enumerate((gk, gv)):
            first = acc[0, 0] + pltpu.roll(acc[0, 1], HD, 1)
            second = pltpu.roll(acc[1, 0], HD, 1) + acc[1, 1]
            merged = jnp.where(low, first, second).astype(BF)
            part[m, :, :, k * LANES : (k + 1) * LANES] = merged.reshape(ctx, rows, LANES)
        arrivals.append(
            [
                links.put(part.at[m, other[1]], land.at[m, c], other)
                for other in others
            ]
        )
    for m in range(micro):
        total = part[m, c].astype(F32)
        for at, source in zip(arrivals[m], back):
            links.arrive(at, land.at[m, source])
            total = total + land[m, source].astype(F32)
        cosine = cos_ref[m * rows : (m + 1) * rows, :]
        sine = sin_ref[m * rows : (m + 1) * rows, :]
        grad_keys = total[:, :LANES]
        grad_keys = grad_keys * cosine - swap_halves(grad_keys) * sine
        gp[m * rows : (m + 1) * rows, width : width + LANES] = grad_keys.astype(BF)
        gp[m * rows : (m + 1) * rows, width + LANES :] = total[:, LANES:].astype(BF)
    for m in range(micro):
        grad_project = gp[m * rows : (m + 1) * rows, :]
        stream = x[m].astype(F32)
        inverse = inverse_norm(stream)
        normed = stream * inverse
        h1 = (normed * gain_attn[...]).astype(BF)
        term = dot(h1.T, grad_project)
        dwq[...] = term if m == 0 else dwq[...] + term
        term = jnp.sum(grad_project.astype(F32), axis=0, keepdims=True)
        dbias[...] = term if m == 0 else dbias[...] + term
        grad = dot_nt(grad_project, wq[...])
        term = jnp.sum(grad * normed, axis=0, keepdims=True)
        dgain_attn[...] = term if m == 0 else dgain_attn[...] + term
        grad = grad * gain_attn[...]
        dx[m] = gx2[m] + inverse * (
            grad - normed * jnp.mean(grad * normed, axis=1, keepdims=True)
        )
    links.drain()


def attention_backward(
    ctx, order, lens, gh2, x2, gy, x, wq, wo, gain_attn, gain_mlp, freq, qs, kv, lse, obt
):
    micro, rows, width = x.shape
    keys = rows * ctx
    vmem = pl.BlockSpec(memory_space=pltpu.VMEM)
    smem = pl.BlockSpec(memory_space=pltpu.SMEM)
    copies = micro * (ctx - 1)
    return pl.pallas_call(
        functools.partial(backward_kernel, (micro, rows, ctx)),
        out_shape=(
            jax.ShapeDtypeStruct((micro, rows, width), F32),
            jax.ShapeDtypeStruct(wq.shape, F32),
            jax.ShapeDtypeStruct(wo.shape, F32),
            jax.ShapeDtypeStruct((1, wq.shape[1]), F32),
            jax.ShapeDtypeStruct((1, width), F32),
            jax.ShapeDtypeStruct((1, width), F32),
        ),
        in_specs=[smem, smem] + [vmem] * 13,
        out_specs=[vmem] * 6,
        scratch_shapes=[
            pltpu.VMEM((micro * rows, LANES), F32),
            pltpu.VMEM((micro * rows, LANES), F32),
            pltpu.VMEM((keys, rows), F32),
            pltpu.VMEM((KVH, 2, keys, LANES), BF),
            pltpu.VMEM((KVH, 2, LANES, keys), BF),
            pltpu.VMEM((KVH, 2, keys, LANES), BF),
            pltpu.VMEM((micro, rows, width), F32),
            pltpu.VMEM((micro, HQ // 2, rows, LANES), BF),
            pltpu.VMEM((micro * rows, wq.shape[1]), BF),
            pltpu.VMEM((KVH, 2, keys, LANES), F32),
            pltpu.VMEM((KVH, 2, keys, LANES), F32),
            pltpu.VMEM((micro, ctx, rows, 2 * LANES), BF),
            pltpu.VMEM((micro, ctx, rows, 2 * LANES), BF),
            pltpu.SemaphoreType.DMA((copies,)),
            pltpu.SemaphoreType.DMA((copies,)),
        ],
        compiler_params=pltpu.CompilerParams(
            collective_id=3, has_side_effects=True, vmem_limit_bytes=VMEM_LIMIT
        ),
        name="attention_backward",
    )(order, lens, gh2, x2, gy, x, wq, wo, gain_attn, gain_mlp, freq, qs, kv, lse, obt)


def add_pieces(dst, a, b, width):
    def body(k, carry):
        at = pl.multiple_of(k * 512, 512)
        dst[:, pl.ds(at, 512)] = (
            a[:, pl.ds(at, 512)].astype(F32) + b[:, pl.ds(at, 512)].astype(F32)
        ).astype(BF)
        return carry

    lax.fori_loop(0, width // 512, body, 0)


def reduce_kernel(
    n, ctx, grads, att,
    out_gu, out_rest,
    peer_in, core_in, core_sum, par_in, par_sum, ring_in,
    total, pre_in, suf_in, pre_out, suf_out, final, land,
    send, recv, pre_s, pre_r, suf_s, suf_r, fin_s, fin_r, here,
):
    replicas = n // TP
    wide = grads.shape[-1]
    slim = att.shape[-1]
    pieces = TP + 3
    f, c = lax.axis_index("fsdp"), lax.axis_index("ctx")
    t, r = f % TP, f // TP
    core, side = t % 2, t // 2
    sib, par, cross = (flip1(f), c), (flip2(f), c), (flip2(flip1(f)), c)
    peers = [((f + TP * j) % n, c) for j in range(1, replicas)]
    barrier = pltpu.get_barrier_semaphore()
    around = [sib, par, cross] + peers
    for device in around:
        pl.semaphore_signal(barrier, inc=1, device_id=device, device_id_type=MESH)
    left, right = (f, (c + ctx - 1) % ctx), (f, (c + 1) % ctx)
    for device in (left, right):
        pl.semaphore_signal(barrier, inc=1, device_id=device, device_id_type=MESH)
    pl.semaphore_wait(barrier, len(around) + 2)
    links = Links(send, recv)
    to_sib = links.put(att.at[:, :, 1 - core], core_in, sib)
    to_peers = [
        links.put(grads.at[(r + j + 1) % replicas], peer_in.at[j], peer)
        for j, peer in enumerate(peers)
    ]
    links.arrive(to_sib, core_in)
    for replica in range(replicas):
        for s in range(2):
            add_pieces(
                core_sum.at[replica, s], att.at[replica, s, core], core_in.at[replica, s], slim
            )
    to_par = links.put(core_sum.at[:, 1 - side], par_in, par)
    links.arrive(to_par, par_in)
    for replica in range(replicas):
        add_pieces(par_sum.at[replica], core_sum.at[replica, side], par_in.at[replica], slim)
    ring = [
        links.put(par_sum.at[(r + j + 1) % replicas], ring_in.at[j], peer)
        for j, peer in enumerate(peers)
    ]
    for j, at in enumerate(to_peers):
        links.arrive(at, peer_in.at[j])
        for k in range(TP + 2):
            add_pieces(
                total.at[k], grads.at[r, k] if j == 0 else total.at[k], peer_in.at[j, k], wide
            )
    for j, at in enumerate(ring):
        links.arrive(at, ring_in.at[j])
        source = par_sum.at[r] if j == 0 else total.at[TP + 2, :, pl.ds(0, slim)]
        add_pieces(total.at[TP + 2, :, pl.ds(0, slim)], source, ring_in.at[j], slim)

    def scan_copy(k, src, dst, s, q, device):
        return pltpu.make_async_remote_copy(
            src_ref=src.at[k],
            dst_ref=dst.at[k],
            send_sem=s.at[k],
            recv_sem=q.at[k],
            device_id=device,
            device_id_type=MESH,
        )

    def scan(k, order_at, src, got, s, q, ahead):
        @pl.when(order_at > 0)
        def _():
            scan_copy(k, src, got, s, q, ahead).wait_recv()

        @pl.when(order_at < ctx - 1)
        def _():
            @pl.when(order_at > 0)
            def _():
                add_pieces(src.at[k], total.at[k], got.at[k], wide)

            @pl.when(order_at == 0)
            def _():
                local = pltpu.make_async_copy(total.at[k], src.at[k], here.at[0])
                local.start()
                local.wait()

            scan_copy(k, src, got, s, q, ahead).start()

    def finish(k):
        @pl.when(c > 0)
        def _():
            add_pieces(final.at[k], total.at[k], pre_in.at[k], wide)

        @pl.when(c == 0)
        def _():
            add_pieces(final.at[k], total.at[k], suf_in.at[k], wide)

        @pl.when((c > 0) & (c < ctx - 1))
        def _():
            add_pieces(final.at[k], final.at[k], suf_in.at[k], wide)

        @pl.when((k < TP) & (k != t))
        def _():
            pltpu.make_async_remote_copy(
                src_ref=final.at[k],
                dst_ref=land.at[t],
                send_sem=fin_s.at[k],
                recv_sem=fin_r.at[t],
                device_id=(f - t + k, c),
                device_id_type=MESH,
            ).start()

    late = jnp.maximum(c, ctx - 1 - c)

    def tick(time, carry):
        k = time - c

        @pl.when((k >= 0) & (k < pieces))
        def _():
            scan(k, c, pre_out, pre_in, pre_s, pre_r, right)

        k2 = time - (ctx - 1 - c)

        @pl.when((k2 >= 0) & (k2 < pieces))
        def _():
            scan(k2, ctx - 1 - c, suf_out, suf_in, suf_s, suf_r, left)

        k3 = time - late

        @pl.when((k3 >= 0) & (k3 < pieces))
        def _():
            finish(k3)

        return carry

    lax.fori_loop(0, pieces + ctx - 1, tick, 0)
    out_rest[...] = final[TP:].astype(F32)
    for k in range(TP):
        @pl.when(k == t)
        def _():
            out_gu[k] = final[k].astype(F32)

        @pl.when(k != t)
        def _():
            copy = pltpu.make_async_remote_copy(
                src_ref=final.at[k],
                dst_ref=land.at[k],
                send_sem=fin_s.at[k],
                recv_sem=fin_r.at[k],
                device_id=(f - t + k, c),
                device_id_type=MESH,
            )
            copy.wait_recv()
            copy.wait_send()
            out_gu[k] = land[k].astype(F32)

    def settle(k, carry):
        @pl.when(c < ctx - 1)
        def _():
            scan_copy(k, pre_out, pre_in, pre_s, pre_r, right).wait_send()

        @pl.when(c > 0)
        def _():
            scan_copy(k, suf_out, suf_in, suf_s, suf_r, left).wait_send()

        return carry

    lax.fori_loop(0, pieces, settle, 0)
    links.drain()


def reduce_grads(n, ctx, grads, att):
    replicas = n // TP
    _, _, high, wide = grads.shape
    slim = att.shape[-1]
    pieces = TP + 3
    copies = 2 + 2 * (replicas - 1)
    vmem = pl.BlockSpec(memory_space=pltpu.VMEM)
    sems = pltpu.SemaphoreType.DMA
    piece = pltpu.VMEM((pieces, high, wide), BF)
    return pl.pallas_call(
        functools.partial(reduce_kernel, n, ctx),
        out_shape=(
            jax.ShapeDtypeStruct((TP, high, wide), F32),
            jax.ShapeDtypeStruct((3, high, wide), F32),
        ),
        in_specs=[vmem, vmem],
        out_specs=[vmem, vmem],
        scratch_shapes=[
            pltpu.VMEM((replicas - 1, TP + 2, high, wide), BF),
            pltpu.VMEM((replicas, 2, high, slim), BF),
            pltpu.VMEM((replicas, 2, high, slim), BF),
            pltpu.VMEM((replicas, high, slim), BF),
            pltpu.VMEM((replicas, high, slim), BF),
            pltpu.VMEM((replicas - 1, high, slim), BF),
            piece, piece, piece, piece, piece, piece,
            pltpu.VMEM((TP, high, wide), BF),
            sems((copies,)), sems((copies,)),
            sems((pieces,)), sems((pieces,)), sems((pieces,)), sems((pieces,)),
            sems((TP,)), sems((TP,)), sems((1,)),
        ],
        compiler_params=pltpu.CompilerParams(
            collective_id=4, has_side_effects=True, vmem_limit_bytes=VMEM_LIMIT
        ),
        name="reduce_grads",
    )(grads, att)


def pad_to(v, axis, size):
    pads = [(0, 0)] * v.ndim
    pads[axis] = (0, size - v.shape[axis])
    return jnp.pad(v, pads)


def local(
    inputs, cotangent, lengths, order, w_qkv, b_qkv, w_out, norm_attn, norm_mlp, w_gate_up, w_down
):
    n = lax.axis_size("fsdp")
    ctx = lax.axis_size("ctx")
    replicas = n // TP
    x, gy = inputs[0], cotangent[0]
    micro, rows, width = x.shape
    high = w_gate_up.shape[0]
    units = w_down.shape[0]
    padded = -(-units // LANES) * LANES
    quarter = replicas * padded
    proj = w_qkv.shape[1]
    qk = (HQ + KVH) * HD
    vw = KVH * HD

    wgu = w_gate_up.reshape(high, 2, replicas, TP, units)
    wgu = pad_to(wgu.transpose(3, 0, 1, 2, 4), 4, padded).reshape(TP, high, 2 * quarter)
    wd = pad_to(w_down, 0, padded)
    small = jnp.concatenate(
        [
            pad_to(b_qkv, 0, 2 * LANES).reshape(2, LANES),
            pad_to(norm_attn, 0, LANES)[None],
            pad_to(norm_mlp, 0, LANES)[None],
            jnp.zeros((12, LANES), BF),
        ]
    )
    wq_all, wo_all, sm_all, wgu_t, wd_t, gd_all = gather_weights(
        n, w_qkv, w_out, small, wgu, wd, gy
    )
    wq_all = wq_all.reshape(width, proj)
    wo_all = wo_all.reshape(width, width)
    bias = sm_all[:, :2].reshape(n, 2 * LANES)[:, : b_qkv.shape[0]].reshape(1, proj).astype(F32)
    gain_attn = sm_all[:, 2, :high].reshape(1, width).astype(F32)
    gain_mlp = sm_all[:, 3, :high].reshape(1, width).astype(F32)
    wgu_t = wgu_t.reshape(width, 2 * quarter)
    wd_t = wd_t.reshape(quarter, width)

    half = HD // 2
    freqs = np.power(np.float32(ROPE_BASE), -(np.arange(half, dtype=np.float32) * (2.0 / HD)))
    freq = jnp.asarray(np.tile(freqs.astype(np.float32), (8, LANES // half)))
    h2, x2, qs, kv, lse, obt = attention_forward(
        ctx, order[0], lengths[0], x, wq_all, wo_all, bias, gain_attn, gain_mlp, freq
    )
    gd_all = gd_all.transpose(1, 0, 2, 3)
    out, gh2, grads = mlp(n, h2, gd_all, wgu_t, wd_t)
    outputs = (x2 + out).astype(BF)
    dx, dwq, dwo, dbias, dgain_attn, dgain_mlp = attention_backward(
        ctx, order[0], lengths[0], gh2, x2, gy, x, wq_all, wo_all, gain_attn, gain_mlp, freq,
        qs, kv, lse, obt,
    )
    vectors = jnp.stack(
        [
            pad_to(dbias[0, :qk].reshape(n, qk // n), 1, LANES),
            pad_to(dbias[0, qk:].reshape(n, vw // n), 1, LANES),
            pad_to(dgain_attn.reshape(n, high), 1, LANES),
            pad_to(dgain_mlp.reshape(n, high), 1, LANES),
        ],
        axis=1,
    )
    slim = -(-(proj + width + LANES) // 512) * 512
    att = jnp.concatenate(
        [dwq.reshape(n, high, proj), dwo.reshape(n, high, width), pad_to(vectors, 1, high)], axis=2
    ).astype(BF)
    att = pad_to(att, 2, slim).reshape(replicas, 2, 2, high, slim)
    out_gu, out_rest = reduce_grads(n, ctx, grads, att)
    g_gu = out_gu.reshape(TP, high, 2, replicas, padded)[..., :units]
    g_gu = g_gu.transpose(1, 2, 3, 0, 4).reshape(high, 2 * replicas * TP * units)
    g_down = out_rest[:2].reshape(2, high, 2 * replicas, padded).transpose(0, 2, 1, 3)
    g_down = g_down.reshape(width, padded)[:, :units].T
    last = out_rest[2]
    g_qkv = last[:, :proj]
    g_out = last[:, proj : proj + width]
    vec = last[:4, proj + width : proj + width + LANES]
    return (
        outputs[None],
        dx[None],
        g_qkv,
        vec[0, : qk // n],
        vec[1, : vw // n],
        g_out,
        vec[2, :high],
        vec[3, :high],
        g_gu,
        g_down,
    )


def solution(mesh):
    return jax.shard_map(
        local,
        mesh=mesh,
        in_specs=(
            P("fsdp", None, "ctx", None),
            P("fsdp", None, "ctx", None),
            P("fsdp", None, None),
            P("fsdp", None, None),
            P("fsdp", None),
            P("fsdp"),
            P("fsdp", None),
            P("fsdp"),
            P("fsdp"),
            P("fsdp", None),
            P("fsdp", None),
        ),
        out_specs=(
            P("fsdp", None, "ctx", None),
            P("fsdp", None, "ctx", None),
            P("fsdp", None),
            P("fsdp"),
            P("fsdp"),
            P("fsdp", None),
            P("fsdp"),
            P("fsdp"),
            P("fsdp", None),
            P("fsdp", None),
        ),
        check_vma=False,
    )
```

```python
import functools
import math

import jax
import jax.numpy as jnp
import numpy as np
from jax import lax
from jax.experimental import pallas as pl
from jax.experimental.pallas import tpu as pltpu
from jax.sharding import PartitionSpec as P

HQ = 14
KVH = 2
HD = 64
EPSILON = 1e-06
ROPE_BASE = 1000000.0
NEGATIVE = -1e30
TP = 4
LANES = 128
CHUNK = 256
PIECES = 3 * TP
ALL_PIECES = PIECES + 2
RING = 4
VEC = 32
BF = jnp.bfloat16
F32 = jnp.float32
MESH = pl.DeviceIdType.MESH
VMEM_LIMIT = 60 * 1024 * 1024


def flip1(v):
    return v + 1 - 2 * (v % 2)


def flip2(v):
    return v + 2 - 4 * ((v // 2) % 2)


def dot(a, b):
    return jnp.dot(a, b, preferred_element_type=F32)


def dot_nt(a, b):
    return lax.dot_general(a, b, (((1,), (1,)), ((), ())), preferred_element_type=F32)


class Links:
    def __init__(self, send_sems, recv_sems):
        self.send_sems, self.recv_sems = send_sems, recv_sems
        self.started = []

    def put(self, src, dst, device):
        at = len(self.started)
        copy = pltpu.make_async_remote_copy(
            src_ref=src,
            dst_ref=dst,
            send_sem=self.send_sems.at[at],
            recv_sem=self.recv_sems.at[at],
            device_id=device,
            device_id_type=MESH,
        )
        copy.start()
        self.started.append((copy, device))
        return at

    def arrive(self, at, slot):
        pltpu.make_async_remote_copy(
            src_ref=slot,
            dst_ref=slot,
            send_sem=self.send_sems.at[at],
            recv_sem=self.recv_sems.at[at],
            device_id=self.started[at][1],
            device_id_type=MESH,
        ).wait_recv()

    def drain(self):
        for copy, _ in self.started:
            copy.wait_send()


def enter(devices):
    barrier = pltpu.get_barrier_semaphore()
    for device in devices:
        pl.semaphore_signal(barrier, inc=1, device_id=device, device_id_type=MESH)
    pl.semaphore_wait(barrier, len(devices))


def gather_kernel(
    n, wq, wo, sm, wgu, wd, gd, wq_all, wo_all, sm_all, wgu_t, wd_t, gd_all, send, recv, here
):
    replicas = n // TP
    f, c = lax.axis_index("fsdp"), lax.axis_index("ctx")
    t, r = f % TP, f // TP
    sib, par, cross = (flip1(f), c), (flip2(f), c), (flip2(flip1(f)), c)
    peers = [((f + TP * j) % n, c) for j in range(1, replicas)]
    back = [(f - TP * j + n) % n for j in range(1, replicas)]
    rback = [(r - j + replicas) % replicas for j in range(1, replicas)]
    enter([sib, par, cross] + peers)
    links = Links(send, recv)
    local = []

    def keep(src, dst):
        copy = pltpu.make_async_copy(src, dst, here.at[len(local)])
        copy.start()
        local.append(copy)

    pending = []
    both = []
    for own, every in ((wq, wq_all), (wo, wo_all), (sm, sm_all)):
        ys = [links.put(own, every.at[f], peer) for peer in peers]
        x = links.put(own, every.at[f], par)
        s = links.put(own, every.at[f], sib)
        keep(own, every.at[f])
        both.append((every, ys, x, s))
    gd_x = links.put(gd, gd_all.at[t], par)
    gd_s = links.put(gd, gd_all.at[t], sib)
    keep(gd, gd_all.at[t])
    gu_s = links.put(wgu.at[flip1(t)], wgu_t.at[r, t], sib)
    gu_x = links.put(wgu.at[flip2(t)], wgu_t.at[r, t], par)
    gu_c = links.put(wgu.at[flip2(flip1(t))], wgu_t.at[r, t], cross)
    keep(wgu.at[t], wgu_t.at[r, t])
    for j, peer in enumerate(peers):
        at = links.put(wgu.at[t], wgu_t.at[r, t], peer)
        pending.append((at, wgu_t.at[rback[j], t]))
        at = links.put(wd, wd_t.at[r], peer)
        pending.append((at, wd_t.at[rback[j]]))
    keep(wd, wd_t.at[r])
    later = []
    for every, ys, x, s in both:
        pending.append((s, every.at[flip1(f)]))
        for j, at in enumerate(ys):
            links.arrive(at, every.at[back[j]])
            at_x = links.put(every.at[back[j]], every.at[back[j]], par)
            later.append((every, at_x, flip2(back[j])))
            at_s = links.put(every.at[back[j]], every.at[back[j]], sib)
            pending.append((at_s, every.at[flip1(back[j])]))
        links.arrive(x, every.at[flip2(f)])
        at_s = links.put(every.at[flip2(f)], every.at[flip2(f)], sib)
        pending.append((at_s, every.at[flip2(flip1(f))]))
    for at, other in ((gu_s, flip1(t)), (gu_x, flip2(t)), (gu_c, flip2(flip1(t)))):
        links.arrive(at, wgu_t.at[r, other])
        for j, peer in enumerate(peers):
            at_y = links.put(wgu_t.at[r, other], wgu_t.at[r, other], peer)
            pending.append((at_y, wgu_t.at[rback[j], other]))
    for every, at, slot in later:
        links.arrive(at, every.at[slot])
        at_s = links.put(every.at[slot], every.at[slot], sib)
        pending.append((at_s, every.at[flip1(slot)]))
    links.arrive(gd_x, gd_all.at[flip2(t)])
    at_s = links.put(gd_all.at[flip2(t)], gd_all.at[flip2(t)], sib)
    pending.append((at_s, gd_all.at[flip2(flip1(t))]))
    pending.append((gd_s, gd_all.at[flip1(t)]))
    for at, slot in pending:
        links.arrive(at, slot)
    links.drain()
    for copy in local:
        copy.wait()


def gather_weights(n, wq, wo, sm, wgu, wd, gd):
    replicas = n // TP
    copies = 3 * ((replicas - 1) * 4 + 3) + 3 + (replicas - 1) * 5 + 3
    anywhere = pl.BlockSpec(memory_space=pl.ANY)
    shapes = (
        jax.ShapeDtypeStruct((n,) + wq.shape, BF),
        jax.ShapeDtypeStruct((n,) + wo.shape, BF),
        jax.ShapeDtypeStruct((n,) + sm.shape, BF),
        jax.ShapeDtypeStruct((replicas,) + wgu.shape, BF),
        jax.ShapeDtypeStruct((replicas,) + wd.shape, BF),
        jax.ShapeDtypeStruct((TP,) + gd.shape, BF),
    )
    return pl.pallas_call(
        functools.partial(gather_kernel, n),
        out_shape=shapes,
        in_specs=[anywhere] * 6,
        out_specs=[anywhere] * 6,
        scratch_shapes=[
            pltpu.SemaphoreType.DMA((copies,)),
            pltpu.SemaphoreType.DMA((copies,)),
            pltpu.SemaphoreType.DMA((6,)),
        ],
        compiler_params=pltpu.CompilerParams(collective_id=0, has_side_effects=True),
        name="gather_weights",
    )(wq, wo, sm, wgu, wd, gd)


def begin_of(natural, lens, m, count):
    begin = jnp.zeros_like(natural)
    end = jnp.int32(0)
    for j in range(count):
        piece = lens[m, j]
        end = end + piece
        begin = begin + jnp.where(end <= natural, piece, 0)
    return begin


def fill_tables(m, rows, c, freq, order, lens, cos_ref, sin_ref):
    block = rows // 2
    lane = lax.broadcasted_iota(jnp.int32, (block, LANES), 1)
    low = (lane % HD) < (HD // 2)
    for b in range(2):
        natural = order[m, c * 2 + b] * block + lax.broadcasted_iota(
            jnp.int32, (block, LANES), 0
        )
        position = natural - begin_of(natural, lens, m, lens.shape[1])
        angle = position.astype(F32) * freq[0:1, :]
        at = m * rows + b * block
        cos_ref[at : at + block, :] = jnp.cos(angle)
        sine = jnp.sin(angle)
        sin_ref[at : at + block, :] = jnp.where(low, -sine, sine)


def swap_halves(u):
    lane = lax.broadcasted_iota(jnp.int32, u.shape, 1)
    low = (lane % HD) < (HD // 2)
    return jnp.where(low, pltpu.roll(u, LANES - HD // 2, 1), pltpu.roll(u, HD // 2, 1))


def fill_bias(m, rows, c, order, lens, bias_ref):
    block = rows // 2
    lane = lax.broadcasted_iota(jnp.int32, (1, rows), 1)
    query = jnp.where(
        lane < block,
        order[m, c * 2] * block + lane,
        order[m, c * 2 + 1] * block + lane - block,
    )
    begin = begin_of(query, lens, m, lens.shape[1])

    def body(k, carry):
        key = order[m, k] * block + lax.broadcasted_iota(jnp.int32, (block, rows), 0)
        allowed = (key <= query) & (key >= begin)
        at = pl.multiple_of(k * block, block)
        bias_ref[pl.ds(at, block), :] = jnp.where(allowed, 0.0, NEGATIVE)
        return carry

    lax.fori_loop(0, order.shape[1], body, 0)


def fill_heads(whole, var_ref):
    rolled = pltpu.roll(whole, HD, 1)
    low = lax.broadcasted_iota(jnp.int32, whole.shape, 1) < HD
    var_ref[0, 0] = jnp.where(low, whole, 0.0).astype(BF)
    var_ref[0, 1] = jnp.where(low, 0.0, rolled).astype(BF)
    var_ref[1, 0] = jnp.where(low, rolled, 0.0).astype(BF)
    var_ref[1, 1] = jnp.where(low, 0.0, whole).astype(BF)


def fill_heads_turned(whole, var_ref):
    turned = whole.T
    rolled = jnp.concatenate([turned[HD:], turned[:HD]], axis=0)
    low = lax.broadcasted_iota(jnp.int32, turned.shape, 0) < HD
    var_ref[0, 0] = jnp.where(low, turned, 0.0).astype(BF)
    var_ref[0, 1] = jnp.where(low, 0.0, rolled).astype(BF)
    var_ref[1, 0] = jnp.where(low, rolled, 0.0).astype(BF)
    var_ref[1, 1] = jnp.where(low, 0.0, turned).astype(BF)


def inverse_norm(v):
    return lax.rsqrt(jnp.mean(v * v, axis=1, keepdims=True) + EPSILON)


def forward_kernel(
    size, order, lens, x, wq, wo, bias_qkv, gain_attn, gain_mlp, freq,
    h2, x2, qs, kv, lse, obt,
    cos_ref, sin_ref, bias_ref, kvar, vvar, ob, land, send, recv, out_sem,
):
    micro, rows, ctx = size
    group = HQ // KVH
    pairs = HQ // 2
    width = HQ * HD
    f, c = lax.axis_index("fsdp"), lax.axis_index("ctx")
    others = [(f, (c + j) % ctx) for j in range(1, ctx)]
    back = [(c - j + ctx) % ctx for j in range(1, ctx)]
    enter(others)
    links = Links(send, recv)
    arrivals = []
    for m in range(micro):
        fill_tables(m, rows, c, freq, order, lens, cos_ref, sin_ref)
    for m in range(micro):
        stream = x[m].astype(F32)
        h1 = (stream * inverse_norm(stream) * gain_attn[...]).astype(BF)
        project = dot(h1, wq[...]) + bias_qkv[...]
        cosine = cos_ref[m * rows : (m + 1) * rows, :]
        sine = sin_ref[m * rows : (m + 1) * rows, :]
        keys = project[:, width : width + LANES]
        keys = keys * cosine + swap_halves(keys) * sine
        land[m, c, :, :LANES] = keys.astype(BF)
        land[m, c, :, LANES:] = project[:, width + LANES :].astype(BF)
        arrivals.append([links.put(land.at[m, c], land.at[m, c], other) for other in others])
        for p in range(pairs):
            query = project[:, p * LANES : (p + 1) * LANES]
            query = query * cosine + swap_halves(query) * sine
            qs[m, p] = (query.astype(BF).astype(F32) * (1.0 / math.sqrt(HD))).astype(BF)
    out_copies = []
    for m in range(micro):
        fill_bias(m, rows, c, order, lens, bias_ref)
        for at, source in zip(arrivals[m], back):
            links.arrive(at, land.at[m, source])
        copy = pltpu.make_async_copy(land.at[m], kv.at[m], out_sem.at[m])
        copy.start()
        out_copies.append(copy)
        both = land[m].reshape(ctx * rows, 2 * LANES).astype(F32)
        fill_heads(both[:, :LANES], kvar)
        fill_heads_turned(both[:, LANES:], vvar)

        def pair(p, carry):
            query = qs[m, p]
            mixed = jnp.zeros((LANES, rows), F32)
            for parity in range(2):
                head = 2 * p + parity
                g = head // group
                scores = dot_nt(kvar[g, parity], query) + bias_ref[...]
                top = jnp.max(scores, axis=0, keepdims=True)
                probs = jnp.exp(scores - top)
                total = jnp.sum(probs, axis=0, keepdims=True)
                mixed = mixed + dot(vvar[g, parity], probs.astype(BF)) / total
                lse[m, pl.ds(head, 1), :] = top + jnp.log(total)
            at = pl.multiple_of(p * LANES, LANES)
            obt[m, pl.ds(at, LANES), :] = mixed.astype(BF)
            ob[:, pl.ds(at, LANES)] = mixed.T.astype(BF)
            return carry

        lax.fori_loop(0, pairs, pair, 0)
        middle = x[m].astype(F32) + dot(ob[...], wo[...])
        x2[m] = middle
        h2[m] = (middle * inverse_norm(middle) * gain_mlp[...]).astype(BF)
    links.drain()
    for copy in out_copies:
        copy.wait()


def attention_forward(ctx, order, lens, x, wq, wo, bias_qkv, gain_attn, gain_mlp, freq):
    micro, rows, width = x.shape
    keys = rows * ctx
    vmem = pl.BlockSpec(memory_space=pltpu.VMEM)
    smem = pl.BlockSpec(memory_space=pltpu.SMEM)
    copies = micro * (ctx - 1)
    return pl.pallas_call(
        functools.partial(forward_kernel, (micro, rows, ctx)),
        out_shape=(
            jax.ShapeDtypeStruct((micro, rows, width), BF),
            jax.ShapeDtypeStruct((micro, rows, width), F32),
            jax.ShapeDtypeStruct((micro, HQ // 2, rows, LANES), BF),
            jax.ShapeDtypeStruct((micro, ctx, rows, 2 * LANES), BF),
            jax.ShapeDtypeStruct((micro, HQ, rows), F32),
            jax.ShapeDtypeStruct((micro, HQ * HD, rows), BF),
        ),
        in_specs=[smem, smem] + [vmem] * 7,
        out_specs=[vmem, vmem, vmem, pl.BlockSpec(memory_space=pl.ANY), vmem, vmem],
        scratch_shapes=[
            pltpu.VMEM((micro * rows, LANES), F32),
            pltpu.VMEM((micro * rows, LANES), F32),
            pltpu.VMEM((keys, rows), F32),
            pltpu.VMEM((KVH, 2, keys, LANES), BF),
            pltpu.VMEM((KVH, 2, LANES, keys), BF),
            pltpu.VMEM((rows, HQ * HD), BF),
            pltpu.VMEM((micro, ctx, rows, 2 * LANES), BF),
            pltpu.SemaphoreType.DMA((copies,)),
            pltpu.SemaphoreType.DMA((copies,)),
            pltpu.SemaphoreType.DMA((micro,)),
        ],
        compiler_params=pltpu.CompilerParams(
            collective_id=1, has_side_effects=True, vmem_limit_bytes=VMEM_LIMIT
        ),
        name="attention_forward",
    )(order, lens, x, wq, wo, bias_qkv, gain_attn, gain_mlp, freq)


def mlp_kernel(
    size, h2, gd, wgu, wd,
    out, gh2, grads,
    hbuf, turned_h, turned_g, acc_out, acc_gh, dgate, dup, ddown,
    sib_out, sib_in, par_out, par_in, keep_sum, stage, send, recv, out_sem,
):
    micro, rows, width, replicas, padded = size
    quarter = replicas * padded
    both = 2 * rows
    f, c = lax.axis_index("fsdp"), lax.axis_index("ctx")
    t = f % TP
    core = t % 2
    mine, theirs = t - core, flip2(t) - core
    sib, par = (flip1(f), c), (flip2(f), c)
    enter([sib, par])
    links = Links(send, recv)
    from_sib, from_par = [], []
    for m in range(micro):
        hbuf[m, t] = h2[m]
        from_sib.append(links.put(hbuf.at[m, t], hbuf.at[m, t], sib))
        from_par.append(links.put(hbuf.at[m, t], hbuf.at[m, t], par))
    from_cross = [None] * micro

    def forward_on(m):
        links.arrive(from_par[m], hbuf.at[m, flip2(t)])
        from_cross[m] = links.put(hbuf.at[m, flip2(t)], hbuf.at[m, flip2(t)], sib)

    def chunk(m, side, first, j):
        at = pl.multiple_of(j * CHUNK, CHUNK)
        up_at = pl.multiple_of(quarter + j * CHUNK, CHUNK)
        hidden_in = hbuf[m, pl.ds(side, 2)].reshape(both, width)
        grad_in = gd[m, pl.ds(side, 2)].reshape(both, width)
        w_gate = wgu[:, pl.ds(at, CHUNK)]
        w_up = wgu[:, pl.ds(up_at, CHUNK)]
        w_down = wd[pl.ds(at, CHUNK), :]
        gate = dot(hidden_in, w_gate)
        up = dot(hidden_in, w_up)
        gm = dot_nt(grad_in, w_down)
        sg = 0.5 * jnp.tanh(0.5 * gate) + 0.5
        silu = gate * sg
        mb = (silu * up).astype(BF)
        ggate = (gm * up * (sg + silu * (1.0 - sg))).astype(BF)
        gup = (gm * silu).astype(BF)
        acc_out[...] += dot(mb, w_down)
        acc_gh[...] += dot_nt(ggate, w_gate) + dot_nt(gup, w_up)
        if first:
            dgate[:, pl.ds(at, CHUNK)] = dot(turned_h[...], ggate)
            dup[:, pl.ds(at, CHUNK)] = dot(turned_h[...], gup)
            ddown[:, pl.ds(at, CHUNK)] = dot(turned_g[...], mb)
        else:
            dgate[:, pl.ds(at, CHUNK)] += dot(turned_h[...], ggate)
            dup[:, pl.ds(at, CHUNK)] += dot(turned_h[...], gup)
            ddown[:, pl.ds(at, CHUNK)] += dot(turned_g[...], mb)

    def compute(m, side, first, middle):
        turned_h[...] = hbuf[m, pl.ds(side, 2)].reshape(both, width).T
        turned_g[...] = gd[m, pl.ds(side, 2)].reshape(both, width).T
        acc_out[...] = jnp.zeros_like(acc_out)
        acc_gh[...] = jnp.zeros_like(acc_gh)
        chunks = quarter // CHUNK

        def body(j, carry):
            chunk(m, side, first, j)
            return carry

        lax.fori_loop(0, 1, body, 0)
        middle()
        lax.fori_loop(1, chunks, body, 0)

    def share(step):
        here = pl.multiple_of(core * rows, rows)
        there = pl.multiple_of(rows - core * rows, rows)
        ats = []
        for k, acc in enumerate((acc_gh, acc_out)):
            sib_out[step, k] = acc[pl.ds(there, rows), :].astype(BF)
            ats.append(links.put(sib_out.at[step, k], sib_in.at[step, k], sib))
            keep_sum[k] = acc[pl.ds(here, rows), :]
        return ats

    def pass_on(step, m, ats):
        got = []
        for k, at in enumerate(ats):
            links.arrive(at, sib_in.at[step, k])
            par_out[m, k] = (keep_sum[k] + sib_in[step, k].astype(F32)).astype(BF)
            got.append(links.put(par_out.at[m, k], par_in.at[m, k], par))
        return got

    def stay(step, m, ats):
        for k, at in enumerate(ats):
            links.arrive(at, sib_in.at[step, k])
            (gh2, out)[k][m] = keep_sum[k] + sib_in[step, k].astype(F32)

    def finish(m, ats):
        for k, (at, ref) in enumerate(zip(ats, (gh2, out))):
            links.arrive(at, par_in.at[m, k])
            ref[m] = ref[m] + par_in[m, k].astype(F32)

    plan = [(0, True)] + [(m, False) for m in range(micro)] + [(m, True) for m in range(1, micro)]
    waiting = None
    sums = [None] * micro
    ready_own = [False] * micro
    for step, (m, own) in enumerate(plan):
        if own:
            links.arrive(from_sib[m], hbuf.at[m, flip1(t)])
        else:
            links.arrive(from_cross[m], hbuf.at[m, flip2(flip1(t))])

        def middle(step=step):
            if step < micro:
                forward_on(step)
            if step > 0:
                last_m, last_own = plan[step - 1]
                if last_own:
                    stay(step - 1, last_m, waiting)
                else:
                    sums[last_m] = pass_on(step - 1, last_m, waiting)

        compute(m, mine if own else theirs, step == 0, middle)
        waiting = share(step)
    high = width // (replicas * TP)
    copies = []
    for replica in range(replicas):
        for k in range(PIECES):
            slot = len(copies) % 2
            if len(copies) >= 2:
                copies[-2].wait()
            if k < 2 * TP:
                at = (replica * TP + k // 2) * high
                stage[slot] = (dgate, dup)[k % 2][at : at + high, :].astype(BF)
            else:
                for q in range(replicas):
                    at = (k - 2 * TP) * replicas + q
                    stage[slot, :, q * padded : (q + 1) * padded] = ddown[
                        at * high : (at + 1) * high, replica * padded : (replica + 1) * padded
                    ].astype(BF)
            copy = pltpu.make_async_copy(stage.at[slot], grads.at[replica, k], out_sem.at[slot])
            copy.start()
            copies.append(copy)
    last_m, last_own = plan[-1]
    if last_own:
        stay(len(plan) - 1, last_m, waiting)
    else:
        sums[last_m] = pass_on(len(plan) - 1, last_m, waiting)
    for m in range(micro):
        finish(m, sums[m])
    for copy in copies[-2:]:
        copy.wait()
    links.drain()


def mlp(n, h2, gd, wgu, wd):
    micro, rows, width = h2.shape
    replicas = n // TP
    padded = wd.shape[0] // replicas
    quarter = replicas * padded
    vmem = pl.BlockSpec(memory_space=pltpu.VMEM)
    steps = 2 * micro
    copies = micro * 3 + steps * 2 + micro * 2
    return pl.pallas_call(
        functools.partial(mlp_kernel, (micro, rows, width, replicas, padded)),
        out_shape=(
            jax.ShapeDtypeStruct((micro, rows, width), F32),
            jax.ShapeDtypeStruct((micro, rows, width), F32),
            jax.ShapeDtypeStruct((replicas, PIECES, width // n, quarter), BF),
        ),
        in_specs=[vmem] * 4,
        out_specs=[vmem, vmem, pl.BlockSpec(memory_space=pl.ANY)],
        scratch_shapes=[
            pltpu.VMEM((micro, TP, rows, width), BF),
            pltpu.VMEM((width, 2 * rows), BF),
            pltpu.VMEM((width, 2 * rows), BF),
            pltpu.VMEM((2 * rows, width), F32),
            pltpu.VMEM((2 * rows, width), F32),
            pltpu.VMEM((width, quarter), F32),
            pltpu.VMEM((width, quarter), F32),
            pltpu.VMEM((width, quarter), F32),
            pltpu.VMEM((steps, 2, rows, width), BF),
            pltpu.VMEM((steps, 2, rows, width), BF),
            pltpu.VMEM((micro, 2, rows, width), BF),
            pltpu.VMEM((micro, 2, rows, width), BF),
            pltpu.VMEM((2, rows, width), F32),
            pltpu.VMEM((2, width // n, quarter), BF),
            pltpu.SemaphoreType.DMA((copies,)),
            pltpu.SemaphoreType.DMA((copies,)),
            pltpu.SemaphoreType.DMA((2,)),
        ],
        compiler_params=pltpu.CompilerParams(
            collective_id=2, has_side_effects=True, vmem_limit_bytes=VMEM_LIMIT
        ),
        name="mlp",
    )(h2, gd, wgu, wd)


def add_into(dst, a, b):
    width = dst.shape[-1]
    step = 256 if width % 256 == 0 else LANES

    def body(k, carry):
        at = pl.ds(pl.multiple_of(k * step, step), step)
        dst[:, at] = (a[:, at].astype(F32) + b[:, at].astype(F32)).astype(BF)
        return carry

    lax.fori_loop(0, width // step, body, 0)


class Sums:
    def __init__(self, n, ctx, grads, fin, scratch):
        self.n, self.ctx, self.grads, self.fin = n, ctx, grads, fin
        (
            self.total, self.peer_in, self.pre, self.suf, self.suf_out, self.land,
            self.core_o, self.par_o, self.ring_o, self.core_q, self.par_q, self.ring_q,
            self.vec, self.vec_in,
            self.ys, self.yr, self.ps, self.pr, self.ss, self.sr, self.fs, self.fr,
            self.asend, self.arecv, self.own_sem, self.out_sem,
        ) = scratch
        self.replicas = n // TP
        self.f, self.c = lax.axis_index("fsdp"), lax.axis_index("ctx")
        f, c = self.f, self.c
        self.t, self.r = f % TP, f // TP
        self.core, self.side = self.t % 2, self.t // 2
        self.sib, self.par, self.cross = (flip1(f), c), (flip2(f), c), (flip2(flip1(f)), c)
        self.peers = [((f + TP * j) % n, c) for j in range(1, self.replicas)]
        self.left, self.right = (f, (c + ctx - 1) % ctx), (f, (c + 1) % ctx)
        self.links = Links(self.asend, self.arecv)

    @staticmethod
    def scratch(n, high, wide, width, proj):
        replicas = n // TP
        sems = pltpu.SemaphoreType.DMA
        peers = replicas - 1
        return [
            pltpu.VMEM((ALL_PIECES, high, wide), BF),
            pltpu.VMEM((peers, PIECES, high, wide), BF),
            pltpu.VMEM((ALL_PIECES, high, wide), BF),
            pltpu.VMEM((ALL_PIECES, high, wide), BF),
            pltpu.VMEM((RING, high, wide), BF),
            pltpu.VMEM((2 * TP, high, wide), BF),
            pltpu.VMEM((replicas, 2, high, width), BF),
            pltpu.VMEM((replicas, high, width), BF),
            pltpu.VMEM((peers, high, width), BF),
            pltpu.VMEM((replicas, 2, high, proj), BF),
            pltpu.VMEM((replicas, high, proj), BF),
            pltpu.VMEM((peers, high, proj), BF),
            pltpu.VMEM((3, VEC, LANES), F32),
            pltpu.VMEM((2 + peers, VEC, LANES), F32),
            sems((peers * PIECES,)), sems((peers * PIECES,)),
            sems((ALL_PIECES,)), sems((ALL_PIECES,)), sems((ALL_PIECES,)), sems((ALL_PIECES,)),
            sems((2 * TP,)), sems((2 * TP,)),
            sems((6 + 3 * peers,)), sems((6 + 3 * peers,)), sems((1,)), sems((ALL_PIECES,)),
        ]

    def around(self):
        return [self.sib, self.par, self.cross] + self.peers + [self.left, self.right]

    def peer_copy(self, j, k):
        at = j * PIECES + k
        return pltpu.make_async_remote_copy(
            src_ref=self.grads.at[(self.r + j + 1) % self.replicas, k],
            dst_ref=self.peer_in.at[j, k],
            send_sem=self.ys.at[at],
            recv_sem=self.yr.at[at],
            device_id=self.peers[j],
            device_id_type=MESH,
        )

    def own_copy(self):
        return pltpu.make_async_copy(
            self.grads.at[self.r], self.total.at[pl.ds(0, PIECES)], self.own_sem.at[0]
        )

    def start(self, ahead):
        self.own_copy().start()
        for k in range(ahead):
            for j in range(self.replicas - 1):
                self.peer_copy(j, k).start()
        self.ahead = ahead

    def pre_copy(self, k, src):
        return pltpu.make_async_remote_copy(
            src_ref=src.at[k], dst_ref=self.pre.at[k], send_sem=self.ps.at[k],
            recv_sem=self.pr.at[k], device_id=self.right, device_id_type=MESH,
        )

    def suf_copy(self, k, src):
        return pltpu.make_async_remote_copy(
            src_ref=src, dst_ref=self.suf.at[k], send_sem=self.ss.at[k],
            recv_sem=self.sr.at[k], device_id=self.left, device_id_type=MESH,
        )

    def fin_copy(self, k, slot):
        return pltpu.make_async_remote_copy(
            src_ref=self.suf.at[k], dst_ref=self.land.at[slot], send_sem=self.fs.at[k],
            recv_sem=self.fr.at[slot], device_id=(self.f - self.t + k // 2, self.c),
            device_id_type=MESH,
        )

    def out_copy(self, k, src):
        return pltpu.make_async_copy(src.at[k], self.fin.at[k], self.out_sem.at[k])

    def tick(self, time):
        c, ctx, total = self.c, self.ctx, self.total

        @pl.when(time + self.ahead < PIECES)
        def _():
            for j in range(self.replicas - 1):
                self.peer_copy(j, time + self.ahead).start()

        @pl.when(time < PIECES)
        def _():
            for j in range(self.replicas - 1):
                self.peer_copy(j, time).wait_recv()
                add_into(total.at[time], total.at[time], self.peer_in.at[j, time])

        k = time - c

        @pl.when((k >= 0) & (k < ALL_PIECES))
        def _():
            @pl.when(c > 0)
            def _():
                self.pre_copy(k, total).wait_recv()
                add_into(self.pre.at[k], self.pre.at[k], total.at[k])

                @pl.when(c < ctx - 1)
                def _():
                    self.pre_copy(k, self.pre).start()

            @pl.when(c == 0)
            def _():
                self.pre_copy(k, total).start()

        k2 = time - (ctx - 1 - c)

        @pl.when((k2 >= 0) & (k2 < ALL_PIECES))
        def _():
            @pl.when(c < ctx - 1)
            def _():
                self.suf_copy(k2, total.at[k2]).wait_recv()

            @pl.when((c > 0) & (c < ctx - 1))
            def _():
                @pl.when(k2 >= RING)
                def _():
                    self.suf_copy(k2 - RING, self.suf_out.at[(k2 - RING) % RING]).wait_send()

                add_into(self.suf_out.at[k2 % RING], self.suf.at[k2], total.at[k2])
                self.suf_copy(k2, self.suf_out.at[k2 % RING]).start()

            @pl.when(c == ctx - 1)
            def _():
                self.suf_copy(k2, total.at[k2]).start()

        k3 = time - jnp.maximum(c, ctx - 1 - c)

        @pl.when((k3 >= 0) & (k3 < ALL_PIECES))
        def _():
            @pl.when(c == 0)
            def _():
                add_into(self.suf.at[k3], self.suf.at[k3], total.at[k3])

            @pl.when((c > 0) & (c < ctx - 1))
            def _():
                add_into(self.suf.at[k3], self.suf.at[k3], self.pre.at[k3])

            @pl.when((k3 < 2 * TP) & (k3 // 2 != self.t))
            def _():
                @pl.when(c == ctx - 1)
                def _():
                    self.fin_copy_from(k3, self.pre).start()

                @pl.when(c < ctx - 1)
                def _():
                    self.fin_copy_from(k3, self.suf).start()

            @pl.when((k3 >= 2 * TP) | (k3 // 2 == self.t))
            def _():
                @pl.when(c == ctx - 1)
                def _():
                    self.out_copy(k3, self.pre).start()

                @pl.when(c < ctx - 1)
                def _():
                    self.out_copy(k3, self.suf).start()

    def fin_copy_from(self, k, src):
        return pltpu.make_async_remote_copy(
            src_ref=src.at[k], dst_ref=self.land.at[2 * self.t + k % 2], send_sem=self.fs.at[k],
            recv_sem=self.fr.at[2 * self.t + k % 2],
            device_id=(self.f - self.t + k // 2, self.c), device_id_type=MESH,
        )

    @property
    def ticks(self):
        return ALL_PIECES + self.ctx - 1

    def close(self):
        c, ctx = self.c, self.ctx

        def arrive(k, carry):
            @pl.when(k // 2 != self.t)
            def _():
                pltpu.make_async_remote_copy(
                    src_ref=self.land.at[k], dst_ref=self.land.at[k], send_sem=self.fs.at[k],
                    recv_sem=self.fr.at[k], device_id=(self.f - self.t + k // 2, c),
                    device_id_type=MESH,
                ).wait_recv()
                self.out_copy(k, self.land).start()
                self.fin_copy_from(k, self.suf).wait_send()

            return carry

        lax.fori_loop(0, 2 * TP, arrive, 0)

        def settle(k, carry):
            @pl.when(c < ctx - 1)
            def _():
                self.pre_copy(k, self.total).wait_send()

            @pl.when((c == ctx - 1) | ((c > 0) & (k >= ALL_PIECES - RING)))
            def _():
                self.suf_copy(k, self.total.at[k]).wait_send()

            self.out_copy(k, self.suf).wait()
            return carry

        lax.fori_loop(0, ALL_PIECES, settle, 0)

        def peers(k, carry):
            for j in range(self.replicas - 1):
                self.peer_copy(j, k).wait_send()
            return carry

        lax.fori_loop(0, PIECES, peers, 0)
        self.links.drain()


    def fold(self, own, got_core, got_par, got_ring, place, extra=None):
        replicas = self.replicas
        at = self.links.put(own.at[:, :, 1 - self.core], got_core, self.sib)
        at_vec = None
        if extra is not None:
            at_vec = self.links.put(self.vec.at[0], self.vec_in.at[0], self.sib)
        yield
        self.links.arrive(at, got_core)
        for replica in range(replicas):
            for s in range(2):
                add_into(
                    got_core.at[replica, s], got_core.at[replica, s],
                    own.at[replica, s, self.core],
                )
        at = self.links.put(got_core.at[:, 1 - self.side], got_par, self.par)
        if extra is not None:
            self.links.arrive(at_vec, self.vec_in.at[0])
            self.vec[1] = self.vec[0] + self.vec_in[0]
            at_vec = self.links.put(self.vec.at[1], self.vec_in.at[1], self.par)
        yield
        self.links.arrive(at, got_par)
        for replica in range(replicas):
            add_into(got_par.at[replica], got_par.at[replica], got_core.at[replica, self.side])
        ats, vec_ats = [], []
        if extra is not None:
            self.links.arrive(at_vec, self.vec_in.at[1])
            self.vec[2] = self.vec[1] + self.vec_in[1]
        for j, peer in enumerate(self.peers):
            ats.append(
                self.links.put(got_par.at[(self.r + j + 1) % replicas], got_ring.at[j], peer)
            )
            if extra is not None:
                vec_ats.append(self.links.put(self.vec.at[2], self.vec_in.at[2 + j], peer))
        yield
        width = got_ring.shape[-1]
        for j, at in enumerate(ats):
            self.links.arrive(at, got_ring.at[j])
            source = got_par.at[self.r] if j == 0 else place
            add_into(place, source, got_ring.at[j])
        if extra is not None:
            vec = self.vec[2]
            for j, at in enumerate(vec_ats):
                self.links.arrive(at, self.vec_in.at[2 + j])
                vec = vec + self.vec_in[2 + j]
            extra[...] = vec.astype(BF)
        yield


def backward_kernel(
    size, merged, order, lens, gh2, x2, gy, x, wq, wo, gain_attn, gain_mlp, freq, qs, kv, lse, obt,
    grads, dx, *rest
):
    n, micro, rows, ctx = size
    outs = 1 if merged else 3
    fin, rest = rest[:outs], rest[outs:]
    (
        cos_ref, sin_ref, bias_ref, kvar, kvar_turned, vvar, go_ref, gp, h1t, gk, gv, part, land,
        att_o, att_q, vec_wide, send, recv,
    ), rest = rest[:18], rest[18:]
    group = HQ // KVH
    pairs = HQ // 2
    width = HQ * HD
    replicas = n // TP
    high = width // n
    proj = wq.shape[1]
    scale = 1.0 / math.sqrt(HD)
    f, c = lax.axis_index("fsdp"), lax.axis_index("ctx")
    others = [(f, (c + j) % ctx) for j in range(1, ctx)]
    back = [(c - j + ctx) % ctx for j in range(1, ctx)]
    if merged:
        sums = Sums(n, ctx, grads, fin[0], rest)
        enter(others + sums.around())
        sums.start(2)
    else:
        enter(others)
    links = Links(send, recv)
    arrivals = []
    for m in range(micro):
        fill_tables(m, rows, c, freq, order, lens, cos_ref, sin_ref)
        stream = x2[m]
        inverse = inverse_norm(stream)
        normed = stream * inverse
        grad = gh2[m]
        term = jnp.sum(grad * normed, axis=0, keepdims=True)
        at = proj + width
        vec_wide[:, at : at + width] = term if m == 0 else vec_wide[:, at : at + width] + term
        grad = grad * gain_mlp[...]
        grad = gy[m].astype(F32) + inverse * (
            grad - normed * jnp.mean(grad * normed, axis=1, keepdims=True)
        )
        dx[m] = grad
        spread = dot_nt(grad.astype(BF), wo[...]).astype(BF)
        for p in range(pairs):
            go_ref[m, p] = spread[:, p * LANES : (p + 1) * LANES]
    for k in range(n):
        term = dot(obt[0, k * high : (k + 1) * high, :], dx[0].astype(BF))
        for m in range(1, micro):
            term = term + dot(obt[m, k * high : (k + 1) * high, :], dx[m].astype(BF))
        att_o[k // TP, (k // 2) % 2, k % 2] = term.astype(BF)
    if merged:
        sums.total[PIECES] = jnp.zeros(sums.total.shape[1:], BF)
        sums.total[PIECES + 1] = jnp.zeros(sums.total.shape[1:], BF)
        sums.own_copy().wait()
        fold_o = sums.fold(
            att_o, sums.core_o, sums.par_o, sums.ring_o,
            sums.total.at[PIECES, :, pl.ds(0, width)],
        )
        next(fold_o)
    for m in range(micro):
        if merged and m > 0:
            next(fold_o)
        fill_bias(m, rows, c, order, lens, bias_ref)
        both = kv[m].reshape(ctx * rows, 2 * LANES).astype(F32)
        fill_heads(both[:, :LANES], kvar)
        fill_heads_turned(both[:, :LANES], kvar_turned)
        fill_heads(both[:, LANES:], vvar)
        gk[...] = jnp.zeros_like(gk)
        gv[...] = jnp.zeros_like(gv)
        cosine = cos_ref[m * rows : (m + 1) * rows, :]
        sine = sin_ref[m * rows : (m + 1) * rows, :]

        def pair(p, carry):
            query = qs[m, p]
            go = go_ref[m, p]
            grad_query = jnp.zeros((LANES, rows), F32)
            for parity in range(2):
                head = 2 * p + parity
                g = head // group
                scores = dot_nt(kvar[g, parity], query) + bias_ref[...]
                probs = jnp.exp(scores - lse[m, pl.ds(head, 1), :])
                grad_probs = dot_nt(vvar[g, parity], go)
                delta = jnp.sum(probs * grad_probs, axis=0, keepdims=True)
                grad_scores = (probs * (grad_probs - delta)).astype(BF)
                grad_query = grad_query + dot(kvar_turned[g, parity], grad_scores)
                gk[g, parity] += dot(grad_scores, query)
                gv[g, parity] += dot(probs.astype(BF), go)
            turned = grad_query.T * scale
            turned = turned * cosine - swap_halves(turned) * sine
            at = pl.multiple_of(p * LANES, LANES)
            gp[m * rows : (m + 1) * rows, pl.ds(at, LANES)] = turned.astype(BF)
            if merged:
                step = m * pairs + p

                @pl.when(step % 3 != 2)
                def _():
                    sums.tick(step - step // 3)

            return carry

        lax.fori_loop(0, pairs, pair, 0)
        low = lax.broadcasted_iota(jnp.int32, (ctx * rows, LANES), 1) < HD
        for k, acc in enumerate((gk, gv)):
            first = acc[0, 0] + pltpu.roll(acc[0, 1], HD, 1)
            second = pltpu.roll(acc[1, 0], HD, 1) + acc[1, 1]
            whole = jnp.where(low, first, second).astype(BF)
            part[m, :, :, k * LANES : (k + 1) * LANES] = whole.reshape(ctx, rows, LANES)
        arrivals.append(
            [links.put(part.at[m, other[1]], land.at[m, c], other) for other in others]
        )
    if merged:
        next(fold_o)
    for m in range(micro):
        stream = x[m].astype(F32)
        h1t[:, m * rows : (m + 1) * rows] = (
            (stream * inverse_norm(stream) * gain_attn[...]).T.astype(BF)
        )
    for m in range(micro):
        total = part[m, c].astype(F32)
        for at, source in zip(arrivals[m], back):
            links.arrive(at, land.at[m, source])
            total = total + land[m, source].astype(F32)
        cosine = cos_ref[m * rows : (m + 1) * rows, :]
        sine = sin_ref[m * rows : (m + 1) * rows, :]
        grad_keys = total[:, :LANES]
        grad_keys = grad_keys * cosine - swap_halves(grad_keys) * sine
        gp[m * rows : (m + 1) * rows, width : width + LANES] = grad_keys.astype(BF)
        gp[m * rows : (m + 1) * rows, width + LANES :] = total[:, LANES:].astype(BF)
    for k in range(n):
        term = dot(h1t[k * high : (k + 1) * high, :], gp[...])
        att_q[k // TP, (k // 2) % 2, k % 2] = term.astype(BF)
    for m in range(micro):
        grad_project = gp[m * rows : (m + 1) * rows, :]
        stream = x[m].astype(F32)
        inverse = inverse_norm(stream)
        normed = stream * inverse
        term = jnp.sum(grad_project.astype(F32), axis=0, keepdims=True)
        vec_wide[:, :proj] = term if m == 0 else vec_wide[:, :proj] + term
        grad = dot_nt(grad_project, wq[...])
        term = jnp.sum(grad * normed, axis=0, keepdims=True)
        at = slice(proj, proj + width)
        vec_wide[:, at] = term if m == 0 else vec_wide[:, at] + term
        grad = grad * gain_attn[...]
        dx[m] = dx[m] + inverse * (
            grad - normed * jnp.mean(grad * normed, axis=1, keepdims=True)
        )
    vec = sums.vec.at[0] if merged else fin[2]
    vec[...] = jnp.zeros((VEC, LANES), F32)
    for k in range(vec_wide.shape[1] // LANES):
        vec[k : k + 1, :] = vec_wide[:, k * LANES : (k + 1) * LANES]
    if merged:
        next(fold_o)
        done = micro * pairs - (micro * pairs) // 3
        fold_sums(sums, att_q, done, width, proj)
    else:
        fin[0][...] = att_o[...]
        fin[1][...] = att_q[...]
    links.drain()


def fold_sums(sums, att_q, done, width, proj):
    fold_q = sums.fold(
        att_q, sums.core_q, sums.par_q, sums.ring_q,
        sums.total.at[PIECES + 1, :, pl.ds(0, proj)],
        sums.total.at[PIECES + 1, pl.ds(0, VEC), pl.ds(proj, LANES)],
    )
    between = max(0, min(2, PIECES - done))

    def body(k, carry):
        sums.tick(k)
        return carry

    next(fold_q)
    for _ in range(between):
        sums.tick(jnp.int32(done))
        done += 1
        next(fold_q)
    for _ in range(3 - between):
        next(fold_q)
    lax.fori_loop(done, sums.ticks, body, 0)
    sums.close()


def attention_backward(
    n, ctx, order, lens, gh2, x2, gy, x, wq, wo, gain_attn, gain_mlp, freq, qs, kv, lse, obt, grads
):
    micro, rows, width = x.shape
    keys = rows * ctx
    proj = wq.shape[1]
    replicas = n // TP
    high, wide = grads.shape[2:]
    merged = ctx <= 4
    vmem = pl.BlockSpec(memory_space=pltpu.VMEM)
    smem = pl.BlockSpec(memory_space=pltpu.SMEM)
    anywhere = pl.BlockSpec(memory_space=pl.ANY)
    copies = micro * (ctx - 1)
    out_shape = [jax.ShapeDtypeStruct((micro, rows, width), F32)]
    shape_o = (replicas, 2, 2, high, width)
    shape_q = (replicas, 2, 2, high, proj)
    if merged:
        out_shape += [jax.ShapeDtypeStruct((ALL_PIECES, high, wide), BF)]
    else:
        out_shape += [
            jax.ShapeDtypeStruct(shape_o, BF),
            jax.ShapeDtypeStruct(shape_q, BF),
            jax.ShapeDtypeStruct((VEC, LANES), F32),
        ]
    result = pl.pallas_call(
        functools.partial(backward_kernel, (n, micro, rows, ctx), merged),
        out_shape=out_shape,
        in_specs=[smem, smem] + [vmem] * 13 + [anywhere],
        out_specs=[vmem] + ([anywhere] if merged else [vmem] * 3),
        scratch_shapes=[
            pltpu.VMEM((micro * rows, LANES), F32),
            pltpu.VMEM((micro * rows, LANES), F32),
            pltpu.VMEM((keys, rows), F32),
            pltpu.VMEM((KVH, 2, keys, LANES), BF),
            pltpu.VMEM((KVH, 2, LANES, keys), BF),
            pltpu.VMEM((KVH, 2, keys, LANES), BF),
            pltpu.VMEM((micro, HQ // 2, rows, LANES), BF),
            pltpu.VMEM((micro * rows, proj), BF),
            pltpu.VMEM((width, micro * rows), BF),
            pltpu.VMEM((KVH, 2, keys, LANES), F32),
            pltpu.VMEM((KVH, 2, keys, LANES), F32),
            pltpu.VMEM((micro, ctx, rows, 2 * LANES), BF),
            pltpu.VMEM((micro, ctx, rows, 2 * LANES), BF),
            pltpu.VMEM(shape_o, BF),
            pltpu.VMEM(shape_q, BF),
            pltpu.VMEM((1, proj + 2 * width), F32),
            pltpu.SemaphoreType.DMA((copies,)),
            pltpu.SemaphoreType.DMA((copies,)),
        ]
        + (Sums.scratch(n, high, wide, width, proj) if merged else []),
        compiler_params=pltpu.CompilerParams(
            collective_id=3, has_side_effects=True, vmem_limit_bytes=VMEM_LIMIT
        ),
        name="attention_backward",
    )(order, lens, gh2, x2, gy, x, wq, wo, gain_attn, gain_mlp, freq, qs, kv, lse, obt, grads)
    if merged:
        return result
    dx, att_o, att_q, vec = result
    return dx, reduce_grads(n, ctx, grads, att_o, att_q, vec)


def reduce_kernel(n, ctx, grads, att_o, att_q, vec, fin, *scratch):
    sums = Sums(n, ctx, grads, fin, scratch)
    width, proj = att_o.shape[-1], att_q.shape[-1]
    enter(sums.around())
    sums.start(2)
    sums.vec[0] = vec[...]
    sums.total[PIECES] = jnp.zeros(sums.total.shape[1:], BF)
    sums.total[PIECES + 1] = jnp.zeros(sums.total.shape[1:], BF)
    sums.own_copy().wait()
    for _ in sums.fold(
        att_o, sums.core_o, sums.par_o, sums.ring_o, sums.total.at[PIECES, :, pl.ds(0, width)]
    ):
        pass
    fold_sums(sums, att_q, 0, width, proj)


def reduce_grads(n, ctx, grads, att_o, att_q, vec):
    high, wide = grads.shape[2:]
    vmem = pl.BlockSpec(memory_space=pltpu.VMEM)
    anywhere = pl.BlockSpec(memory_space=pl.ANY)
    return pl.pallas_call(
        functools.partial(reduce_kernel, n, ctx),
        out_shape=jax.ShapeDtypeStruct((ALL_PIECES, high, wide), BF),
        in_specs=[anywhere, vmem, vmem, vmem],
        out_specs=anywhere,
        scratch_shapes=Sums.scratch(n, high, wide, att_o.shape[-1], att_q.shape[-1]),
        compiler_params=pltpu.CompilerParams(
            collective_id=4, has_side_effects=True, vmem_limit_bytes=VMEM_LIMIT
        ),
        name="reduce_grads",
    )(grads, att_o, att_q, vec)


def finish_kernel(size, fin, g_gu, g_down, g_qkv, g_out, vec, turn):
    n, units, padded, proj, width = size
    replicas = n // TP
    high = width // n
    for half in range(2):
        for k in range(TP):
            whole = fin[2 * k + half].astype(F32)
            for q in range(replicas):
                at = ((half * replicas + q) * TP + k) * units
                g_gu[:, at : at + units] = whole[:, q * padded : q * padded + units]
    for k in range(n):
        at = (k % replicas) * padded
        turn[k * high : (k + 1) * high, :] = fin[2 * TP + k // replicas, :, at : at + padded].astype(
            F32
        )
    g_down[...] = turn[...].T[:units, :]
    g_out[...] = fin[PIECES, :, :width].astype(F32)
    g_qkv[...] = fin[PIECES + 1, :, :proj].astype(F32)
    vec[...] = fin[PIECES + 1, :VEC, proj : proj + LANES].astype(F32)


def finish_grads(n, fin, units, padded, proj, width):
    high = width // n
    vmem = pl.BlockSpec(memory_space=pltpu.VMEM)
    return pl.pallas_call(
        functools.partial(finish_kernel, (n, units, padded, proj, width)),
        out_shape=(
            jax.ShapeDtypeStruct((high, 2 * n * units), F32),
            jax.ShapeDtypeStruct((units, width), F32),
            jax.ShapeDtypeStruct((high, proj), F32),
            jax.ShapeDtypeStruct((high, width), F32),
            jax.ShapeDtypeStruct((VEC, LANES), F32),
        ),
        in_specs=[vmem],
        out_specs=[vmem] * 5,
        scratch_shapes=[pltpu.VMEM((width, padded), F32)],
        compiler_params=pltpu.CompilerParams(vmem_limit_bytes=VMEM_LIMIT),
        name="finish_grads",
    )(fin)


def pad_to(v, axis, size):
    pads = [(0, 0)] * v.ndim
    pads[axis] = (0, size - v.shape[axis])
    return jnp.pad(v, pads)


def local(
    inputs, cotangent, lengths, order, w_qkv, b_qkv, w_out, norm_attn, norm_mlp, w_gate_up, w_down
):
    n = lax.axis_size("fsdp")
    ctx = lax.axis_size("ctx")
    replicas = n // TP
    x, gy = inputs[0], cotangent[0]
    micro, rows, width = x.shape
    high = w_gate_up.shape[0]
    units = w_down.shape[0]
    padded = -(-units // LANES) * LANES
    quarter = replicas * padded
    proj = w_qkv.shape[1]
    qk = (HQ + KVH) * HD
    vw = KVH * HD

    wgu = w_gate_up.reshape(high, 2, replicas, TP, units)
    wgu = pad_to(wgu.transpose(3, 0, 1, 2, 4), 4, padded).reshape(TP, high, 2 * quarter)
    wd = pad_to(w_down, 0, padded)
    small = jnp.concatenate(
        [
            pad_to(b_qkv, 0, 2 * LANES).reshape(2, LANES),
            pad_to(norm_attn, 0, LANES)[None],
            pad_to(norm_mlp, 0, LANES)[None],
            jnp.zeros((12, LANES), BF),
        ]
    )
    wq_all, wo_all, sm_all, wgu_t, wd_t, gd_all = gather_weights(
        n, w_qkv, w_out, small, wgu, wd, gy
    )
    wq_all = wq_all.reshape(width, proj)
    wo_all = wo_all.reshape(width, width)
    bias = sm_all[:, :2].reshape(n, 2 * LANES)[:, : b_qkv.shape[0]].reshape(1, proj).astype(F32)
    gain_attn = sm_all[:, 2, :high].reshape(1, width).astype(F32)
    gain_mlp = sm_all[:, 3, :high].reshape(1, width).astype(F32)
    wgu_t = wgu_t.reshape(width, 2 * quarter)
    wd_t = wd_t.reshape(quarter, width)

    half = HD // 2
    freqs = np.power(np.float32(ROPE_BASE), -(np.arange(half, dtype=np.float32) * (2.0 / HD)))
    freq = jnp.asarray(np.tile(freqs.astype(np.float32), (8, LANES // half)))
    h2, x2, qs, kv, lse, obt = attention_forward(
        ctx, order[0], lengths[0], x, wq_all, wo_all, bias, gain_attn, gain_mlp, freq
    )
    gd_all = gd_all.transpose(1, 0, 2, 3)
    out, gh2, grads = mlp(n, h2, gd_all, wgu_t, wd_t)
    outputs = (x2 + out).astype(BF)
    dx, fin = attention_backward(
        n, ctx, order[0], lengths[0], gh2, x2, gy, x, wq_all, wo_all, gain_attn, gain_mlp, freq,
        qs, kv, lse, obt, grads,
    )
    g_gu, g_down, g_qkv, g_out, vec = finish_grads(n, fin, units, padded, proj, width)
    vec = vec.reshape(VEC * LANES)
    f = lax.axis_index("fsdp")

    def own(first, size):
        return lax.dynamic_slice(vec, (first + f * size,), (size,))

    return (
        outputs[None],
        dx[None],
        g_qkv,
        own(0, qk // n),
        own(qk, vw // n),
        g_out,
        own(proj, high),
        own(proj + width, high),
        g_gu,
        g_down,
    )


def solution(mesh):
    return jax.shard_map(
        local,
        mesh=mesh,
        in_specs=(
            P("fsdp", None, "ctx", None),
            P("fsdp", None, "ctx", None),
            P("fsdp", None, None),
            P("fsdp", None, None),
            P("fsdp", None),
            P("fsdp"),
            P("fsdp", None),
            P("fsdp"),
            P("fsdp"),
            P("fsdp", None),
            P("fsdp", None),
        ),
        out_specs=(
            P("fsdp", None, "ctx", None),
            P("fsdp", None, "ctx", None),
            P("fsdp", None),
            P("fsdp"),
            P("fsdp"),
            P("fsdp", None),
            P("fsdp"),
            P("fsdp"),
            P("fsdp", None),
            P("fsdp", None),
        ),
        check_vma=False,
    )
```

```python
import functools
import math

import jax
import jax.numpy as jnp
import numpy as np
from jax import lax
from jax.experimental import pallas as pl
from jax.experimental.pallas import tpu as pltpu
from jax.sharding import PartitionSpec as P

HQ = 14
KVH = 2
HD = 64
EPSILON = 1e-06
ROPE_BASE = 1000000.0
NEGATIVE = -1e30
TP = 4
LANES = 128
CHUNK = 256
PIECES = 6 * TP
ALL_PIECES = PIECES + 4
RING = 6
HOP = 2
RATE = 3
EARLY = 2
SLOTS = 8
VEC = 32
BF = jnp.bfloat16
F32 = jnp.float32
MESH = pl.DeviceIdType.MESH
VMEM_LIMIT = 60 * 1024 * 1024


def flip1(v):
    return v + 1 - 2 * (v % 2)


def flip2(v):
    return v + 2 - 4 * ((v // 2) % 2)


def dot(a, b):
    return jnp.dot(a, b, preferred_element_type=F32)


def dot_nt(a, b):
    return lax.dot_general(a, b, (((1,), (1,)), ((), ())), preferred_element_type=F32)


class Links:
    def __init__(self, send_sems, recv_sems):
        self.send_sems, self.recv_sems = send_sems, recv_sems
        self.started = []

    def put(self, src, dst, device):
        at = len(self.started)
        copy = pltpu.make_async_remote_copy(
            src_ref=src,
            dst_ref=dst,
            send_sem=self.send_sems.at[at],
            recv_sem=self.recv_sems.at[at],
            device_id=device,
            device_id_type=MESH,
        )
        copy.start()
        self.started.append((src, device))
        return at

    def arrive(self, at, slot):
        pltpu.make_async_remote_copy(
            src_ref=slot,
            dst_ref=slot,
            send_sem=self.send_sems.at[at],
            recv_sem=self.recv_sems.at[at],
            device_id=self.started[at][1],
            device_id_type=MESH,
        ).wait_recv()

    def drain(self):
        for at, (src, device) in enumerate(self.started):
            pltpu.make_async_remote_copy(
                src_ref=src,
                dst_ref=src,
                send_sem=self.send_sems.at[at],
                recv_sem=self.recv_sems.at[at],
                device_id=device,
                device_id_type=MESH,
            ).wait_send()


class Staged:
    def __init__(self, pairs, sems):
        self.copies = [
            pltpu.make_async_copy(src, dst, sems.at[at]) for at, (src, dst) in enumerate(pairs)
        ]
        self.waited = 0
        for copy in self.copies:
            copy.start()

    def need(self, count):
        for copy in self.copies[self.waited : count]:
            copy.wait()
        self.waited = max(self.waited, count)


def enter(devices):
    barrier = pltpu.get_barrier_semaphore()
    for device in devices:
        pl.semaphore_signal(barrier, inc=1, device_id=device, device_id_type=MESH)
    pl.semaphore_wait(barrier, len(devices))


def gather_kernel(
    n, wq, wo, sm, wgu, wd, gd, wq_all, wo_all, sm_all, wgu_t, wd_t, gd_all, send, recv, here
):
    replicas = n // TP
    f, c = lax.axis_index("fsdp"), lax.axis_index("ctx")
    t, r = f % TP, f // TP
    sib, par, cross = (flip1(f), c), (flip2(f), c), (flip2(flip1(f)), c)
    peers = [((f + TP * j) % n, c) for j in range(1, replicas)]
    back = [(f - TP * j + n) % n for j in range(1, replicas)]
    rback = [(r - j + replicas) % replicas for j in range(1, replicas)]
    enter([sib, par, cross] + peers)
    links = Links(send, recv)
    local = []

    def keep(src, dst):
        copy = pltpu.make_async_copy(src, dst, here.at[len(local)])
        copy.start()
        local.append(copy)

    pending = []
    both = []
    for own, every in ((wq, wq_all), (wo, wo_all), (sm, sm_all)):
        ys = [links.put(own, every.at[f], peer) for peer in peers]
        x = links.put(own, every.at[f], par)
        s = links.put(own, every.at[f], sib)
        keep(own, every.at[f])
        both.append((every, ys, x, s))
    gd_x = links.put(gd, gd_all.at[:, t], par)
    gd_s = links.put(gd, gd_all.at[:, t], sib)
    keep(gd, gd_all.at[:, t])
    arrivals = []
    for half in range(2):
        for other, device in ((flip1(t), sib), (flip2(t), par), (flip2(flip1(t)), cross)):
            at = links.put(wgu.at[other, half], wgu_t.at[half, r, t], device)
            arrivals.append((at, half, other))
        keep(wgu.at[t, half], wgu_t.at[half, r, t])
        for j, peer in enumerate(peers):
            at = links.put(wgu.at[t, half], wgu_t.at[half, r, t], peer)
            pending.append((at, wgu_t.at[half, rback[j], t]))
    for j, peer in enumerate(peers):
        at = links.put(wd, wd_t.at[r], peer)
        pending.append((at, wd_t.at[rback[j]]))
    keep(wd, wd_t.at[r])
    later = []
    for every, ys, x, s in both:
        pending.append((s, every.at[flip1(f)]))
        for j, at in enumerate(ys):
            links.arrive(at, every.at[back[j]])
            at_x = links.put(every.at[back[j]], every.at[back[j]], par)
            later.append((every, at_x, flip2(back[j])))
            at_s = links.put(every.at[back[j]], every.at[back[j]], sib)
            pending.append((at_s, every.at[flip1(back[j])]))
        links.arrive(x, every.at[flip2(f)])
        at_s = links.put(every.at[flip2(f)], every.at[flip2(f)], sib)
        pending.append((at_s, every.at[flip2(flip1(f))]))
    for at, half, other in arrivals:
        links.arrive(at, wgu_t.at[half, r, other])
        for j, peer in enumerate(peers):
            at_y = links.put(wgu_t.at[half, r, other], wgu_t.at[half, r, other], peer)
            pending.append((at_y, wgu_t.at[half, rback[j], other]))
    for every, at, slot in later:
        links.arrive(at, every.at[slot])
        at_s = links.put(every.at[slot], every.at[slot], sib)
        pending.append((at_s, every.at[flip1(slot)]))
    links.arrive(gd_x, gd_all.at[:, flip2(t)])
    at_s = links.put(gd_all.at[:, flip2(t)], gd_all.at[:, flip2(t)], sib)
    pending.append((at_s, gd_all.at[:, flip2(flip1(t))]))
    pending.append((gd_s, gd_all.at[:, flip1(t)]))
    for at, slot in pending:
        links.arrive(at, slot)
    links.drain()
    for copy in local:
        copy.wait()


def gather_weights(n, wq, wo, sm, wgu, wd, gd):
    replicas = n // TP
    peers = replicas - 1
    copies = 3 * (4 * peers + 3) + 3 + 2 * (3 + 4 * peers) + peers
    anywhere = pl.BlockSpec(memory_space=pl.ANY)
    high, quarter = wgu.shape[2:]
    shapes = (
        jax.ShapeDtypeStruct((n,) + wq.shape, BF),
        jax.ShapeDtypeStruct((n,) + wo.shape, BF),
        jax.ShapeDtypeStruct((n,) + sm.shape, BF),
        jax.ShapeDtypeStruct((2, replicas, TP, high, quarter), BF),
        jax.ShapeDtypeStruct((replicas,) + wd.shape, BF),
        jax.ShapeDtypeStruct((gd.shape[0], TP) + gd.shape[1:], BF),
    )
    return pl.pallas_call(
        functools.partial(gather_kernel, n),
        out_shape=shapes,
        in_specs=[anywhere] * 6,
        out_specs=[anywhere] * 6,
        scratch_shapes=[
            pltpu.SemaphoreType.DMA((copies,)),
            pltpu.SemaphoreType.DMA((copies,)),
            pltpu.SemaphoreType.DMA((7,)),
        ],
        compiler_params=pltpu.CompilerParams(collective_id=0, has_side_effects=True),
        name="gather_weights",
    )(wq, wo, sm, wgu, wd, gd)


def begin_of(natural, lens, m, count):
    begin = jnp.zeros_like(natural)
    end = jnp.int32(0)
    for j in range(count):
        piece = lens[m, j]
        end = end + piece
        begin = begin + jnp.where(end <= natural, piece, 0)
    return begin


def fill_tables(m, rows, c, freq, order, lens, cos_ref, sin_ref):
    block = rows // 2
    lane = lax.broadcasted_iota(jnp.int32, (block, LANES), 1)
    low = (lane % HD) < (HD // 2)
    for b in range(2):
        natural = order[m, c * 2 + b] * block + lax.broadcasted_iota(
            jnp.int32, (block, LANES), 0
        )
        position = natural - begin_of(natural, lens, m, lens.shape[1])
        angle = position.astype(F32) * freq[0:1, :]
        at = m * rows + b * block
        cos_ref[at : at + block, :] = jnp.cos(angle)
        sine = jnp.sin(angle)
        sin_ref[at : at + block, :] = jnp.where(low, -sine, sine)


def swap_halves(u):
    lane = lax.broadcasted_iota(jnp.int32, u.shape, 1)
    low = (lane % HD) < (HD // 2)
    return jnp.where(low, pltpu.roll(u, LANES - HD // 2, 1), pltpu.roll(u, HD // 2, 1))


def fill_bias(m, rows, c, order, lens, bias_ref):
    block = rows // 2
    lane = lax.broadcasted_iota(jnp.int32, (1, rows), 1)
    query = jnp.where(
        lane < block,
        order[m, c * 2] * block + lane,
        order[m, c * 2 + 1] * block + lane - block,
    )
    begin = begin_of(query, lens, m, lens.shape[1])

    def body(k, carry):
        key = order[m, k] * block + lax.broadcasted_iota(jnp.int32, (block, rows), 0)
        allowed = (key <= query) & (key >= begin)
        at = pl.multiple_of(k * block, block)
        bias_ref[pl.ds(at, block), :] = jnp.where(allowed, 0.0, NEGATIVE)
        return carry

    lax.fori_loop(0, order.shape[1], body, 0)


def fill_heads(whole, var_ref):
    rolled = pltpu.roll(whole, HD, 1)
    low = lax.broadcasted_iota(jnp.int32, whole.shape, 1) < HD
    var_ref[0, 0] = jnp.where(low, whole, 0.0).astype(BF)
    var_ref[0, 1] = jnp.where(low, 0.0, rolled).astype(BF)
    var_ref[1, 0] = jnp.where(low, rolled, 0.0).astype(BF)
    var_ref[1, 1] = jnp.where(low, 0.0, whole).astype(BF)


def fill_heads_turned(whole, var_ref):
    turned = whole.T
    rolled = jnp.concatenate([turned[HD:], turned[:HD]], axis=0)
    low = lax.broadcasted_iota(jnp.int32, turned.shape, 0) < HD
    var_ref[0, 0] = jnp.where(low, turned, 0.0).astype(BF)
    var_ref[0, 1] = jnp.where(low, 0.0, rolled).astype(BF)
    var_ref[1, 0] = jnp.where(low, rolled, 0.0).astype(BF)
    var_ref[1, 1] = jnp.where(low, 0.0, turned).astype(BF)


def inverse_norm(v):
    return lax.rsqrt(jnp.mean(v * v, axis=1, keepdims=True) + EPSILON)


class Forward:
    def __init__(self, size, order, lens, x, freq, outs, scratch):
        self.micro, self.rows, self.ctx = size
        self.order, self.lens, self.x, self.freq = order, lens, x, freq
        self.h2, self.x2, self.qs, self.kv, self.lse, self.obt = outs
        (
            self.cos_ref, self.sin_ref, self.bias_ref, self.kvar, self.vvar, self.ob, self.h1,
            self.land, send, recv, self.out_sem,
        ) = scratch
        f, c = lax.axis_index("fsdp"), lax.axis_index("ctx")
        self.c = c
        self.others = [(f, (c + j) % self.ctx) for j in range(1, self.ctx)]
        self.back = [(c - j + self.ctx) % self.ctx for j in range(1, self.ctx)]
        self.links = Links(send, recv)
        self.arrivals, self.out_copies = [], []

    @staticmethod
    def scratch(micro, rows, ctx, width):
        keys = rows * ctx
        copies = micro * (ctx - 1)
        return [
            pltpu.VMEM((micro * rows, LANES), F32),
            pltpu.VMEM((micro * rows, LANES), F32),
            pltpu.VMEM((keys, rows), F32),
            pltpu.VMEM((KVH, 2, keys, LANES), BF),
            pltpu.VMEM((KVH, 2, LANES, keys), BF),
            pltpu.VMEM((micro, rows, HQ * HD), BF),
            pltpu.VMEM((micro, rows, width), BF),
            pltpu.VMEM((micro, ctx, rows, 2 * LANES), BF),
            pltpu.SemaphoreType.DMA((copies,)),
            pltpu.SemaphoreType.DMA((copies,)),
            pltpu.SemaphoreType.DMA((micro,)),
        ]

    @staticmethod
    def shapes(micro, rows, ctx, width):
        return (
            jax.ShapeDtypeStruct((micro, rows, width), BF),
            jax.ShapeDtypeStruct((micro, rows, width), F32),
            jax.ShapeDtypeStruct((micro, HQ // 2, rows, LANES), BF),
            jax.ShapeDtypeStruct((micro, ctx, rows, 2 * LANES), BF),
            jax.ShapeDtypeStruct((micro, HQ, rows), F32),
            jax.ShapeDtypeStruct((micro, HQ * HD, rows), BF),
        )

    @staticmethod
    def specs():
        vmem = pl.BlockSpec(memory_space=pltpu.VMEM)
        return [vmem, vmem, vmem, pl.BlockSpec(memory_space=pl.ANY), vmem, vmem]

    def tables(self):
        for m in range(self.micro):
            fill_tables(
                m, self.rows, self.c, self.freq, self.order, self.lens, self.cos_ref, self.sin_ref
            )

    def norms(self, gain_attn):
        for m in range(self.micro):
            stream = self.x[m].astype(F32)
            self.h1[m] = (stream * inverse_norm(stream) * gain_attn).astype(BF)

    def project(self, m, wq, bias_qkv):
        rows, width = self.rows, HQ * HD
        project = dot(self.h1[m], wq) + bias_qkv
        cosine = self.cos_ref[m * rows : (m + 1) * rows, :]
        sine = self.sin_ref[m * rows : (m + 1) * rows, :]
        keys = project[:, width : width + LANES]
        keys = keys * cosine + swap_halves(keys) * sine
        self.land[m, self.c, :, :LANES] = keys.astype(BF)
        self.land[m, self.c, :, LANES:] = project[:, width + LANES :].astype(BF)
        own = self.land.at[m, self.c]
        self.arrivals.append([self.links.put(own, own, other) for other in self.others])
        for p in range(HQ // 2):
            query = project[:, p * LANES : (p + 1) * LANES]
            query = query * cosine + swap_halves(query) * sine
            self.qs[m, p] = (query.astype(BF).astype(F32) * (1.0 / math.sqrt(HD))).astype(BF)

    def attend(self, m, tick):
        rows, ctx, group, pairs = self.rows, self.ctx, HQ // KVH, HQ // 2
        fill_bias(m, rows, self.c, self.order, self.lens, self.bias_ref)
        for at, source in zip(self.arrivals[m], self.back):
            self.links.arrive(at, self.land.at[m, source])
        copy = pltpu.make_async_copy(self.land.at[m], self.kv.at[m], self.out_sem.at[m])
        copy.start()
        self.out_copies.append(copy)
        both = self.land[m].reshape(ctx * rows, 2 * LANES).astype(F32)
        fill_heads(both[:, :LANES], self.kvar)
        fill_heads_turned(both[:, LANES:], self.vvar)

        def pair(p, carry):
            query = self.qs[m, p]
            mixed = jnp.zeros((LANES, rows), F32)
            for parity in range(2):
                head = 2 * p + parity
                g = head // group
                scores = dot_nt(self.kvar[g, parity], query) + self.bias_ref[...]
                top = jnp.max(scores, axis=0, keepdims=True)
                probs = jnp.exp(scores - top)
                total = jnp.sum(probs, axis=0, keepdims=True)
                mixed = mixed + dot(self.vvar[g, parity], probs.astype(BF)) / total
                self.lse[m, pl.ds(head, 1), :] = top + jnp.log(total)
            at = pl.multiple_of(p * LANES, LANES)
            self.obt[m, pl.ds(at, LANES), :] = mixed.astype(BF)
            self.ob[m, :, pl.ds(at, LANES)] = mixed.T.astype(BF)
            tick(p)
            return carry

        lax.fori_loop(0, pairs, pair, 0)

    def close(self, m, wo, gain_mlp):
        middle = self.x[m].astype(F32) + dot(self.ob[m], wo)
        self.x2[m] = middle
        self.h2[m] = (middle * inverse_norm(middle) * gain_mlp).astype(BF)

    def drain(self):
        self.links.drain()
        for copy in self.out_copies:
            copy.wait()


def forward_kernel(size, order, lens, x, wq, wo, bias_qkv, gain_attn, gain_mlp, freq, *rest):
    work = Forward(size, order, lens, x, freq, rest[:6], rest[6:])
    enter(work.others)
    work.tables()
    work.norms(gain_attn[...])
    for m in range(work.micro):
        work.project(m, wq[...], bias_qkv[...])
    for m in range(work.micro):
        work.attend(m, lambda p: None)
        work.close(m, wo[...], gain_mlp[...])
    work.drain()


def attention_forward(ctx, order, lens, x, wq, wo, bias_qkv, gain_attn, gain_mlp, freq):
    micro, rows, width = x.shape
    vmem = pl.BlockSpec(memory_space=pltpu.VMEM)
    smem = pl.BlockSpec(memory_space=pltpu.SMEM)
    return pl.pallas_call(
        functools.partial(forward_kernel, (micro, rows, ctx)),
        out_shape=Forward.shapes(micro, rows, ctx, width),
        in_specs=[smem, smem] + [vmem] * 7,
        out_specs=Forward.specs(),
        scratch_shapes=Forward.scratch(micro, rows, ctx, width),
        compiler_params=pltpu.CompilerParams(
            collective_id=1, has_side_effects=True, vmem_limit_bytes=VMEM_LIMIT
        ),
        name="attention_forward",
    )(order, lens, x, wq, wo, bias_qkv, gain_attn, gain_mlp, freq)


def front_kernel(
    size, order, lens, x, wq, wo, sm, wgu_raw, wd, gy, freq,
    h2, x2, qs, kv, lse, obt, wq_out, wo_out, gain_attn, gain_mlp, wgu_t, wd_t, gd_all,
    wq_all, wo_all, sm_all, pieces, bias_qkv, zeros, wgu_in, wd_in, gy_in, staged_sems,
    send, recv, ys, yr, zs, zr, here, *scratch
):
    n, micro, rows, ctx = size
    replicas = n // TP
    peers_n = replicas - 1
    high = wgu_raw.shape[0]
    staged = Staged([(wgu_raw, wgu_in), (wd, wd_in), (gy, gy_in)], staged_sems)
    units, width = wd.shape
    padded = wd_t.shape[1]
    proj = wq.shape[1]
    work = Forward((micro, rows, ctx), order, lens, x, freq, (h2, x2, qs, kv, lse, obt), scratch)
    f, c = lax.axis_index("fsdp"), lax.axis_index("ctx")
    t, r = f % TP, f // TP
    even = c % 2 == 0
    odd = c % 2 == 1
    sib, par, cross = (flip1(f), c), (flip2(f), c), (flip2(flip1(f)), c)
    t_sib, t_par, t_cross = flip1(t), flip2(t), flip2(flip1(t))
    twin = (f, flip1(c))
    peers = [((f + TP * j) % n, c) for j in range(1, replicas)]
    back = [(f - TP * j + n) % n for j in range(1, replicas)]
    rback = [(r - j + replicas) % replicas for j in range(1, replicas)]
    enter([sib, par, cross] + peers + work.others)
    links = Links(send, recv)
    local = []

    def keep(src, dst):
        copy = pltpu.make_async_copy(src, dst, here.at[len(local)])
        copy.start()
        local.append(copy)
        return copy

    class Spread:
        def __init__(self, own, every):
            self.every = every
            self.ys = [links.put(own, every.at[f], peer) for peer in peers]
            self.mine = own
            self.pending = [(links.put(own, every.at[f], sib), every.at[flip1(f)])]
            self.own = keep(own, every.at[f])
            self.later = []
            self.slots = [
                tuple(every.at[k] for k in (p, flip1(p), flip2(p), flip1(flip2(p)))) for p in back
            ]
            self.across = (every.at[flip2(f)], every.at[flip1(flip2(f))])

        def start_x(self):
            self.x = links.put(self.mine, self.every.at[f], par)

        def on_y(self):
            for at, (p, p_sib, p_par, p_cross) in zip(self.ys, self.slots):
                links.arrive(at, p)
                self.later.append((links.put(p, p, par), p_par, p_cross))
                self.pending.append((links.put(p, p, sib), p_sib))

        def on_x(self):
            p, p_cross = self.across
            links.arrive(self.x, p)
            self.pending.append((links.put(p, p, sib), p_cross))

        def on_late(self):
            for at, p, p_cross in self.later:
                links.arrive(at, p)
                self.pending.append((links.put(p, p, sib), p_cross))

        def done(self):
            for at, p in self.pending:
                links.arrive(at, p)
            self.own.wait()

    first = [Spread(wq, wq_all), Spread(sm, sm_all)]
    for one in first:
        one.start_x()
    second = Spread(wo, wo_all)
    pieces[...] = jnp.zeros_like(pieces)
    zeros[...] = jnp.zeros_like(zeros)
    staged.need(3)
    for k in range(TP):
        for q in range(2 * replicas):
            at = (q * TP + k) * units
            to = (q % replicas) * padded
            pieces[k, q // replicas, :, to : to + units] = wgu_in[:, at : at + units]
    gu_s = [links.put(pieces.at[t_sib, k], wgu_t.at[k, r, t], sib) for k in range(2)]
    half = units // 2
    last = wd_in.at[pl.ds(half, half)], wd_t.at[r, pl.ds(half, half)]
    head = wd_in.at[pl.ds(0, half)], wd_t.at[r, pl.ds(0, half)]

    def y_copy(at, j, src, dst):
        at = at * peers_n + j
        return pltpu.make_async_remote_copy(
            src_ref=src, dst_ref=dst, send_sem=ys.at[at], recv_sem=yr.at[at],
            device_id=peers[j], device_id_type=MESH,
        )

    def z_copy(at, j, src):
        at = at * peers_n + j
        return pltpu.make_async_remote_copy(
            src_ref=src, dst_ref=src, send_sem=zs.at[at], recv_sem=zr.at[at],
            device_id=twin, device_id_type=MESH,
        )

    def down_put(at, pair):
        for j in range(peers_n):
            y_copy(at, j, *pair).start()

    kinds = ((t, t_sib), (t_par, t_cross))

    def piece(parity, item, replica):
        return wgu_t.at[item % 2, replica, kinds[parity][item // 2]]

    def y_put(parity, item):
        for j in range(peers_n):
            mine = piece(parity, item, r)
            src = pieces.at[t, item] if (parity, item // 2) == (0, 0) else mine
            y_copy(item, j, src, mine).start()

    def z_put(parity, item):
        for j in range(peers_n):
            got = piece(parity, item, rback[j])
            y_copy(item, j, got, got).wait_recv()
            z_copy(item, j, got).start()

    @pl.when(even)
    def _():
        y_put(0, 0)
        y_put(0, 1)

    @pl.when(odd)
    def _():
        down_put(4, head)

    for q in range(replicas):
        keep(zeros, wd_t.at[q, pl.ds(units, padded - units)])
    keep(wd_in, wd_t.at[r, pl.ds(0, units)])
    for k in range(2):
        keep(pieces.at[t, k], wgu_t.at[k, r, t])
    keep(gy_in, gd_all.at[:, t])
    gd_s = links.put(gy_in, gd_all.at[:, t], sib)
    for one in first:
        one.on_y()
    gu_x = [links.put(pieces.at[t_par, k], wgu_t.at[k, r, t], par) for k in range(2)]
    gu_c = [links.put(pieces.at[t_cross, k], wgu_t.at[k, r, t], cross) for k in range(2)]
    second.start_x()
    work.tables()
    for one in first:
        one.on_x()
    for k in range(2):
        links.arrive(gu_s[k], wgu_t.at[k, r, t_sib])

    @pl.when(even)
    def _():
        y_put(0, 2)
        y_put(0, 3)
        down_put(4, head)
        down_put(5, last)

    for one in first:
        one.on_late()
    for one in first:
        one.done()
    keep(wq_all, wq_out)
    share = proj // n
    for k in range(n):
        small = sm_all[k].astype(F32)
        bias_qkv[:, k * share : k * share + min(share, LANES)] = small[0:1, : min(share, LANES)]
        if share > LANES:
            bias_qkv[:, k * share + LANES : (k + 1) * share] = small[1:2, : share - LANES]
        gain_attn[:, k * high : (k + 1) * high] = small[2:3, :high]
        gain_mlp[:, k * high : (k + 1) * high] = small[3:4, :high]
    work.norms(gain_attn[...])
    for m in range(micro):
        work.project(m, wq_all[...].reshape(width, proj), bias_qkv[...])
    second.on_y()
    gd_x = [links.put(gy_in.at[m], gd_all.at[m, t], par) for m in range(micro)]
    gd_par = [gd_all.at[m, t_par] for m in range(micro)]
    gd_c = []

    def x_piece(k):
        links.arrive(gu_x[k], wgu_t.at[k, r, t_par])
        pl.when(odd)(lambda: y_put(1, k))

    def c_piece(k):
        links.arrive(gu_c[k], wgu_t.at[k, r, t_cross])

        @pl.when(odd)
        def _():
            y_put(1, 2 + k)
            if k == 1:
                down_put(5, last)

    def on_gd():
        links.arrive(gd_x[0], gd_par[0])
        gd_c.append(links.put(gd_par[0], gd_par[0], sib))

    x_piece(0)
    x_piece(1)
    steps = {
        (0, 0): [lambda: pl.when(even)(lambda: z_put(0, 0))],
        (0, 1): [lambda: pl.when(even)(lambda: z_put(0, 1)), lambda: c_piece(0)],
        (0, 2): [lambda: pl.when(even)(lambda: z_put(0, 2))],
        (0, 3): [lambda: c_piece(1), lambda: pl.when(odd)(lambda: z_put(1, 0))],
        (0, 4): [lambda: pl.when(even)(lambda: z_put(0, 3))],
        (0, 6): [lambda: pl.when(odd)(lambda: z_put(1, 1))],
        (1, 1): [lambda: pl.when(odd)(lambda: z_put(1, 2)), second.on_x],
        (1, 3): [lambda: pl.when(odd)(lambda: z_put(1, 3)), second.on_late],
        (1, 6): [on_gd],
    }
    for m in range(micro):

        def tick(p, m=m):
            for (at_m, at_p), todo in steps.items():
                if at_m == m:

                    @pl.when(p == at_p)
                    def _(todo=todo):
                        for one in todo:
                            one()

        work.attend(m, tick)
    second.done()
    keep(wo_all, wo_out)
    for m in range(micro):
        work.close(m, wo_all[...].reshape(width, width), gain_mlp[...])
    for m in range(1, micro):
        links.arrive(gd_x[m], gd_par[m])
        gd_c.append(links.put(gd_par[m], gd_par[m], sib))
    links.arrive(gd_s, gd_all.at[:, t_sib])
    for m in range(micro):
        links.arrive(gd_c[m], gd_all.at[m, t_cross])
    for parity in range(2):

        @pl.when(even if parity == 0 else odd)
        def _(parity=parity):
            for j in range(peers_n):
                for item in range(4):
                    z_copy(item, j, piece(1 - parity, item, rback[j])).wait_recv()
                    mine = piece(parity, item, r)
                    z_copy(item, j, mine).wait_send()
                    y_copy(item, j, mine, mine).wait_send()

    for j in range(peers_n):
        for at, pair in ((4, head), (5, last)):
            y_copy(at, j, *pair).wait_send()
            first_row = 0 if at == 4 else half
            y_copy(at, j, pair[0], wd_t.at[rback[j], pl.ds(first_row, half)]).wait_recv()
    for copy in local:
        if copy is not second.own and all(copy is not one.own for one in first):
            copy.wait()
    work.drain()
    links.drain()


def gather_and_attend(n, ctx, order, lens, x, wq, wo, sm, wgu, wd, gy, freq, padded):
    micro, rows, width = x.shape
    replicas = n // TP
    peers = replicas - 1
    high, proj = wq.shape
    quarter = replicas * padded
    vmem = pl.BlockSpec(memory_space=pltpu.VMEM)
    smem = pl.BlockSpec(memory_space=pltpu.SMEM)
    anywhere = pl.BlockSpec(memory_space=pl.ANY)
    sems = pltpu.SemaphoreType.DMA
    copies = 3 * (4 * peers + 3) + 6 + 1 + 2 * micro
    gain = jax.ShapeDtypeStruct((1, width), F32)
    return pl.pallas_call(
        functools.partial(front_kernel, (n, micro, rows, ctx)),
        out_shape=Forward.shapes(micro, rows, ctx, width) + (
            jax.ShapeDtypeStruct((n, high, proj), BF),
            jax.ShapeDtypeStruct((n, high, width), BF),
            gain,
            gain,
            jax.ShapeDtypeStruct((2, replicas, TP, high, quarter), BF),
            jax.ShapeDtypeStruct((replicas, padded, width), BF),
            jax.ShapeDtypeStruct((micro, TP, rows, width), BF),
        ),
        in_specs=[smem, smem, vmem] + [anywhere] * 6 + [vmem],
        out_specs=Forward.specs() + [anywhere, anywhere, vmem, vmem] + [anywhere] * 3,
        scratch_shapes=[
            pltpu.VMEM((n, high, proj), BF),
            pltpu.VMEM((n, high, width), BF),
            pltpu.VMEM((n,) + sm.shape, BF),
            pltpu.VMEM((TP, 2, high, quarter), BF),
            pltpu.VMEM((1, proj), F32),
            pltpu.VMEM((padded - wd.shape[0], width), BF),
            pltpu.VMEM(wgu.shape, BF),
            pltpu.VMEM(wd.shape, BF),
            pltpu.VMEM(gy.shape, BF),
            sems((3,)),
            sems((copies,)), sems((copies,)),
            sems((6 * peers,)), sems((6 * peers,)), sems((4 * peers,)), sems((4 * peers,)),
            sems((9 + replicas,)),
        ] + Forward.scratch(micro, rows, ctx, width),
        compiler_params=pltpu.CompilerParams(
            collective_id=5, has_side_effects=True, vmem_limit_bytes=VMEM_LIMIT
        ),
        name="gather_and_attend",
    )(order, lens, x, wq, wo, sm, wgu, wd, gy, freq)


def mlp_kernel(
    size, h2, gd_hbm, wgu_hbm, wd_hbm,
    out, out_par, gh2, grads,
    gd, wgu, wd, hbuf, turned_h, turned_g, acc_out, acc_gh, dgate, dup, ddown,
    sib_out, sib_in, par_out, par_in, keep_sum, stage, send, recv, out_sem, staged_sems,
):
    micro, rows, width, replicas, padded = size
    quarter = replicas * padded
    both = 2 * rows
    f, c = lax.axis_index("fsdp"), lax.axis_index("ctx")
    t = f % TP
    core = t % 2
    mine, theirs = t - core, flip2(t) - core
    t_sib, t_par, t_cross = flip1(t), flip2(t), flip2(flip1(t))
    sib, par = (flip1(f), c), (flip2(f), c)
    staged = Staged(
        [(h2.at[m], hbuf.at[m, t]) for m in range(micro)]
        + [(gd_hbm.at[0], gd.at[0]), (wgu_hbm, wgu), (wd_hbm, wd)]
        + [(gd_hbm.at[m], gd.at[m]) for m in range(1, micro)],
        staged_sems,
    )
    enter([sib, par])
    links = Links(send, recv)
    from_sib, from_par, from_cross = [], [], [None] * micro
    for m in range(micro):
        from_par.append(links.put(h2.at[m], hbuf.at[m, t], par))
        from_sib.append(links.put(h2.at[m], hbuf.at[m, t], sib))

    def grad_of(m, side):
        return gd[m, pl.ds(side, 2)].reshape(both, width)

    def forward_on(m):
        buf = hbuf.at[m, t_par]
        links.arrive(from_par[m], buf)
        from_cross[m] = links.put(buf, buf, sib)

    def chunk(m, side, first, j):
        at = pl.multiple_of(j * CHUNK, CHUNK)
        hidden_in = hbuf[m, pl.ds(side, 2)].reshape(both, width)
        grad_in = grad_of(m, side)
        w_gate = wgu[0, :, pl.ds(at, CHUNK)]
        w_up = wgu[1, :, pl.ds(at, CHUNK)]
        w_down = wd[pl.ds(at, CHUNK), :]
        gate = dot(hidden_in, w_gate)
        up = dot(hidden_in, w_up)
        gm = dot_nt(grad_in, w_down)
        sg = 0.5 * jnp.tanh(0.5 * gate) + 0.5
        silu = gate * sg
        mb = (silu * up).astype(BF)
        ggate = (gm * up * (sg + silu * (1.0 - sg))).astype(BF)
        gup = (gm * silu).astype(BF)
        acc_out[...] += dot(mb, w_down)
        acc_gh[...] += dot_nt(ggate, w_gate) + dot_nt(gup, w_up)
        if first:
            dgate[:, pl.ds(at, CHUNK)] = dot(turned_h[...], ggate)
            dup[:, pl.ds(at, CHUNK)] = dot(turned_h[...], gup)
            ddown[:, pl.ds(at, CHUNK)] = dot(turned_g[...], mb)
        else:
            dgate[:, pl.ds(at, CHUNK)] += dot(turned_h[...], ggate)
            dup[:, pl.ds(at, CHUNK)] += dot(turned_h[...], gup)
            ddown[:, pl.ds(at, CHUNK)] += dot(turned_g[...], mb)

    def compute(m, side, first, middle, late):
        turned_h[...] = hbuf[m, pl.ds(side, 2)].reshape(both, width).T
        turned_g[...] = grad_of(m, side).T
        acc_out[...] = jnp.zeros_like(acc_out)
        acc_gh[...] = jnp.zeros_like(acc_gh)
        chunks = quarter // CHUNK

        def body(j, carry):
            chunk(m, side, first, j)
            return carry

        lax.fori_loop(0, 2, body, 0)
        middle()
        lax.fori_loop(2, chunks - 1, body, 0)
        late()
        lax.fori_loop(chunks - 1, chunks, body, 0)

    def share(step):
        here = pl.multiple_of(core * rows, rows)
        there = pl.multiple_of(rows - core * rows, rows)
        ats = []
        for k, acc in enumerate((acc_gh, acc_out)):
            sib_out[step, k] = acc[pl.ds(there, rows), :].astype(BF)
            ats.append(links.put(sib_out.at[step, k], sib_in.at[step, k], sib))
            keep_sum[k] = acc[pl.ds(here, rows), :]
        return ats

    def pass_on(step, m, ats):
        for k, (at, ref) in enumerate(zip(ats, (par_out, out_par))):
            links.arrive(at, sib_in.at[step, k])
            ref[m] = (keep_sum[k] + sib_in[step, k].astype(F32)).astype(BF)
        return links.put(par_out.at[m], par_in.at[m], par)

    def stay(step, m, ats):
        for k, (at, ref) in enumerate(zip(ats, (gh2, out))):
            links.arrive(at, sib_in.at[step, k])
            ref[m] = keep_sum[k] + sib_in[step, k].astype(F32)

    def finish(m, at):
        links.arrive(at, par_in.at[m])
        gh2[m] = gh2[m] + par_in[m].astype(F32)

    plan = [(0, True)] + [(m, False) for m in range(micro)] + [(m, True) for m in range(1, micro)]
    waiting = None
    sums = [None] * micro
    ready_own = [False] * micro
    for step, (m, own) in enumerate(plan):
        if own:
            links.arrive(from_sib[m], hbuf.at[m, t_sib])
        else:
            links.arrive(from_cross[m], hbuf.at[m, t_cross])
        staged.need((micro + 3) if m == 0 else len(staged.copies))

        def late(step=step):
            if step < micro:
                forward_on(step)

        def middle(step=step):
            if step > 0:
                last_m, last_own = plan[step - 1]
                if last_own:
                    stay(step - 1, last_m, waiting)
                else:
                    sums[last_m] = pass_on(step - 1, last_m, waiting)

        compute(m, mine if own else theirs, step == 0, middle, late)
        waiting = share(step)
    high = width // (replicas * TP)
    copies = []
    for replica in range(replicas):
        for k in range(PIECES):
            slot = len(copies) % SLOTS
            if len(copies) >= SLOTS:
                copies[-SLOTS].wait()
            if k < 4 * TP:
                at = (replica * TP + k // 4) * high
                lane = (k % 2) * (quarter // 2)
                stage[slot] = (dgate, dup)[(k // 2) % 2][
                    at : at + high, lane : lane + quarter // 2
                ].astype(BF)
            else:
                for q in range(replicas // 2):
                    at = (k - 4 * TP) * (replicas // 2) + q
                    stage[slot, :, q * padded : (q + 1) * padded] = ddown[
                        at * high : (at + 1) * high, replica * padded : (replica + 1) * padded
                    ].astype(BF)
            copy = pltpu.make_async_copy(stage.at[slot], grads.at[replica, k], out_sem.at[slot])
            copy.start()
            copies.append(copy)
    last_m, last_own = plan[-1]
    if last_own:
        stay(len(plan) - 1, last_m, waiting)
    else:
        sums[last_m] = pass_on(len(plan) - 1, last_m, waiting)
    for m in range(micro):
        finish(m, sums[m])
    for copy in copies[-SLOTS:]:
        copy.wait()
    links.drain()


def mlp(n, h2, gd, wgu, wd):
    micro, rows, width = h2.shape
    replicas = n // TP
    padded = wd.shape[0] // replicas
    quarter = replicas * padded
    vmem = pl.BlockSpec(memory_space=pltpu.VMEM)
    steps = 2 * micro
    copies = micro * 3 + steps * 2 + micro
    whole = jax.ShapeDtypeStruct((micro, rows, width), F32)
    return pl.pallas_call(
        functools.partial(mlp_kernel, (micro, rows, width, replicas, padded)),
        out_shape=(
            whole,
            jax.ShapeDtypeStruct((micro, rows, width), BF),
            whole,
            jax.ShapeDtypeStruct((replicas, PIECES, width // n, quarter // 2), BF),
        ),
        in_specs=[pl.BlockSpec(memory_space=pl.ANY)] * 4,
        out_specs=[vmem, vmem, vmem, pl.BlockSpec(memory_space=pl.ANY)],
        scratch_shapes=[
            pltpu.VMEM(gd.shape, BF),
            pltpu.VMEM(wgu.shape, BF),
            pltpu.VMEM(wd.shape, BF),
            pltpu.VMEM((micro, TP, rows, width), BF),
            pltpu.VMEM((width, 2 * rows), BF),
            pltpu.VMEM((width, 2 * rows), BF),
            pltpu.VMEM((2 * rows, width), F32),
            pltpu.VMEM((2 * rows, width), F32),
            pltpu.VMEM((width, quarter), F32),
            pltpu.VMEM((width, quarter), F32),
            pltpu.VMEM((width, quarter), F32),
            pltpu.VMEM((steps, 2, rows, width), BF),
            pltpu.VMEM((steps, 2, rows, width), BF),
            pltpu.VMEM((micro, rows, width), BF),
            pltpu.VMEM((micro, rows, width), BF),
            pltpu.VMEM((2, rows, width), F32),
            pltpu.VMEM((SLOTS, width // n, quarter // 2), BF),
            pltpu.SemaphoreType.DMA((copies,)),
            pltpu.SemaphoreType.DMA((copies,)),
            pltpu.SemaphoreType.DMA((SLOTS,)),
            pltpu.SemaphoreType.DMA((2 * micro + 2,)),
        ],
        compiler_params=pltpu.CompilerParams(
            collective_id=2, has_side_effects=True, vmem_limit_bytes=VMEM_LIMIT
        ),
        name="mlp",
    )(h2, gd, wgu, wd)


def add_into(dst, a, b):
    dst[...] = (a[...].astype(F32) + b[...].astype(F32)).astype(BF)


class Sums:
    def __init__(self, n, ctx, grads, fin, scratch):
        self.n, self.ctx, self.grads, self.fin = n, ctx, grads, fin
        (
            self.total, self.peer_in, self.pre, self.suf, self.suf_out, self.land,
            self.core_o, self.par_o, self.ring_o, self.core_q, self.par_q, self.ring_q,
            self.vec, self.vec_in,
            self.ys, self.yr, self.ps, self.pr, self.ss, self.sr, self.fs, self.fr,
            self.asend, self.arecv, self.own_sem, self.out_sem,
        ) = scratch
        self.replicas = n // TP
        self.f, self.c = lax.axis_index("fsdp"), lax.axis_index("ctx")
        f, c = self.f, self.c
        self.t, self.r = f % TP, f // TP
        self.core, self.side = self.t % 2, self.t // 2
        self.sib, self.par, self.cross = (flip1(f), c), (flip2(f), c), (flip2(flip1(f)), c)
        self.peers = [((f + TP * j) % n, c) for j in range(1, self.replicas)]
        self.left, self.right = (f, (c + ctx - 1) % ctx), (f, (c + 1) % ctx)
        self.links = Links(self.asend, self.arecv)

    @staticmethod
    def scratch(n, high, wide, width, proj):
        replicas = n // TP
        sems = pltpu.SemaphoreType.DMA
        peers = replicas - 1
        return [
            pltpu.VMEM((ALL_PIECES, high, wide), BF),
            pltpu.VMEM((peers, PIECES, high, wide), BF),
            pltpu.VMEM((ALL_PIECES, high, wide), BF),
            pltpu.VMEM((ALL_PIECES, high, wide), BF),
            pltpu.VMEM((RING, high, wide), BF),
            pltpu.VMEM((4 * TP, high, wide), BF),
            pltpu.VMEM((replicas, 2, high, width), BF),
            pltpu.VMEM((replicas, high, width), BF),
            pltpu.VMEM((peers, high, width), BF),
            pltpu.VMEM((replicas, 2, high, proj), BF),
            pltpu.VMEM((replicas, high, proj), BF),
            pltpu.VMEM((peers, high, proj), BF),
            pltpu.VMEM((3, VEC, LANES), F32),
            pltpu.VMEM((2 + peers, VEC, LANES), F32),
            sems((peers * PIECES,)), sems((peers * PIECES,)),
            sems((ALL_PIECES,)), sems((ALL_PIECES,)), sems((ALL_PIECES,)), sems((ALL_PIECES,)),
            sems((4 * TP,)), sems((4 * TP,)),
            sems((6 + 3 * peers,)), sems((6 + 3 * peers,)), sems((1,)), sems((ALL_PIECES,)),
        ]

    def around(self):
        return [self.sib, self.par, self.cross] + self.peers + [self.left, self.right]

    def peer_copy(self, j, k):
        at = j * PIECES + k
        return pltpu.make_async_remote_copy(
            src_ref=self.grads.at[(self.r + j + 1) % self.replicas, k],
            dst_ref=self.peer_in.at[j, k],
            send_sem=self.ys.at[at],
            recv_sem=self.yr.at[at],
            device_id=self.peers[j],
            device_id_type=MESH,
        )

    def own_copy(self):
        return pltpu.make_async_copy(
            self.grads.at[self.r], self.total.at[pl.ds(0, PIECES)], self.own_sem.at[0]
        )

    def start(self):
        self.own_copy().start()

        def body(k, carry):
            for j in range(self.replicas - 1):
                self.peer_copy(j, k).start()
            return carry

        lax.fori_loop(0, PIECES, body, 0)

    def pre_copy(self, k, src):
        return pltpu.make_async_remote_copy(
            src_ref=src.at[k], dst_ref=self.pre.at[k], send_sem=self.ps.at[k],
            recv_sem=self.pr.at[k], device_id=self.right, device_id_type=MESH,
        )

    def suf_copy(self, k, src):
        return pltpu.make_async_remote_copy(
            src_ref=src, dst_ref=self.suf.at[k], send_sem=self.ss.at[k],
            recv_sem=self.sr.at[k], device_id=self.left, device_id_type=MESH,
        )

    def out_copy(self, k, src):
        return pltpu.make_async_copy(src.at[k], self.fin.at[k], self.out_sem.at[k])

    def step(self, time, carry):
        self.tick(time)
        return carry

    def tick(self, time):
        c, ctx, total = self.c, self.ctx, self.total

        @pl.when(time < PIECES)
        def _():
            for j in range(self.replicas - 1):
                self.peer_copy(j, time).wait_recv()
                add_into(total.at[time], total.at[time], self.peer_in.at[j, time])

        k = time - HOP * c

        @pl.when((k >= 0) & (k < ALL_PIECES))
        def _():
            @pl.when(c > 0)
            def _():
                self.pre_copy(k, total).wait_recv()
                add_into(self.pre.at[k], self.pre.at[k], total.at[k])

                @pl.when(c < ctx - 1)
                def _():
                    self.pre_copy(k, self.pre).start()

            @pl.when(c == 0)
            def _():
                self.pre_copy(k, total).start()

        k2 = time - HOP * (ctx - 1 - c)

        @pl.when((k2 >= 0) & (k2 < ALL_PIECES))
        def _():
            @pl.when(c < ctx - 1)
            def _():
                self.suf_copy(k2, total.at[k2]).wait_recv()

            @pl.when((c > 0) & (c < ctx - 1))
            def _():
                @pl.when(k2 >= RING)
                def _():
                    self.suf_copy(k2 - RING, self.suf_out.at[(k2 - RING) % RING]).wait_send()

                add_into(self.suf_out.at[k2 % RING], self.suf.at[k2], total.at[k2])
                self.suf_copy(k2, self.suf_out.at[k2 % RING]).start()

            @pl.when(c == ctx - 1)
            def _():
                self.suf_copy(k2, total.at[k2]).start()

        k3 = time - HOP * jnp.maximum(c, ctx - 1 - c)

        @pl.when((k3 >= 0) & (k3 < ALL_PIECES))
        def _():
            @pl.when(c == 0)
            def _():
                add_into(self.suf.at[k3], self.suf.at[k3], total.at[k3])

            @pl.when((c > 0) & (c < ctx - 1))
            def _():
                add_into(self.suf.at[k3], self.suf.at[k3], self.pre.at[k3])

            @pl.when((k3 < 4 * TP) & (k3 // 4 != self.t))
            def _():
                @pl.when(c == ctx - 1)
                def _():
                    self.fin_copy_from(k3, self.pre).start()

                @pl.when(c < ctx - 1)
                def _():
                    self.fin_copy_from(k3, self.suf).start()

            @pl.when((k3 >= 4 * TP) | (k3 // 4 == self.t))
            def _():
                @pl.when(c == ctx - 1)
                def _():
                    self.out_copy(k3, self.pre).start()

                @pl.when(c < ctx - 1)
                def _():
                    self.out_copy(k3, self.suf).start()

    def fin_copy_from(self, k, src):
        return pltpu.make_async_remote_copy(
            src_ref=src.at[k], dst_ref=self.land.at[4 * self.t + k % 4], send_sem=self.fs.at[k],
            recv_sem=self.fr.at[4 * self.t + k % 4],
            device_id=(self.f - self.t + k // 4, self.c), device_id_type=MESH,
        )

    @property
    def ticks(self):
        return ALL_PIECES + HOP * (self.ctx - 1)

    def close(self):
        c, ctx = self.c, self.ctx

        def arrive(k, carry):
            @pl.when(k // 4 != self.t)
            def _():
                pltpu.make_async_remote_copy(
                    src_ref=self.land.at[k], dst_ref=self.land.at[k], send_sem=self.fs.at[k],
                    recv_sem=self.fr.at[k], device_id=(self.f - self.t + k // 4, c),
                    device_id_type=MESH,
                ).wait_recv()
                self.out_copy(k, self.land).start()
                self.fin_copy_from(k, self.suf).wait_send()

            return carry

        lax.fori_loop(0, 4 * TP, arrive, 0)

        def settle(k, carry):
            @pl.when(c < ctx - 1)
            def _():
                self.pre_copy(k, self.total).wait_send()

            @pl.when((c == ctx - 1) | ((c > 0) & (k >= ALL_PIECES - RING)))
            def _():
                self.suf_copy(k, self.total.at[k]).wait_send()

            self.out_copy(k, self.suf).wait()
            return carry

        lax.fori_loop(0, ALL_PIECES, settle, 0)

        def peers(k, carry):
            for j in range(self.replicas - 1):
                self.peer_copy(j, k).wait_send()
            return carry

        lax.fori_loop(0, PIECES, peers, 0)
        self.links.drain()


    def fold(self, own, got_core, got_par, got_ring, first, extra=False):
        replicas = self.replicas
        at = self.links.put(own.at[:, :, 1 - self.core], got_core, self.sib)
        at_vec = None
        if extra:
            at_vec = self.links.put(self.vec.at[0], self.vec_in.at[0], self.sib)
        yield
        self.links.arrive(at, got_core)
        for replica in range(replicas):
            for s in range(2):
                add_into(
                    got_core.at[replica, s], got_core.at[replica, s],
                    own.at[replica, s, self.core],
                )
        at = self.links.put(got_core.at[:, 1 - self.side], got_par, self.par)
        if extra:
            self.links.arrive(at_vec, self.vec_in.at[0])
            self.vec[1] = self.vec[0] + self.vec_in[0]
            at_vec = self.links.put(self.vec.at[1], self.vec_in.at[1], self.par)
        yield
        self.links.arrive(at, got_par)
        for replica in range(replicas):
            add_into(got_par.at[replica], got_par.at[replica], got_core.at[replica, self.side])
        ats, vec_ats = [], []
        if extra:
            self.links.arrive(at_vec, self.vec_in.at[1])
            self.vec[2] = self.vec[1] + self.vec_in[1]
        for j, peer in enumerate(self.peers):
            ats.append(
                self.links.put(got_par.at[(self.r + j + 1) % replicas], got_ring.at[j], peer)
            )
            if extra:
                vec_ats.append(self.links.put(self.vec.at[2], self.vec_in.at[2 + j], peer))
        yield
        width, wide = got_ring.shape[-1], self.total.shape[-1]
        mine = got_par.at[self.r]
        for j, at in enumerate(ats):
            self.links.arrive(at, got_ring.at[j])
            add_into(mine, mine, got_ring.at[j])
        self.total[first] = mine[:, :wide]
        self.total[first + 1, :, : width - wide] = mine[:, wide:]
        if extra:
            vec = self.vec[2]
            for j, at in enumerate(vec_ats):
                self.links.arrive(at, self.vec_in.at[2 + j])
                vec = vec + self.vec_in[2 + j]
            self.total[first + 1, :VEC, width - wide : width - wide + LANES] = vec.astype(BF)
        yield


def backward_kernel(
    size, merged, order, lens, gain_attn, gain_mlp, freq, *rest
):
    n, micro, rows, ctx = size
    hbm, rest = rest[:11], rest[11:]
    out_par, grads, dx, outputs = rest[:4]
    rest = rest[4:]
    outs = 1 if merged else 3
    fin, rest = rest[:outs], rest[outs:]
    (
        x2, gh2, gy, wo, obt, kv, qs, lse, x, wq, out, staged_sems,
        out_in, out_send, out_recv, cos_ref, sin_ref, bias_ref, kvar, kvar_turned, vvar, go_ref, gp, h1t, gk, gv, part, land,
        att_o, att_q, vec_wide, send, recv,
    ), rest = rest[:33], rest[33:]
    staged = Staged(
        list(zip(hbm, (x2, gh2, gy, wo, obt, kv, qs, lse, x, wq, out))), staged_sems
    )
    group = HQ // KVH
    pairs = HQ // 2
    width = HQ * HD
    replicas = n // TP
    high = width // n
    proj = wq.shape[1]
    scale = 1.0 / math.sqrt(HD)
    f, c = lax.axis_index("fsdp"), lax.axis_index("ctx")
    others = [(f, (c + j) % ctx) for j in range(1, ctx)]
    back = [(c - j + ctx) % ctx for j in range(1, ctx)]
    if merged:
        sums = Sums(n, ctx, grads, fin[0], rest)
        enter(others + sums.around())
        sums.start()
    else:
        enter(others + [(flip2(f), c)])
    out_links = Links(out_send, out_recv)
    out_at = out_links.put(out_par, out_in, (flip2(f), c))
    links = Links(send, recv)
    arrivals = []
    if merged:
        for k in range(PIECES, ALL_PIECES):
            sums.total[k] = jnp.zeros(sums.total.shape[1:], BF)
        sums.own_copy().wait()
    for m in range(micro):
        fill_tables(m, rows, c, freq, order, lens, cos_ref, sin_ref)
        if merged:
            lax.fori_loop(EARLY * m // micro, EARLY * (m + 1) // micro, sums.step, 0)
        staged.need(4)
        stream = x2[m]
        inverse = inverse_norm(stream)
        normed = stream * inverse
        grad = gh2[m]
        term = jnp.sum(grad * normed, axis=0, keepdims=True)
        at = proj + width
        vec_wide[:, at : at + width] = term if m == 0 else vec_wide[:, at : at + width] + term
        grad = grad * gain_mlp[...]
        grad = gy[m].astype(F32) + inverse * (
            grad - normed * jnp.mean(grad * normed, axis=1, keepdims=True)
        )
        dx[m] = grad
        spread = dot_nt(grad.astype(BF), wo[...]).astype(BF)
        for p in range(pairs):
            go_ref[m, p] = spread[:, p * LANES : (p + 1) * LANES]
    staged.need(len(staged.copies))
    for k in range(n):
        term = dot(obt[0, k * high : (k + 1) * high, :], dx[0].astype(BF))
        for m in range(1, micro):
            term = term + dot(obt[m, k * high : (k + 1) * high, :], dx[m].astype(BF))
        att_o[k // TP, (k // 2) % 2, k % 2] = term.astype(BF)
    if merged:
        fold_o = sums.fold(att_o, sums.core_o, sums.par_o, sums.ring_o, PIECES)
        next(fold_o)
    for m in range(micro):
        if merged and m > 0:
            next(fold_o)
        fill_bias(m, rows, c, order, lens, bias_ref)
        both = kv[m].reshape(ctx * rows, 2 * LANES).astype(F32)
        fill_heads(both[:, :LANES], kvar)
        fill_heads_turned(both[:, :LANES], kvar_turned)
        fill_heads(both[:, LANES:], vvar)
        gk[...] = jnp.zeros_like(gk)
        gv[...] = jnp.zeros_like(gv)
        cosine = cos_ref[m * rows : (m + 1) * rows, :]
        sine = sin_ref[m * rows : (m + 1) * rows, :]

        def pair(p, carry):
            query = qs[m, p]
            go = go_ref[m, p]
            grad_query = jnp.zeros((LANES, rows), F32)
            for parity in range(2):
                head = 2 * p + parity
                g = head // group
                scores = dot_nt(kvar[g, parity], query) + bias_ref[...]
                probs = jnp.exp(scores - lse[m, pl.ds(head, 1), :])
                grad_probs = dot_nt(vvar[g, parity], go)
                delta = jnp.sum(probs * grad_probs, axis=0, keepdims=True)
                grad_scores = (probs * (grad_probs - delta)).astype(BF)
                grad_query = grad_query + dot(kvar_turned[g, parity], grad_scores)
                gk[g, parity] += dot(grad_scores, query)
                gv[g, parity] += dot(probs.astype(BF), go)
            turned = grad_query.T * scale
            turned = turned * cosine - swap_halves(turned) * sine
            at = pl.multiple_of(p * LANES, LANES)
            gp[m * rows : (m + 1) * rows, pl.ds(at, LANES)] = turned.astype(BF)
            if merged:
                step = m * pairs + p
                lax.fori_loop(
                    EARLY + RATE * step // 2, EARLY + RATE * (step + 1) // 2, sums.step, 0
                )

            return carry

        lax.fori_loop(0, pairs, pair, 0)
        low = lax.broadcasted_iota(jnp.int32, (ctx * rows, LANES), 1) < HD
        for k, acc in enumerate((gk, gv)):
            first = acc[0, 0] + pltpu.roll(acc[0, 1], HD, 1)
            second = pltpu.roll(acc[1, 0], HD, 1) + acc[1, 1]
            whole = jnp.where(low, first, second).astype(BF)
            part[m, :, :, k * LANES : (k + 1) * LANES] = whole.reshape(ctx, rows, LANES)
        arrivals.append(
            [links.put(part.at[m, other[1]], land.at[m, c], other) for other in others]
        )
    if merged:
        next(fold_o)
    for m in range(micro):
        stream = x[m].astype(F32)
        h1t[:, m * rows : (m + 1) * rows] = (
            (stream * inverse_norm(stream) * gain_attn[...]).T.astype(BF)
        )
    for m in range(micro):
        total = part[m, c].astype(F32)
        for at, source in zip(arrivals[m], back):
            links.arrive(at, land.at[m, source])
            total = total + land[m, source].astype(F32)
        cosine = cos_ref[m * rows : (m + 1) * rows, :]
        sine = sin_ref[m * rows : (m + 1) * rows, :]
        grad_keys = total[:, :LANES]
        grad_keys = grad_keys * cosine - swap_halves(grad_keys) * sine
        gp[m * rows : (m + 1) * rows, width : width + LANES] = grad_keys.astype(BF)
        gp[m * rows : (m + 1) * rows, width + LANES :] = total[:, LANES:].astype(BF)
    for k in range(n):
        term = dot(h1t[k * high : (k + 1) * high, :], gp[...])
        att_q[k // TP, (k // 2) % 2, k % 2] = term.astype(BF)
    for m in range(micro):
        grad_project = gp[m * rows : (m + 1) * rows, :]
        stream = x[m].astype(F32)
        inverse = inverse_norm(stream)
        normed = stream * inverse
        term = jnp.sum(grad_project.astype(F32), axis=0, keepdims=True)
        vec_wide[:, :proj] = term if m == 0 else vec_wide[:, :proj] + term
        grad = dot_nt(grad_project, wq[...])
        term = jnp.sum(grad * normed, axis=0, keepdims=True)
        at = slice(proj, proj + width)
        vec_wide[:, at] = term if m == 0 else vec_wide[:, at] + term
        grad = grad * gain_attn[...]
        dx[m] = dx[m] + inverse * (
            grad - normed * jnp.mean(grad * normed, axis=1, keepdims=True)
        )
    out_links.arrive(out_at, out_in)
    for m in range(micro):
        outputs[m] = (x2[m] + out[m] + out_in[m].astype(F32)).astype(BF)
    out_links.drain()
    vec = sums.vec.at[0] if merged else fin[2]
    vec[...] = jnp.zeros((VEC, LANES), F32)
    for k in range(vec_wide.shape[1] // LANES):
        vec[k : k + 1, :] = vec_wide[:, k * LANES : (k + 1) * LANES]
    if merged:
        next(fold_o)
        fold_sums(sums, att_q, EARLY + RATE * micro * pairs // 2)
    else:
        fin[0][...] = att_o[...]
        fin[1][...] = att_q[...]
    links.drain()


def fold_sums(sums, att_q, done):
    fold_q = sums.fold(att_q, sums.core_q, sums.par_q, sums.ring_q, PIECES + 2, True)
    ready = max(0, PIECES + 2 - done)
    next(fold_q)
    for k in range(3):
        upto = done + ready * (k + 1) // 3
        lax.fori_loop(done + ready * k // 3, upto, sums.step, 0)
        next(fold_q)
    lax.fori_loop(done + ready, sums.ticks, sums.step, 0)
    sums.close()


def attention_backward(
    n, ctx, order, lens, gh2, x2, gy, x, wq, wo, gain_attn, gain_mlp, freq, qs, kv, lse, obt,
    out, out_par, grads,
):
    micro, rows, width = x.shape
    keys = rows * ctx
    proj = wq.shape[1]
    replicas = n // TP
    high, wide = grads.shape[2:]
    merged = ctx <= 4
    vmem = pl.BlockSpec(memory_space=pltpu.VMEM)
    smem = pl.BlockSpec(memory_space=pltpu.SMEM)
    anywhere = pl.BlockSpec(memory_space=pl.ANY)
    copies = micro * (ctx - 1)
    out_shape = [
        jax.ShapeDtypeStruct((micro, rows, width), F32),
        jax.ShapeDtypeStruct((micro, rows, width), BF),
    ]
    shape_o = (replicas, 2, 2, high, width)
    shape_q = (replicas, 2, 2, high, proj)
    if merged:
        out_shape += [jax.ShapeDtypeStruct((ALL_PIECES, high, wide), BF)]
    else:
        out_shape += [
            jax.ShapeDtypeStruct(shape_o, BF),
            jax.ShapeDtypeStruct(shape_q, BF),
            jax.ShapeDtypeStruct((VEC, LANES), F32),
        ]
    operands = (x2, gh2, gy, wo, obt, kv, qs, lse, x, wq, out)
    result = pl.pallas_call(
        functools.partial(backward_kernel, (n, micro, rows, ctx), merged),
        out_shape=out_shape,
        in_specs=[smem, smem] + [vmem] * 3 + [anywhere] * 13,
        out_specs=[vmem] * 2 + ([anywhere] if merged else [vmem] * 3),
        scratch_shapes=[pltpu.VMEM(one.shape, one.dtype) for one in operands]
        + [
            pltpu.SemaphoreType.DMA((len(operands),)),
            pltpu.VMEM((micro, rows, width), BF),
            pltpu.SemaphoreType.DMA((1,)),
            pltpu.SemaphoreType.DMA((1,)),
            pltpu.VMEM((micro * rows, LANES), F32),
            pltpu.VMEM((micro * rows, LANES), F32),
            pltpu.VMEM((keys, rows), F32),
            pltpu.VMEM((KVH, 2, keys, LANES), BF),
            pltpu.VMEM((KVH, 2, LANES, keys), BF),
            pltpu.VMEM((KVH, 2, keys, LANES), BF),
            pltpu.VMEM((micro, HQ // 2, rows, LANES), BF),
            pltpu.VMEM((micro * rows, proj), BF),
            pltpu.VMEM((width, micro * rows), BF),
            pltpu.VMEM((KVH, 2, keys, LANES), F32),
            pltpu.VMEM((KVH, 2, keys, LANES), F32),
            pltpu.VMEM((micro, ctx, rows, 2 * LANES), BF),
            pltpu.VMEM((micro, ctx, rows, 2 * LANES), BF),
            pltpu.VMEM(shape_o, BF),
            pltpu.VMEM(shape_q, BF),
            pltpu.VMEM((1, proj + 2 * width), F32),
            pltpu.SemaphoreType.DMA((copies,)),
            pltpu.SemaphoreType.DMA((copies,)),
        ]
        + (Sums.scratch(n, high, wide, width, proj) if merged else []),
        compiler_params=pltpu.CompilerParams(
            collective_id=3, has_side_effects=True, vmem_limit_bytes=VMEM_LIMIT
        ),
        name="attention_backward",
    )(order, lens, gain_attn, gain_mlp, freq, *operands, out_par, grads)
    if merged:
        return result
    dx, outputs, att_o, att_q, vec = result
    return dx, outputs, reduce_grads(n, ctx, grads, att_o, att_q, vec)


def reduce_kernel(n, ctx, grads, att_o, att_q, vec, fin, *scratch):
    sums = Sums(n, ctx, grads, fin, scratch)
    enter(sums.around())
    sums.start()
    sums.vec[0] = vec[...]
    for k in range(PIECES, ALL_PIECES):
        sums.total[k] = jnp.zeros(sums.total.shape[1:], BF)
    sums.own_copy().wait()
    for _ in sums.fold(att_o, sums.core_o, sums.par_o, sums.ring_o, PIECES):
        pass
    fold_sums(sums, att_q, 0)


def reduce_grads(n, ctx, grads, att_o, att_q, vec):
    high, wide = grads.shape[2:]
    vmem = pl.BlockSpec(memory_space=pltpu.VMEM)
    anywhere = pl.BlockSpec(memory_space=pl.ANY)
    return pl.pallas_call(
        functools.partial(reduce_kernel, n, ctx),
        out_shape=jax.ShapeDtypeStruct((ALL_PIECES, high, wide), BF),
        in_specs=[anywhere, vmem, vmem, vmem],
        out_specs=anywhere,
        scratch_shapes=Sums.scratch(n, high, wide, att_o.shape[-1], att_q.shape[-1]),
        compiler_params=pltpu.CompilerParams(
            collective_id=4, has_side_effects=True, vmem_limit_bytes=VMEM_LIMIT
        ),
        name="reduce_grads",
    )(grads, att_o, att_q, vec)


def finish_kernel(size, fin, g_gu, g_down, g_qkv, g_out, vec, turn):
    n, units, padded, proj, width = size
    replicas = n // TP
    high = width // n
    wide = fin.shape[-1]
    for half in range(2):
        for k in range(TP):
            whole = jnp.concatenate(
                [fin[4 * k + 2 * half + q].astype(F32) for q in range(2)], axis=1
            )
            for q in range(replicas):
                at = ((half * replicas + q) * TP + k) * units
                g_gu[:, at : at + units] = whole[:, q * padded : q * padded + units]
    each = wide // padded
    for k in range(n):
        at = (k % each) * padded
        turn[k * high : (k + 1) * high, :] = fin[4 * TP + k // each, :, at : at + padded].astype(F32)
    g_down[...] = turn[...].T[:units, :]
    g_out[:, :wide] = fin[PIECES].astype(F32)
    g_out[:, wide:] = fin[PIECES + 1, :, : width - wide].astype(F32)
    g_qkv[:, :wide] = fin[PIECES + 2].astype(F32)
    g_qkv[:, wide:] = fin[PIECES + 3, :, : proj - wide].astype(F32)
    vec[...] = fin[PIECES + 3, :VEC, proj - wide : proj - wide + LANES].astype(F32)


def finish_grads(n, fin, units, padded, proj, width):
    high = width // n
    vmem = pl.BlockSpec(memory_space=pltpu.VMEM)
    return pl.pallas_call(
        functools.partial(finish_kernel, (n, units, padded, proj, width)),
        out_shape=(
            jax.ShapeDtypeStruct((high, 2 * n * units), F32),
            jax.ShapeDtypeStruct((units, width), F32),
            jax.ShapeDtypeStruct((high, proj), F32),
            jax.ShapeDtypeStruct((high, width), F32),
            jax.ShapeDtypeStruct((VEC, LANES), F32),
        ),
        in_specs=[vmem],
        out_specs=[vmem] * 5,
        scratch_shapes=[pltpu.VMEM((width, padded), F32)],
        compiler_params=pltpu.CompilerParams(vmem_limit_bytes=VMEM_LIMIT),
        name="finish_grads",
    )(fin)


def pad_to(v, axis, size):
    pads = [(0, 0)] * v.ndim
    pads[axis] = (0, size - v.shape[axis])
    return jnp.pad(v, pads)


def local(
    inputs, cotangent, lengths, order, w_qkv, b_qkv, w_out, norm_attn, norm_mlp, w_gate_up, w_down
):
    n = lax.axis_size("fsdp")
    ctx = lax.axis_size("ctx")
    replicas = n // TP
    x, gy = inputs[0], cotangent[0]
    micro, rows, width = x.shape
    high = w_gate_up.shape[0]
    units = w_down.shape[0]
    padded = -(-units // LANES) * LANES
    quarter = replicas * padded
    proj = w_qkv.shape[1]
    qk = (HQ + KVH) * HD
    vw = KVH * HD

    small = jnp.concatenate(
        [
            pad_to(b_qkv, 0, 2 * LANES).reshape(2, LANES),
            pad_to(norm_attn, 0, LANES)[None],
            pad_to(norm_mlp, 0, LANES)[None],
            jnp.zeros((12, LANES), BF),
        ]
    )
    half = HD // 2
    freqs = np.power(np.float32(ROPE_BASE), -(np.arange(half, dtype=np.float32) * (2.0 / HD)))
    freq = jnp.asarray(np.tile(freqs.astype(np.float32), (8, LANES // half)))
    if ctx <= 4 and high % 16 == 0 and units % 32 == 0:
        (
            h2, x2, qs, kv, lse, obt, wq_all, wo_all, gain_attn, gain_mlp, wgu_t, wd_t, gd_all,
        ) = gather_and_attend(
            n, ctx, order[0], lengths[0], x, w_qkv, w_out, small, w_gate_up, w_down, gy, freq,
            padded,
        )
        wq_all = wq_all.reshape(width, proj)
        wo_all = wo_all.reshape(width, width)
    else:
        wgu = w_gate_up.reshape(high, 2, replicas, TP, units)
        wgu = pad_to(wgu.transpose(3, 1, 0, 2, 4), 4, padded).reshape(TP, 2, high, quarter)
        wq_all, wo_all, sm_all, wgu_t, wd_t, gd_all = gather_weights(
            n, w_qkv, w_out, small, wgu, pad_to(w_down, 0, padded), gy
        )
        wq_all = wq_all.reshape(width, proj)
        wo_all = wo_all.reshape(width, width)
        bias = sm_all[:, :2].reshape(n, 2 * LANES)[:, : b_qkv.shape[0]].reshape(1, proj)
        gain_attn = sm_all[:, 2, :high].reshape(1, width).astype(F32)
        gain_mlp = sm_all[:, 3, :high].reshape(1, width).astype(F32)
        h2, x2, qs, kv, lse, obt = attention_forward(
            ctx, order[0], lengths[0], x, wq_all, wo_all, bias.astype(F32), gain_attn, gain_mlp,
            freq,
        )
    wgu_t = wgu_t.reshape(2, width, quarter)
    wd_t = wd_t.reshape(quarter, width)
    out, out_par, gh2, grads = mlp(n, h2, gd_all, wgu_t, wd_t)
    dx, outputs, fin = attention_backward(
        n, ctx, order[0], lengths[0], gh2, x2, gy, x, wq_all, wo_all, gain_attn, gain_mlp, freq,
        qs, kv, lse, obt, out, out_par, grads,
    )
    g_gu, g_down, g_qkv, g_out, vec = finish_grads(n, fin, units, padded, proj, width)
    vec = vec.reshape(VEC * LANES)
    f = lax.axis_index("fsdp")

    def own(first, size):
        return lax.dynamic_slice(vec, (first + f * size,), (size,))

    return (
        outputs[None],
        dx[None],
        g_qkv,
        own(0, qk // n),
        own(qk, vw // n),
        g_out,
        own(proj, high),
        own(proj + width, high),
        g_gu,
        g_down,
    )


def solution(mesh):
    return jax.shard_map(
        local,
        mesh=mesh,
        in_specs=(
            P("fsdp", None, "ctx", None),
            P("fsdp", None, "ctx", None),
            P("fsdp", None, None),
            P("fsdp", None, None),
            P("fsdp", None),
            P("fsdp"),
            P("fsdp", None),
            P("fsdp"),
            P("fsdp"),
            P("fsdp", None),
            P("fsdp", None),
        ),
        out_specs=(
            P("fsdp", None, "ctx", None),
            P("fsdp", None, "ctx", None),
            P("fsdp", None),
            P("fsdp"),
            P("fsdp"),
            P("fsdp", None),
            P("fsdp"),
            P("fsdp"),
            P("fsdp", None),
            P("fsdp", None),
        ),
        check_vma=False,
    )
```

```python
import functools
import math

import jax
import jax.numpy as jnp
import numpy as np
from jax import lax
from jax.experimental import pallas as pl
from jax.experimental.pallas import tpu as pltpu
from jax.sharding import PartitionSpec as P

HQ = 14
KVH = 2
HD = 64
EPSILON = 1e-06
ROPE_BASE = 1000000.0
NEGATIVE = -1e30
TP = 4
LANES = 128
CHUNK = 256
PIECES = 6 * TP
ALL_PIECES = PIECES + 4
RING = 6
HOP = 2
RATE = 2
EARLY = 2
AHEAD = 4
SLOTS = 8
VEC = 32
BF = jnp.bfloat16
F32 = jnp.float32
MESH = pl.DeviceIdType.MESH
VMEM_LIMIT = 62 * 1024 * 1024


def flip1(v):
    return v + 1 - 2 * (v % 2)


def flip2(v):
    return v + 2 - 4 * ((v // 2) % 2)


def dot(a, b):
    return jnp.dot(a, b, preferred_element_type=F32)


def dot_nt(a, b):
    return lax.dot_general(a, b, (((1,), (1,)), ((), ())), preferred_element_type=F32)


class Links:
    def __init__(self, send_sems, recv_sems):
        self.send_sems, self.recv_sems = send_sems, recv_sems
        self.started = []

    def put(self, src, dst, device):
        at = len(self.started)
        copy = pltpu.make_async_remote_copy(
            src_ref=src,
            dst_ref=dst,
            send_sem=self.send_sems.at[at],
            recv_sem=self.recv_sems.at[at],
            device_id=device,
            device_id_type=MESH,
        )
        copy.start()
        self.started.append((src, device))
        return at

    def arrive(self, at, slot):
        pltpu.make_async_remote_copy(
            src_ref=slot,
            dst_ref=slot,
            send_sem=self.send_sems.at[at],
            recv_sem=self.recv_sems.at[at],
            device_id=self.started[at][1],
            device_id_type=MESH,
        ).wait_recv()

    def drain(self):
        for at, (src, device) in enumerate(self.started):
            pltpu.make_async_remote_copy(
                src_ref=src,
                dst_ref=src,
                send_sem=self.send_sems.at[at],
                recv_sem=self.recv_sems.at[at],
                device_id=device,
                device_id_type=MESH,
            ).wait_send()


class Staged:
    def __init__(self, pairs, sems):
        self.copies = [
            pltpu.make_async_copy(src, dst, sems.at[at]) for at, (src, dst) in enumerate(pairs)
        ]
        self.waited = 0
        for copy in self.copies:
            copy.start()

    def need(self, count):
        for copy in self.copies[self.waited : count]:
            copy.wait()
        self.waited = max(self.waited, count)


def enter(devices):
    barrier = pltpu.get_barrier_semaphore()
    for device in devices:
        pl.semaphore_signal(barrier, inc=1, device_id=device, device_id_type=MESH)
    pl.semaphore_wait(barrier, len(devices))


def gather_kernel(
    n, wq, wo, sm, wgu, wd, gd, wq_all, wo_all, sm_all, wgu_t, wd_t, gd_all, send, recv, here
):
    replicas = n // TP
    f, c = lax.axis_index("fsdp"), lax.axis_index("ctx")
    t, r = f % TP, f // TP
    sib, par, cross = (flip1(f), c), (flip2(f), c), (flip2(flip1(f)), c)
    peers = [((f + TP * j) % n, c) for j in range(1, replicas)]
    back = [(f - TP * j + n) % n for j in range(1, replicas)]
    rback = [(r - j + replicas) % replicas for j in range(1, replicas)]
    enter([sib, par, cross] + peers)
    links = Links(send, recv)
    local = []

    def keep(src, dst):
        copy = pltpu.make_async_copy(src, dst, here.at[len(local)])
        copy.start()
        local.append(copy)

    pending = []
    both = []
    for own, every in ((wq, wq_all), (wo, wo_all), (sm, sm_all)):
        ys = [links.put(own, every.at[f], peer) for peer in peers]
        x = links.put(own, every.at[f], par)
        s = links.put(own, every.at[f], sib)
        keep(own, every.at[f])
        both.append((every, ys, x, s))
    gd_x = links.put(gd, gd_all.at[:, t], par)
    gd_s = links.put(gd, gd_all.at[:, t], sib)
    keep(gd, gd_all.at[:, t])
    arrivals = []
    for half in range(2):
        for other, device in ((flip1(t), sib), (flip2(t), par), (flip2(flip1(t)), cross)):
            at = links.put(wgu.at[other, half], wgu_t.at[half, r, t], device)
            arrivals.append((at, half, other))
        keep(wgu.at[t, half], wgu_t.at[half, r, t])
        for j, peer in enumerate(peers):
            at = links.put(wgu.at[t, half], wgu_t.at[half, r, t], peer)
            pending.append((at, wgu_t.at[half, rback[j], t]))
    for j, peer in enumerate(peers):
        at = links.put(wd, wd_t.at[r], peer)
        pending.append((at, wd_t.at[rback[j]]))
    keep(wd, wd_t.at[r])
    later = []
    for every, ys, x, s in both:
        pending.append((s, every.at[flip1(f)]))
        for j, at in enumerate(ys):
            links.arrive(at, every.at[back[j]])
            at_x = links.put(every.at[back[j]], every.at[back[j]], par)
            later.append((every, at_x, flip2(back[j])))
            at_s = links.put(every.at[back[j]], every.at[back[j]], sib)
            pending.append((at_s, every.at[flip1(back[j])]))
        links.arrive(x, every.at[flip2(f)])
        at_s = links.put(every.at[flip2(f)], every.at[flip2(f)], sib)
        pending.append((at_s, every.at[flip2(flip1(f))]))
    for at, half, other in arrivals:
        links.arrive(at, wgu_t.at[half, r, other])
        for j, peer in enumerate(peers):
            at_y = links.put(wgu_t.at[half, r, other], wgu_t.at[half, r, other], peer)
            pending.append((at_y, wgu_t.at[half, rback[j], other]))
    for every, at, slot in later:
        links.arrive(at, every.at[slot])
        at_s = links.put(every.at[slot], every.at[slot], sib)
        pending.append((at_s, every.at[flip1(slot)]))
    links.arrive(gd_x, gd_all.at[:, flip2(t)])
    at_s = links.put(gd_all.at[:, flip2(t)], gd_all.at[:, flip2(t)], sib)
    pending.append((at_s, gd_all.at[:, flip2(flip1(t))]))
    pending.append((gd_s, gd_all.at[:, flip1(t)]))
    for at, slot in pending:
        links.arrive(at, slot)
    links.drain()
    for copy in local:
        copy.wait()


def gather_weights(n, wq, wo, sm, wgu, wd, gd):
    replicas = n // TP
    peers = replicas - 1
    copies = 3 * (4 * peers + 3) + 3 + 2 * (3 + 4 * peers) + peers
    anywhere = pl.BlockSpec(memory_space=pl.ANY)
    high, quarter = wgu.shape[2:]
    shapes = (
        jax.ShapeDtypeStruct((n,) + wq.shape, BF),
        jax.ShapeDtypeStruct((n,) + wo.shape, BF),
        jax.ShapeDtypeStruct((n,) + sm.shape, BF),
        jax.ShapeDtypeStruct((2, replicas, TP, high, quarter), BF),
        jax.ShapeDtypeStruct((replicas,) + wd.shape, BF),
        jax.ShapeDtypeStruct((gd.shape[0], TP) + gd.shape[1:], BF),
    )
    return pl.pallas_call(
        functools.partial(gather_kernel, n),
        out_shape=shapes,
        in_specs=[anywhere] * 6,
        out_specs=[anywhere] * 6,
        scratch_shapes=[
            pltpu.SemaphoreType.DMA((copies,)),
            pltpu.SemaphoreType.DMA((copies,)),
            pltpu.SemaphoreType.DMA((7,)),
        ],
        compiler_params=pltpu.CompilerParams(collective_id=0, has_side_effects=True),
        name="gather_weights",
    )(wq, wo, sm, wgu, wd, gd)


def begin_of(natural, lens, m, count):
    begin = jnp.zeros_like(natural)
    end = jnp.int32(0)
    for j in range(count):
        piece = lens[m, j]
        end = end + piece
        begin = begin + jnp.where(end <= natural, piece, 0)
    return begin


def fill_tables(m, rows, c, freq, order, lens, cos_ref, sin_ref):
    block = rows // 2
    lane = lax.broadcasted_iota(jnp.int32, (block, LANES), 1)
    low = (lane % HD) < (HD // 2)
    for b in range(2):
        natural = order[m, c * 2 + b] * block + lax.broadcasted_iota(
            jnp.int32, (block, LANES), 0
        )
        position = natural - begin_of(natural, lens, m, lens.shape[1])
        angle = position.astype(F32) * freq[0:1, :]
        at = m * rows + b * block
        cos_ref[at : at + block, :] = jnp.cos(angle)
        sine = jnp.sin(angle)
        sin_ref[at : at + block, :] = jnp.where(low, -sine, sine)


def swap_halves(u):
    lane = lax.broadcasted_iota(jnp.int32, u.shape, 1)
    low = (lane % HD) < (HD // 2)
    return jnp.where(low, pltpu.roll(u, LANES - HD // 2, 1), pltpu.roll(u, HD // 2, 1))


def fill_bias(m, rows, c, order, lens, bias_ref):
    block = rows // 2
    lane = lax.broadcasted_iota(jnp.int32, (1, rows), 1)
    query = jnp.where(
        lane < block,
        order[m, c * 2] * block + lane,
        order[m, c * 2 + 1] * block + lane - block,
    )
    begin = begin_of(query, lens, m, lens.shape[1])

    def body(k, carry):
        key = order[m, k] * block + lax.broadcasted_iota(jnp.int32, (block, rows), 0)
        allowed = (key <= query) & (key >= begin)
        at = pl.multiple_of(k * block, block)
        bias_ref[pl.ds(at, block), :] = jnp.where(allowed, 0.0, NEGATIVE)
        return carry

    lax.fori_loop(0, order.shape[1], body, 0)


def fill_heads(whole, var_ref):
    rolled = pltpu.roll(whole, HD, 1)
    low = lax.broadcasted_iota(jnp.int32, whole.shape, 1) < HD
    var_ref[0, 0] = jnp.where(low, whole, 0.0).astype(BF)
    var_ref[0, 1] = jnp.where(low, 0.0, rolled).astype(BF)
    var_ref[1, 0] = jnp.where(low, rolled, 0.0).astype(BF)
    var_ref[1, 1] = jnp.where(low, 0.0, whole).astype(BF)


def fill_heads_turned(whole, var_ref):
    turned = whole.T
    rolled = jnp.concatenate([turned[HD:], turned[:HD]], axis=0)
    low = lax.broadcasted_iota(jnp.int32, turned.shape, 0) < HD
    var_ref[0, 0] = jnp.where(low, turned, 0.0).astype(BF)
    var_ref[0, 1] = jnp.where(low, 0.0, rolled).astype(BF)
    var_ref[1, 0] = jnp.where(low, rolled, 0.0).astype(BF)
    var_ref[1, 1] = jnp.where(low, 0.0, turned).astype(BF)


def inverse_norm(v):
    return lax.rsqrt(jnp.mean(v * v, axis=1, keepdims=True) + EPSILON)


class Forward:
    def __init__(self, size, order, lens, x, freq, outs, scratch):
        self.micro, self.rows, self.ctx = size
        self.order, self.lens, self.x, self.freq = order, lens, x, freq
        self.h2, self.x2, self.qs, self.kv, self.lse, self.obt = outs
        (
            self.cos_ref, self.sin_ref, self.bias_ref, self.kvar, self.vvar, self.ob, self.h1,
            self.land, send, recv, self.out_sem,
        ) = scratch
        f, c = lax.axis_index("fsdp"), lax.axis_index("ctx")
        self.c = c
        self.others = [(f, (c + j) % self.ctx) for j in range(1, self.ctx)]
        self.back = [(c - j + self.ctx) % self.ctx for j in range(1, self.ctx)]
        self.links = Links(send, recv)
        self.arrivals, self.out_copies = [], []

    @staticmethod
    def scratch(micro, rows, ctx, width):
        keys = rows * ctx
        copies = micro * (ctx - 1)
        return [
            pltpu.VMEM((micro * rows, LANES), F32),
            pltpu.VMEM((micro * rows, LANES), F32),
            pltpu.VMEM((keys, rows), F32),
            pltpu.VMEM((KVH, 2, keys, LANES), BF),
            pltpu.VMEM((KVH, 2, LANES, keys), BF),
            pltpu.VMEM((micro, rows, HQ * HD), BF),
            pltpu.VMEM((micro, rows, width), BF),
            pltpu.VMEM((micro, ctx, rows, 2 * LANES), BF),
            pltpu.SemaphoreType.DMA((copies,)),
            pltpu.SemaphoreType.DMA((copies,)),
            pltpu.SemaphoreType.DMA((micro,)),
        ]

    @staticmethod
    def shapes(micro, rows, ctx, width):
        return (
            jax.ShapeDtypeStruct((micro, rows, width), BF),
            jax.ShapeDtypeStruct((micro, rows, width), F32),
            jax.ShapeDtypeStruct((micro, HQ // 2, rows, LANES), BF),
            jax.ShapeDtypeStruct((micro, ctx, rows, 2 * LANES), BF),
            jax.ShapeDtypeStruct((micro, HQ, rows), F32),
            jax.ShapeDtypeStruct((micro, HQ * HD, rows), BF),
        )

    @staticmethod
    def specs():
        vmem = pl.BlockSpec(memory_space=pltpu.VMEM)
        return [vmem, vmem, vmem, pl.BlockSpec(memory_space=pl.ANY), vmem, vmem]

    def tables(self):
        for m in range(self.micro):
            fill_tables(
                m, self.rows, self.c, self.freq, self.order, self.lens, self.cos_ref, self.sin_ref
            )

    def norms(self, gain_attn):
        for m in range(self.micro):
            stream = self.x[m].astype(F32)
            self.h1[m] = (stream * inverse_norm(stream) * gain_attn).astype(BF)

    def project(self, m, wq, bias_qkv):
        rows, width = self.rows, HQ * HD
        project = dot(self.h1[m], wq) + bias_qkv
        cosine = self.cos_ref[m * rows : (m + 1) * rows, :]
        sine = self.sin_ref[m * rows : (m + 1) * rows, :]
        keys = project[:, width : width + LANES]
        keys = keys * cosine + swap_halves(keys) * sine
        self.land[m, self.c, :, :LANES] = keys.astype(BF)
        self.land[m, self.c, :, LANES:] = project[:, width + LANES :].astype(BF)
        own = self.land.at[m, self.c]
        self.arrivals.append([self.links.put(own, own, other) for other in self.others])
        for p in range(HQ // 2):
            query = project[:, p * LANES : (p + 1) * LANES]
            query = query * cosine + swap_halves(query) * sine
            self.qs[m, p] = (query.astype(BF).astype(F32) * (1.0 / math.sqrt(HD))).astype(BF)

    def attend(self, m, tick):
        rows, ctx, group, pairs = self.rows, self.ctx, HQ // KVH, HQ // 2
        fill_bias(m, rows, self.c, self.order, self.lens, self.bias_ref)
        for at, source in zip(self.arrivals[m], self.back):
            self.links.arrive(at, self.land.at[m, source])
        copy = pltpu.make_async_copy(self.land.at[m], self.kv.at[m], self.out_sem.at[m])
        copy.start()
        self.out_copies.append(copy)
        both = self.land[m].reshape(ctx * rows, 2 * LANES).astype(F32)
        fill_heads(both[:, :LANES], self.kvar)
        fill_heads_turned(both[:, LANES:], self.vvar)

        def pair(p, carry):
            query = self.qs[m, p]
            mixed = jnp.zeros((LANES, rows), F32)
            for parity in range(2):
                head = 2 * p + parity
                g = head // group
                scores = dot_nt(self.kvar[g, parity], query) + self.bias_ref[...]
                top = jnp.max(scores, axis=0, keepdims=True)
                probs = jnp.exp(scores - top)
                total = jnp.sum(probs, axis=0, keepdims=True)
                mixed = mixed + dot(self.vvar[g, parity], probs.astype(BF)) / total
                self.lse[m, pl.ds(head, 1), :] = top + jnp.log(total)
            at = pl.multiple_of(p * LANES, LANES)
            self.obt[m, pl.ds(at, LANES), :] = mixed.astype(BF)
            self.ob[m, :, pl.ds(at, LANES)] = mixed.T.astype(BF)
            tick(p)
            return carry

        lax.fori_loop(0, pairs, pair, 0)

    def close(self, m, wo, gain_mlp):
        middle = self.x[m].astype(F32) + dot(self.ob[m], wo)
        self.x2[m] = middle
        self.h2[m] = (middle * inverse_norm(middle) * gain_mlp).astype(BF)

    def drain(self):
        self.links.drain()
        for copy in self.out_copies:
            copy.wait()


def forward_kernel(size, order, lens, x, wq, wo, bias_qkv, gain_attn, gain_mlp, freq, *rest):
    work = Forward(size, order, lens, x, freq, rest[:6], rest[6:])
    enter(work.others)
    work.tables()
    work.norms(gain_attn[...])
    for m in range(work.micro):
        work.project(m, wq[...], bias_qkv[...])
    for m in range(work.micro):
        work.attend(m, lambda p: None)
        work.close(m, wo[...], gain_mlp[...])
    work.drain()


def attention_forward(ctx, order, lens, x, wq, wo, bias_qkv, gain_attn, gain_mlp, freq):
    micro, rows, width = x.shape
    vmem = pl.BlockSpec(memory_space=pltpu.VMEM)
    smem = pl.BlockSpec(memory_space=pltpu.SMEM)
    return pl.pallas_call(
        functools.partial(forward_kernel, (micro, rows, ctx)),
        out_shape=Forward.shapes(micro, rows, ctx, width),
        in_specs=[smem, smem] + [vmem] * 7,
        out_specs=Forward.specs(),
        scratch_shapes=Forward.scratch(micro, rows, ctx, width),
        compiler_params=pltpu.CompilerParams(
            collective_id=1, has_side_effects=True, vmem_limit_bytes=VMEM_LIMIT
        ),
        name="attention_forward",
    )(order, lens, x, wq, wo, bias_qkv, gain_attn, gain_mlp, freq)


def front_kernel(
    size, order, lens, x, wq, wo, sm, wgu_raw, wd, gy, freq,
    h2, x2, qs, kv, lse, obt, wq_out, wo_out, gain_attn, gain_mlp, wgu_t, wd_t, gd_all,
    wq_all, wo_all, sm_all, pieces, bias_qkv, zeros, wgu_in, wd_in, gy_in, staged_sems,
    send, recv, ys, yr, zs, zr, here, *scratch
):
    n, micro, rows, ctx = size
    replicas = n // TP
    peers_n = replicas - 1
    high = wgu_raw.shape[0]
    staged = Staged([(wgu_raw, wgu_in), (wd, wd_in), (gy, gy_in)], staged_sems)
    units, width = wd.shape
    padded = wd_t.shape[1]
    proj = wq.shape[1]
    work = Forward((micro, rows, ctx), order, lens, x, freq, (h2, x2, qs, kv, lse, obt), scratch)
    f, c = lax.axis_index("fsdp"), lax.axis_index("ctx")
    t, r = f % TP, f // TP
    even = c % 2 == 0
    odd = c % 2 == 1
    sib, par, cross = (flip1(f), c), (flip2(f), c), (flip2(flip1(f)), c)
    t_sib, t_par, t_cross = flip1(t), flip2(t), flip2(flip1(t))
    twin = (f, flip1(c))
    peers = [((f + TP * j) % n, c) for j in range(1, replicas)]
    back = [(f - TP * j + n) % n for j in range(1, replicas)]
    rback = [(r - j + replicas) % replicas for j in range(1, replicas)]
    enter([sib, par, cross] + peers + work.others)
    links = Links(send, recv)
    local = []

    def keep(src, dst):
        copy = pltpu.make_async_copy(src, dst, here.at[len(local)])
        copy.start()
        local.append(copy)
        return copy

    class Spread:
        def __init__(self, own, every):
            self.every = every
            self.ys = [links.put(own, every.at[f], peer) for peer in peers]
            self.mine = own
            self.pending = [(links.put(own, every.at[f], sib), every.at[flip1(f)])]
            self.own = keep(own, every.at[f])
            self.later = []
            self.slots = [
                tuple(every.at[k] for k in (p, flip1(p), flip2(p), flip1(flip2(p)))) for p in back
            ]
            self.across = (every.at[flip2(f)], every.at[flip1(flip2(f))])

        def start_x(self):
            self.x = links.put(self.mine, self.every.at[f], par)

        def on_y(self):
            for at, (p, p_sib, p_par, p_cross) in zip(self.ys, self.slots):
                links.arrive(at, p)
                self.later.append((links.put(p, p, par), p_par, p_cross))
                self.pending.append((links.put(p, p, sib), p_sib))

        def on_x(self):
            p, p_cross = self.across
            links.arrive(self.x, p)
            self.pending.append((links.put(p, p, sib), p_cross))

        def on_late(self):
            for at, p, p_cross in self.later:
                links.arrive(at, p)
                self.pending.append((links.put(p, p, sib), p_cross))

        def done(self):
            for at, p in self.pending:
                links.arrive(at, p)
            self.own.wait()

    first = [Spread(wq, wq_all), Spread(sm, sm_all)]
    for one in first:
        one.start_x()
    second = Spread(wo, wo_all)
    pieces[...] = jnp.zeros_like(pieces)
    zeros[...] = jnp.zeros_like(zeros)
    staged.need(3)
    for k in range(TP):
        for q in range(2 * replicas):
            at = (q * TP + k) * units
            to = (q % replicas) * padded
            pieces[k, q // replicas, :, to : to + units] = wgu_in[:, at : at + units]
    gu_s = [links.put(pieces.at[t_sib, k], wgu_t.at[k, r, t], sib) for k in range(2)]
    half = units // 2
    last = wd_in.at[pl.ds(half, half)], wd_t.at[r, pl.ds(half, half)]
    head = wd_in.at[pl.ds(0, half)], wd_t.at[r, pl.ds(0, half)]

    def y_copy(at, j, src, dst):
        at = at * peers_n + j
        return pltpu.make_async_remote_copy(
            src_ref=src, dst_ref=dst, send_sem=ys.at[at], recv_sem=yr.at[at],
            device_id=peers[j], device_id_type=MESH,
        )

    def z_copy(at, j, src):
        at = at * peers_n + j
        return pltpu.make_async_remote_copy(
            src_ref=src, dst_ref=src, send_sem=zs.at[at], recv_sem=zr.at[at],
            device_id=twin, device_id_type=MESH,
        )

    def down_put(at, pair):
        for j in range(peers_n):
            y_copy(at, j, *pair).start()

    kinds = ((t, t_sib), (t_par, t_cross))

    def piece(parity, item, replica):
        return wgu_t.at[item % 2, replica, kinds[parity][item // 2]]

    def y_put(parity, item):
        for j in range(peers_n):
            mine = piece(parity, item, r)
            src = pieces.at[t, item] if (parity, item // 2) == (0, 0) else mine
            y_copy(item, j, src, mine).start()

    def z_put(parity, item):
        for j in range(peers_n):
            got = piece(parity, item, rback[j])
            y_copy(item, j, got, got).wait_recv()
            z_copy(item, j, got).start()

    @pl.when(even)
    def _():
        y_put(0, 0)
        y_put(0, 1)

    @pl.when(odd)
    def _():
        down_put(4, head)

    for q in range(replicas):
        keep(zeros, wd_t.at[q, pl.ds(units, padded - units)])
    keep(wd_in, wd_t.at[r, pl.ds(0, units)])
    for k in range(2):
        keep(pieces.at[t, k], wgu_t.at[k, r, t])
    keep(gy_in, gd_all.at[:, t])
    gd_s = links.put(gy_in, gd_all.at[:, t], sib)
    for one in first:
        one.on_y()
    gu_x = [links.put(pieces.at[t_par, k], wgu_t.at[k, r, t], par) for k in range(2)]
    gu_c = [links.put(pieces.at[t_cross, k], wgu_t.at[k, r, t], cross) for k in range(2)]
    second.start_x()
    work.tables()
    for one in first:
        one.on_x()
    for k in range(2):
        links.arrive(gu_s[k], wgu_t.at[k, r, t_sib])

    @pl.when(even)
    def _():
        y_put(0, 2)
        y_put(0, 3)
        down_put(4, head)
        down_put(5, last)

    for one in first:
        one.on_late()
    for one in first:
        one.done()
    keep(wq_all, wq_out)
    share = proj // n
    for k in range(n):
        small = sm_all[k].astype(F32)
        bias_qkv[:, k * share : k * share + min(share, LANES)] = small[0:1, : min(share, LANES)]
        if share > LANES:
            bias_qkv[:, k * share + LANES : (k + 1) * share] = small[1:2, : share - LANES]
        gain_attn[:, k * high : (k + 1) * high] = small[2:3, :high]
        gain_mlp[:, k * high : (k + 1) * high] = small[3:4, :high]
    work.norms(gain_attn[...])
    for m in range(micro):
        work.project(m, wq_all[...].reshape(width, proj), bias_qkv[...])
    second.on_y()
    gd_x = [links.put(gy_in.at[m], gd_all.at[m, t], par) for m in range(micro)]
    gd_par = [gd_all.at[m, t_par] for m in range(micro)]
    gd_c = []

    def x_piece(k):
        links.arrive(gu_x[k], wgu_t.at[k, r, t_par])
        pl.when(odd)(lambda: y_put(1, k))

    def c_piece(k):
        links.arrive(gu_c[k], wgu_t.at[k, r, t_cross])

        @pl.when(odd)
        def _():
            y_put(1, 2 + k)
            if k == 1:
                down_put(5, last)

    def on_gd():
        links.arrive(gd_x[0], gd_par[0])
        gd_c.append(links.put(gd_par[0], gd_par[0], sib))

    x_piece(0)
    x_piece(1)
    steps = {
        (0, 0): [lambda: pl.when(even)(lambda: z_put(0, 0))],
        (0, 1): [lambda: pl.when(even)(lambda: z_put(0, 1)), lambda: c_piece(0)],
        (0, 2): [lambda: pl.when(even)(lambda: z_put(0, 2))],
        (0, 3): [lambda: c_piece(1), lambda: pl.when(odd)(lambda: z_put(1, 0))],
        (0, 4): [lambda: pl.when(even)(lambda: z_put(0, 3))],
        (0, 6): [lambda: pl.when(odd)(lambda: z_put(1, 1))],
        (1, 1): [lambda: pl.when(odd)(lambda: z_put(1, 2)), second.on_x],
        (1, 3): [lambda: pl.when(odd)(lambda: z_put(1, 3)), second.on_late],
        (1, 6): [on_gd],
    }
    for m in range(micro):

        def tick(p, m=m):
            for (at_m, at_p), todo in steps.items():
                if at_m == m:

                    @pl.when(p == at_p)
                    def _(todo=todo):
                        for one in todo:
                            one()

        work.attend(m, tick)
    second.done()
    keep(wo_all, wo_out)
    for m in range(micro):
        work.close(m, wo_all[...].reshape(width, width), gain_mlp[...])
    for m in range(1, micro):
        links.arrive(gd_x[m], gd_par[m])
        gd_c.append(links.put(gd_par[m], gd_par[m], sib))
    links.arrive(gd_s, gd_all.at[:, t_sib])
    for m in range(micro):
        links.arrive(gd_c[m], gd_all.at[m, t_cross])
    for parity in range(2):

        @pl.when(even if parity == 0 else odd)
        def _(parity=parity):
            for j in range(peers_n):
                for item in range(4):
                    z_copy(item, j, piece(1 - parity, item, rback[j])).wait_recv()
                    mine = piece(parity, item, r)
                    z_copy(item, j, mine).wait_send()
                    y_copy(item, j, mine, mine).wait_send()

    for j in range(peers_n):
        for at, pair in ((4, head), (5, last)):
            y_copy(at, j, *pair).wait_send()
            first_row = 0 if at == 4 else half
            y_copy(at, j, pair[0], wd_t.at[rback[j], pl.ds(first_row, half)]).wait_recv()
    for copy in local:
        if copy is not second.own and all(copy is not one.own for one in first):
            copy.wait()
    work.drain()
    links.drain()


def gather_and_attend(n, ctx, order, lens, x, wq, wo, sm, wgu, wd, gy, freq, padded):
    micro, rows, width = x.shape
    replicas = n // TP
    peers = replicas - 1
    high, proj = wq.shape
    quarter = replicas * padded
    vmem = pl.BlockSpec(memory_space=pltpu.VMEM)
    smem = pl.BlockSpec(memory_space=pltpu.SMEM)
    anywhere = pl.BlockSpec(memory_space=pl.ANY)
    sems = pltpu.SemaphoreType.DMA
    copies = 3 * (4 * peers + 3) + 6 + 1 + 2 * micro
    gain = jax.ShapeDtypeStruct((1, width), F32)
    return pl.pallas_call(
        functools.partial(front_kernel, (n, micro, rows, ctx)),
        out_shape=Forward.shapes(micro, rows, ctx, width) + (
            jax.ShapeDtypeStruct((n, high, proj), BF),
            jax.ShapeDtypeStruct((n, high, width), BF),
            gain,
            gain,
            jax.ShapeDtypeStruct((2, replicas, TP, high, quarter), BF),
            jax.ShapeDtypeStruct((replicas, padded, width), BF),
            jax.ShapeDtypeStruct((micro, TP, rows, width), BF),
        ),
        in_specs=[smem, smem, vmem] + [anywhere] * 6 + [vmem],
        out_specs=Forward.specs() + [anywhere, anywhere, vmem, vmem] + [anywhere] * 3,
        scratch_shapes=[
            pltpu.VMEM((n, high, proj), BF),
            pltpu.VMEM((n, high, width), BF),
            pltpu.VMEM((n,) + sm.shape, BF),
            pltpu.VMEM((TP, 2, high, quarter), BF),
            pltpu.VMEM((1, proj), F32),
            pltpu.VMEM((padded - wd.shape[0], width), BF),
            pltpu.VMEM(wgu.shape, BF),
            pltpu.VMEM(wd.shape, BF),
            pltpu.VMEM(gy.shape, BF),
            sems((3,)),
            sems((copies,)), sems((copies,)),
            sems((6 * peers,)), sems((6 * peers,)), sems((4 * peers,)), sems((4 * peers,)),
            sems((9 + replicas,)),
        ] + Forward.scratch(micro, rows, ctx, width),
        compiler_params=pltpu.CompilerParams(
            collective_id=5, has_side_effects=True, vmem_limit_bytes=VMEM_LIMIT
        ),
        name="gather_and_attend",
    )(order, lens, x, wq, wo, sm, wgu, wd, gy, freq)


def mlp_kernel(
    size, h2, gd_hbm, wgu_hbm, wd_hbm,
    out, out_par, gh2, grads,
    gd, wgu, wd, hbuf, turned_h, turned_g, acc_out, acc_gh, dgate, dup, ddown,
    sib_out, sib_in, par_out, par_in, keep_sum, stage, send, recv, out_sem, staged_sems,
):
    micro, rows, width, replicas, padded = size
    quarter = replicas * padded
    both = 2 * rows
    f, c = lax.axis_index("fsdp"), lax.axis_index("ctx")
    t = f % TP
    core = t % 2
    mine, theirs = t - core, flip2(t) - core
    t_sib, t_par, t_cross = flip1(t), flip2(t), flip2(flip1(t))
    sib, par = (flip1(f), c), (flip2(f), c)
    staged = Staged(
        [(h2.at[m], hbuf.at[m, t]) for m in range(micro)]
        + [(gd_hbm.at[0], gd.at[0]), (wgu_hbm, wgu), (wd_hbm, wd)]
        + [(gd_hbm.at[m], gd.at[m]) for m in range(1, micro)],
        staged_sems,
    )
    enter([sib, par])
    links = Links(send, recv)
    from_sib, from_par, from_cross = [], [], [None] * micro
    for m in range(micro):
        from_par.append(links.put(h2.at[m], hbuf.at[m, t], par))
        from_sib.append(links.put(h2.at[m], hbuf.at[m, t], sib))

    def grad_of(m, side):
        return gd[m, pl.ds(side, 2)].reshape(both, width)

    def forward_on(m):
        buf = hbuf.at[m, t_par]
        links.arrive(from_par[m], buf)
        from_cross[m] = links.put(buf, buf, sib)

    def chunk(m, side, first, j):
        at = pl.multiple_of(j * CHUNK, CHUNK)
        hidden_in = hbuf[m, pl.ds(side, 2)].reshape(both, width)
        grad_in = grad_of(m, side)
        w_gate = wgu[0, :, pl.ds(at, CHUNK)]
        w_up = wgu[1, :, pl.ds(at, CHUNK)]
        w_down = wd[pl.ds(at, CHUNK), :]
        gate = dot(hidden_in, w_gate)
        up = dot(hidden_in, w_up)
        gm = dot_nt(grad_in, w_down)
        sg = 0.5 * jnp.tanh(0.5 * gate) + 0.5
        silu = gate * sg
        mb = (silu * up).astype(BF)
        ggate = (gm * up * (sg + silu * (1.0 - sg))).astype(BF)
        gup = (gm * silu).astype(BF)
        acc_out[...] += dot(mb, w_down)
        acc_gh[...] += dot_nt(ggate, w_gate) + dot_nt(gup, w_up)
        if first:
            dgate[:, pl.ds(at, CHUNK)] = dot(turned_h[...], ggate)
            dup[:, pl.ds(at, CHUNK)] = dot(turned_h[...], gup)
            ddown[:, pl.ds(at, CHUNK)] = dot(turned_g[...], mb)
        else:
            dgate[:, pl.ds(at, CHUNK)] += dot(turned_h[...], ggate)
            dup[:, pl.ds(at, CHUNK)] += dot(turned_h[...], gup)
            ddown[:, pl.ds(at, CHUNK)] += dot(turned_g[...], mb)

    def compute(m, side, first, middle, late):
        turned_h[...] = hbuf[m, pl.ds(side, 2)].reshape(both, width).T
        turned_g[...] = grad_of(m, side).T
        acc_out[...] = jnp.zeros_like(acc_out)
        acc_gh[...] = jnp.zeros_like(acc_gh)
        chunks = quarter // CHUNK

        def body(j, carry):
            chunk(m, side, first, j)
            return carry

        lax.fori_loop(0, 2, body, 0)
        middle()
        lax.fori_loop(2, chunks - 1, body, 0)
        late()
        lax.fori_loop(chunks - 1, chunks, body, 0)

    def share(step):
        here = pl.multiple_of(core * rows, rows)
        there = pl.multiple_of(rows - core * rows, rows)
        ats = []
        for k, acc in enumerate((acc_gh, acc_out)):
            sib_out[step, k] = acc[pl.ds(there, rows), :].astype(BF)
            ats.append(links.put(sib_out.at[step, k], sib_in.at[step, k], sib))
            keep_sum[k] = acc[pl.ds(here, rows), :]
        return ats

    def pass_on(step, m, ats):
        for k, (at, ref) in enumerate(zip(ats, (par_out, out_par))):
            links.arrive(at, sib_in.at[step, k])
            ref[m] = (keep_sum[k] + sib_in[step, k].astype(F32)).astype(BF)
        return links.put(par_out.at[m], par_in.at[m], par)

    def stay(step, m, ats):
        for k, (at, ref) in enumerate(zip(ats, (gh2, out))):
            links.arrive(at, sib_in.at[step, k])
            ref[m] = keep_sum[k] + sib_in[step, k].astype(F32)

    def finish(m, at):
        links.arrive(at, par_in.at[m])
        gh2[m] = gh2[m] + par_in[m].astype(F32)

    plan = [(0, True)] + [(m, False) for m in range(micro)] + [(m, True) for m in range(1, micro)]
    waiting = None
    sums = [None] * micro
    ready_own = [False] * micro
    for step, (m, own) in enumerate(plan):
        if own:
            links.arrive(from_sib[m], hbuf.at[m, t_sib])
        else:
            links.arrive(from_cross[m], hbuf.at[m, t_cross])
        staged.need((micro + 3) if m == 0 else len(staged.copies))

        def late(step=step):
            if step < micro:
                forward_on(step)

        def middle(step=step):
            if step > 0:
                last_m, last_own = plan[step - 1]
                if last_own:
                    stay(step - 1, last_m, waiting)
                else:
                    sums[last_m] = pass_on(step - 1, last_m, waiting)

        compute(m, mine if own else theirs, step == 0, middle, late)
        waiting = share(step)
    high = width // (replicas * TP)
    copies = []
    for replica in range(replicas):
        for k in range(PIECES):
            slot = len(copies) % SLOTS
            if len(copies) >= SLOTS:
                copies[-SLOTS].wait()
            if k < 4 * TP:
                at = (replica * TP + k // 4) * high
                lane = (k % 2) * (quarter // 2)
                stage[slot] = (dgate, dup)[(k // 2) % 2][
                    at : at + high, lane : lane + quarter // 2
                ].astype(BF)
            else:
                for q in range(replicas // 2):
                    at = (k - 4 * TP) * (replicas // 2) + q
                    stage[slot, :, q * padded : (q + 1) * padded] = ddown[
                        at * high : (at + 1) * high, replica * padded : (replica + 1) * padded
                    ].astype(BF)
            copy = pltpu.make_async_copy(stage.at[slot], grads.at[replica, k], out_sem.at[slot])
            copy.start()
            copies.append(copy)
    last_m, last_own = plan[-1]
    if last_own:
        stay(len(plan) - 1, last_m, waiting)
    else:
        sums[last_m] = pass_on(len(plan) - 1, last_m, waiting)
    for m in range(micro):
        finish(m, sums[m])
    for copy in copies[-SLOTS:]:
        copy.wait()
    links.drain()


def mlp(n, h2, gd, wgu, wd):
    micro, rows, width = h2.shape
    replicas = n // TP
    padded = wd.shape[0] // replicas
    quarter = replicas * padded
    vmem = pl.BlockSpec(memory_space=pltpu.VMEM)
    steps = 2 * micro
    copies = micro * 3 + steps * 2 + micro
    whole = jax.ShapeDtypeStruct((micro, rows, width), F32)
    return pl.pallas_call(
        functools.partial(mlp_kernel, (micro, rows, width, replicas, padded)),
        out_shape=(
            whole,
            jax.ShapeDtypeStruct((micro, rows, width), BF),
            whole,
            jax.ShapeDtypeStruct((replicas, PIECES, width // n, quarter // 2), BF),
        ),
        in_specs=[pl.BlockSpec(memory_space=pl.ANY)] * 4,
        out_specs=[vmem, vmem, vmem, pl.BlockSpec(memory_space=pl.ANY)],
        scratch_shapes=[
            pltpu.VMEM(gd.shape, BF),
            pltpu.VMEM(wgu.shape, BF),
            pltpu.VMEM(wd.shape, BF),
            pltpu.VMEM((micro, TP, rows, width), BF),
            pltpu.VMEM((width, 2 * rows), BF),
            pltpu.VMEM((width, 2 * rows), BF),
            pltpu.VMEM((2 * rows, width), F32),
            pltpu.VMEM((2 * rows, width), F32),
            pltpu.VMEM((width, quarter), F32),
            pltpu.VMEM((width, quarter), F32),
            pltpu.VMEM((width, quarter), F32),
            pltpu.VMEM((steps, 2, rows, width), BF),
            pltpu.VMEM((steps, 2, rows, width), BF),
            pltpu.VMEM((micro, rows, width), BF),
            pltpu.VMEM((micro, rows, width), BF),
            pltpu.VMEM((2, rows, width), F32),
            pltpu.VMEM((SLOTS, width // n, quarter // 2), BF),
            pltpu.SemaphoreType.DMA((copies,)),
            pltpu.SemaphoreType.DMA((copies,)),
            pltpu.SemaphoreType.DMA((SLOTS,)),
            pltpu.SemaphoreType.DMA((2 * micro + 2,)),
        ],
        compiler_params=pltpu.CompilerParams(
            collective_id=2, has_side_effects=True, vmem_limit_bytes=VMEM_LIMIT
        ),
        name="mlp",
    )(h2, gd, wgu, wd)


def add_into(dst, a, b):
    dst[...] = (a[...].astype(F32) + b[...].astype(F32)).astype(BF)


class Sums:
    def __init__(self, n, ctx, grads, fin, scratch):
        self.n, self.ctx, self.grads, self.fin = n, ctx, grads, fin
        (
            self.total, self.peer_in, self.pre, self.suf, self.suf_out, self.land,
            self.vec, self.vec_in,
            self.ys, self.yr, self.ps, self.pr, self.ss, self.sr, self.fs, self.fr,
            self.asend, self.arecv, self.own_sem, self.out_sem,
        ) = scratch[:20]
        self.fold_scratch = scratch[20:]
        self.replicas = n // TP
        self.f, self.c = lax.axis_index("fsdp"), lax.axis_index("ctx")
        f, c = self.f, self.c
        self.t, self.r = f % TP, f // TP
        self.core, self.side = self.t % 2, self.t // 2
        self.sib, self.par, self.cross = (flip1(f), c), (flip2(f), c), (flip2(flip1(f)), c)
        self.peers = [((f + TP * j) % n, c) for j in range(1, self.replicas)]
        self.left, self.right = (f, (c + ctx - 1) % ctx), (f, (c + 1) % ctx)
        self.links = Links(self.asend, self.arecv)

    @staticmethod
    def scratch(n, high, wide, columns):
        replicas = n // TP
        sems = pltpu.SemaphoreType.DMA
        peers = replicas - 1
        return [
            pltpu.VMEM((ALL_PIECES, high, wide), BF),
            pltpu.VMEM((peers, PIECES, high, wide), BF),
            pltpu.VMEM((ALL_PIECES, high, wide), BF),
            pltpu.VMEM((ALL_PIECES, high, wide), BF),
            pltpu.VMEM((RING, high, wide), BF),
            pltpu.VMEM((4 * TP, high, wide), BF),
            pltpu.VMEM((3, VEC, LANES), F32),
            pltpu.VMEM((2 + peers, VEC, LANES), F32),
            sems((peers * PIECES,)), sems((peers * PIECES,)),
            sems((ALL_PIECES,)), sems((ALL_PIECES,)), sems((ALL_PIECES,)), sems((ALL_PIECES,)),
            sems((4 * TP,)), sems((4 * TP,)),
            sems(((len(columns) + 1) * (2 + peers),)), sems(((len(columns) + 1) * (2 + peers),)),
            sems((1,)), sems((ALL_PIECES,)),
        ] + [
            one
            for wide_here in columns
            for one in (
                pltpu.VMEM((replicas, 2, 2, high, wide_here), BF),
                pltpu.VMEM((replicas, 2, high, wide_here), BF),
                pltpu.VMEM((replicas, high, wide_here), BF),
                pltpu.VMEM((peers, high, wide_here), BF),
            )
        ]

    def around(self):
        return [self.sib, self.par, self.cross] + self.peers + [self.left, self.right]

    def peer_copy(self, j, k):
        at = j * PIECES + k
        return pltpu.make_async_remote_copy(
            src_ref=self.grads.at[(self.r + j + 1) % self.replicas, k],
            dst_ref=self.peer_in.at[j, k],
            send_sem=self.ys.at[at],
            recv_sem=self.yr.at[at],
            device_id=self.peers[j],
            device_id_type=MESH,
        )

    def own_copy(self):
        return pltpu.make_async_copy(
            self.grads.at[self.r], self.total.at[pl.ds(0, PIECES)], self.own_sem.at[0]
        )

    def start(self):
        self.own_copy().start()
        for k in range(AHEAD):
            for j in range(self.replicas - 1):
                self.peer_copy(j, k).start()

    def pre_copy(self, k, src):
        return pltpu.make_async_remote_copy(
            src_ref=src.at[k], dst_ref=self.pre.at[k], send_sem=self.ps.at[k],
            recv_sem=self.pr.at[k], device_id=self.right, device_id_type=MESH,
        )

    def suf_copy(self, k, src):
        return pltpu.make_async_remote_copy(
            src_ref=src, dst_ref=self.suf.at[k], send_sem=self.ss.at[k],
            recv_sem=self.sr.at[k], device_id=self.left, device_id_type=MESH,
        )

    def out_copy(self, k, src):
        return pltpu.make_async_copy(src.at[k], self.fin.at[k], self.out_sem.at[k])

    def step(self, time, carry):
        self.tick(time)
        return carry

    def tick(self, time):
        c, ctx, total = self.c, self.ctx, self.total

        @pl.when(time + AHEAD < PIECES)
        def _():
            for j in range(self.replicas - 1):
                self.peer_copy(j, time + AHEAD).start()

        @pl.when(time < PIECES)
        def _():
            for j in range(self.replicas - 1):
                self.peer_copy(j, time).wait_recv()
                add_into(total.at[time], total.at[time], self.peer_in.at[j, time])

        k = time - HOP * c

        @pl.when((k >= 0) & (k < ALL_PIECES))
        def _():
            @pl.when(c > 0)
            def _():
                self.pre_copy(k, total).wait_recv()
                add_into(self.pre.at[k], self.pre.at[k], total.at[k])

                @pl.when(c < ctx - 1)
                def _():
                    self.pre_copy(k, self.pre).start()

            @pl.when(c == 0)
            def _():
                self.pre_copy(k, total).start()

        k2 = time - HOP * (ctx - 1 - c)

        @pl.when((k2 >= 0) & (k2 < ALL_PIECES))
        def _():
            @pl.when(c < ctx - 1)
            def _():
                self.suf_copy(k2, total.at[k2]).wait_recv()

            @pl.when((c > 0) & (c < ctx - 1))
            def _():
                @pl.when(k2 >= RING)
                def _():
                    self.suf_copy(k2 - RING, self.suf_out.at[(k2 - RING) % RING]).wait_send()

                add_into(self.suf_out.at[k2 % RING], self.suf.at[k2], total.at[k2])
                self.suf_copy(k2, self.suf_out.at[k2 % RING]).start()

            @pl.when(c == ctx - 1)
            def _():
                self.suf_copy(k2, total.at[k2]).start()

        k3 = time - HOP * jnp.maximum(c, ctx - 1 - c)

        @pl.when((k3 >= 0) & (k3 < ALL_PIECES))
        def _():
            @pl.when(c == 0)
            def _():
                add_into(self.suf.at[k3], self.suf.at[k3], total.at[k3])

            @pl.when((c > 0) & (c < ctx - 1))
            def _():
                add_into(self.suf.at[k3], self.suf.at[k3], self.pre.at[k3])

            @pl.when((k3 < 4 * TP) & (k3 // 4 != self.t))
            def _():
                @pl.when(c == ctx - 1)
                def _():
                    self.fin_copy_from(k3, self.pre).start()

                @pl.when(c < ctx - 1)
                def _():
                    self.fin_copy_from(k3, self.suf).start()

            @pl.when((k3 >= 4 * TP) | (k3 // 4 == self.t))
            def _():
                @pl.when(c == ctx - 1)
                def _():
                    self.out_copy(k3, self.pre).start()

                @pl.when(c < ctx - 1)
                def _():
                    self.out_copy(k3, self.suf).start()

    def fin_copy_from(self, k, src):
        return pltpu.make_async_remote_copy(
            src_ref=src.at[k], dst_ref=self.land.at[4 * self.t + k % 4], send_sem=self.fs.at[k],
            recv_sem=self.fr.at[4 * self.t + k % 4],
            device_id=(self.f - self.t + k // 4, self.c), device_id_type=MESH,
        )

    @property
    def ticks(self):
        return ALL_PIECES + HOP * (self.ctx - 1)

    def close(self):
        c, ctx = self.c, self.ctx

        def arrive(k, carry):
            @pl.when(k // 4 != self.t)
            def _():
                pltpu.make_async_remote_copy(
                    src_ref=self.land.at[k], dst_ref=self.land.at[k], send_sem=self.fs.at[k],
                    recv_sem=self.fr.at[k], device_id=(self.f - self.t + k // 4, c),
                    device_id_type=MESH,
                ).wait_recv()
                self.out_copy(k, self.land).start()
                self.fin_copy_from(k, self.suf).wait_send()

            return carry

        lax.fori_loop(0, 4 * TP, arrive, 0)

        def settle(k, carry):
            @pl.when(c < ctx - 1)
            def _():
                self.pre_copy(k, self.total).wait_send()

            @pl.when((c == ctx - 1) | ((c > 0) & (k >= ALL_PIECES - RING)))
            def _():
                self.suf_copy(k, self.total.at[k]).wait_send()

            self.out_copy(k, self.suf).wait()
            return carry

        lax.fori_loop(0, ALL_PIECES, settle, 0)

        def peers(k, carry):
            for j in range(self.replicas - 1):
                self.peer_copy(j, k).wait_send()
            return carry

        lax.fori_loop(0, PIECES, peers, 0)
        self.links.drain()

    def place(self, column, value):
        wide = self.total.shape[-1]
        done = 0
        while done < value.shape[1]:
            piece, at = divmod(column + done, wide)
            count = min(wide - at, value.shape[1] - done)
            self.total[PIECES + piece, : value.shape[0], at : at + count] = value[
                :, done : done + count
            ]
            done += count


class Fold:
    def __init__(self, sums, index, column):
        self.sums, self.column = sums, column
        self.own, self.got_core, self.got_par, self.got_ring = sums.fold_scratch[
            4 * index : 4 * index + 4
        ]
        replicas, r = sums.replicas, sums.r
        self.src_core = self.own.at[:, :, 1 - sums.core]
        self.mine_core = [
            [self.own.at[k, s, sums.core] for s in range(2)] for k in range(replicas)
        ]
        self.src_par = self.got_core.at[:, 1 - sums.side]
        self.mine_par = [self.got_core.at[k, sums.side] for k in range(replicas)]
        self.src_ring = [
            self.got_par.at[(r + j + 1) % replicas] for j in range(replicas - 1)
        ]
        self.mine = self.got_par.at[r]

    def set(self, k, value):
        self.own[k // TP, (k // 2) % 2, k % 2] = value.astype(BF)

    def over_core(self):
        self.at = self.sums.links.put(self.src_core, self.got_core, self.sums.sib)

    def over_x(self):
        links = self.sums.links
        links.arrive(self.at, self.got_core)
        for k, pair in enumerate(self.mine_core):
            for s, mine in enumerate(pair):
                add_into(self.got_core.at[k, s], self.got_core.at[k, s], mine)
        self.at = links.put(self.src_par, self.got_par, self.sums.par)

    def over_y(self):
        links = self.sums.links
        links.arrive(self.at, self.got_par)
        for k, mine in enumerate(self.mine_par):
            add_into(self.got_par.at[k], self.got_par.at[k], mine)
        self.ats = [
            links.put(src, self.got_ring.at[j], peer)
            for j, (src, peer) in enumerate(zip(self.src_ring, self.sums.peers))
        ]

    def finish(self):
        for j, at in enumerate(self.ats):
            self.sums.links.arrive(at, self.got_ring.at[j])
            add_into(self.mine, self.mine, self.got_ring.at[j])
        self.sums.place(self.column, self.mine[...])


class FoldVectors:
    def __init__(self, sums, column):
        self.sums, self.column = sums, column

    def over_core(self):
        sums = self.sums
        self.at = sums.links.put(sums.vec.at[0], sums.vec_in.at[0], sums.sib)

    def over_x(self):
        sums = self.sums
        sums.links.arrive(self.at, sums.vec_in.at[0])
        sums.vec[1] = sums.vec[0] + sums.vec_in[0]
        self.at = sums.links.put(sums.vec.at[1], sums.vec_in.at[1], sums.par)

    def over_y(self):
        sums = self.sums
        sums.links.arrive(self.at, sums.vec_in.at[1])
        sums.vec[2] = sums.vec[1] + sums.vec_in[1]
        self.ats = [
            sums.links.put(sums.vec.at[2], sums.vec_in.at[2 + j], peer)
            for j, peer in enumerate(sums.peers)
        ]

    def finish(self):
        sums = self.sums
        vec = sums.vec[2]
        for j, at in enumerate(self.ats):
            sums.links.arrive(at, sums.vec_in.at[2 + j])
            vec = vec + sums.vec_in[2 + j]
        sums.place(self.column, vec.astype(BF))


def fold_columns(width, proj):
    pairs = HQ // 2
    early = (pairs // 2 + 1) * LANES
    sizes = (width, early, HQ * HD - early, proj - HQ * HD)
    return sizes, (0, width, width + early)


class Plain:
    def __init__(self, own):
        self.own = own

    def set(self, k, value):
        self.own[k // TP, (k // 2) % 2, k % 2] = value.astype(BF)

    def over_core(self):
        pass

    over_x = over_y = finish = over_core


def backward_kernel(size, merged, order, lens, gain_attn, gain_mlp, freq, *rest):
    n, micro, rows, ctx = size
    hbm, rest = rest[:11], rest[11:]
    out_par, grads, dx, outputs = rest[:4]
    rest = rest[4:]
    outs = 1 if merged else 5
    fin, rest = rest[:outs], rest[outs:]
    (
        x2, gh2, gy, wo, x, obt, kv, qs, lse, wq, out, staged_sems,
        out_in, out_send, out_recv, cos_ref, sin_ref, bias_ref, kvar, kvar_turned, vvar,
        go_ref, gp, h1t, gk, gv, part, land, vec_wide, send, recv,
    ), rest = rest[:31], rest[31:]
    staged = Staged(
        list(zip(hbm, (x2, gh2, gy, wo, x, obt, kv, qs, lse, wq, out))), staged_sems
    )
    group = HQ // KVH
    pairs = HQ // 2
    width = HQ * HD
    high = width // n
    proj = wq.shape[1]
    scale = 1.0 / math.sqrt(HD)
    f, c = lax.axis_index("fsdp"), lax.axis_index("ctx")
    others = [(f, (c + j) % ctx) for j in range(1, ctx)]
    back = [(c - j + ctx) % ctx for j in range(1, ctx)]
    sizes, starts = fold_columns(width, proj)
    if merged:
        sums = Sums(n, ctx, grads, fin[0], rest)
        enter(others + sums.around())
        sums.start()
        last = (ALL_PIECES - PIECES - 1) * sums.total.shape[-1]
        folds = [Fold(sums, k, start) for k, start in enumerate(starts + (last,))]
        fold_v = FoldVectors(sums, last + sizes[3])
    else:
        enter(others + [(flip2(f), c)])
        folds = [Plain(own) for own in fin[:4]]
        fold_v = Plain(None)
    fold_o, fold_a, fold_b, fold_k = folds
    out_links = Links(out_send, out_recv)
    out_at = out_links.put(out_par, out_in, (flip2(f), c))
    links = Links(send, recv)
    ticks = [0]

    def advance(upto):
        if merged and upto > ticks[0]:
            lax.fori_loop(ticks[0], upto, sums.step, 0)
            ticks[0] = upto

    if merged:
        for k in range(PIECES, ALL_PIECES):
            sums.total[k] = jnp.zeros(sums.total.shape[1:], BF)
        sums.own_copy().wait()
    for m in range(micro):
        fill_tables(m, rows, c, freq, order, lens, cos_ref, sin_ref)
        advance(EARLY * (m + 1) // micro)
        staged.need(5)
        stream = x2[m]
        inverse = inverse_norm(stream)
        normed = stream * inverse
        grad = gh2[m]
        term = jnp.sum(grad * normed, axis=0, keepdims=True)
        at = proj + width
        vec_wide[:, at : at + width] = term if m == 0 else vec_wide[:, at : at + width] + term
        grad = grad * gain_mlp[...]
        grad = gy[m].astype(F32) + inverse * (
            grad - normed * jnp.mean(grad * normed, axis=1, keepdims=True)
        )
        dx[m] = grad
        spread = dot_nt(grad.astype(BF), wo[...]).astype(BF)
        for p in range(pairs):
            go_ref[m, p] = spread[:, p * LANES : (p + 1) * LANES]
        stream = x[m].astype(F32)
        h1t[:, m * rows : (m + 1) * rows] = (
            (stream * inverse_norm(stream) * gain_attn[...]).T.astype(BF)
        )
    staged.need(len(staged.copies))
    for k in range(n):
        term = dot(obt[0, k * high : (k + 1) * high, :], dx[0].astype(BF))
        for m in range(1, micro):
            term = term + dot(obt[m, k * high : (k + 1) * high, :], dx[m].astype(BF))
        fold_o.set(k, term)
    fold_o.over_core()

    def columns(fold, lo, hi):
        for k in range(n):
            fold.set(k, dot(h1t[k * high : (k + 1) * high, :], gp[:, lo:hi]))

    low = lax.broadcasted_iota(jnp.int32, (ctx * rows, LANES), 1) < HD
    mid = pairs // 2
    part_src = [
        [[part.at[m, g, other[1]] for other in others] for g in range(KVH)] for m in range(micro)
    ]
    part_dst = [[land.at[m, g, c] for g in range(KVH)] for m in range(micro)]
    arrivals = [[None] * KVH for _ in range(micro)]

    def send_group(m, g):
        keys = gk[g, 0] + pltpu.roll(gk[g, 1], HD, 1)
        values = pltpu.roll(gv[g, 0], HD, 1) + gv[g, 1]
        whole = jnp.where(low, keys, values).astype(BF)
        part[m, g] = whole.reshape(ctx, rows, LANES)
        arrivals[m][g] = [
            links.put(src, part_dst[m][g], other) for src, other in zip(part_src[m][g], others)
        ]

    for m in range(micro):
        fill_bias(m, rows, c, order, lens, bias_ref)
        both = kv[m].reshape(ctx * rows, 2 * LANES).astype(F32)
        fill_heads(both[:, :LANES], kvar)
        fill_heads_turned(both[:, :LANES], kvar_turned)
        fill_heads(both[:, LANES:], vvar)
        gk[...] = jnp.zeros_like(gk)
        gv[...] = jnp.zeros_like(gv)
        cosine = cos_ref[m * rows : (m + 1) * rows, :]
        sine = sin_ref[m * rows : (m + 1) * rows, :]

        def pair(p, carry):
            query = qs[m, p]
            go = go_ref[m, p]
            grad_query = jnp.zeros((LANES, rows), F32)
            for parity in range(2):
                head = 2 * p + parity
                g = head // group
                scores = dot_nt(kvar[g, parity], query) + bias_ref[...]
                probs = jnp.exp(scores - lse[m, pl.ds(head, 1), :])
                grad_probs = dot_nt(vvar[g, parity], go)
                delta = jnp.sum(probs * grad_probs, axis=0, keepdims=True)
                grad_scores = (probs * (grad_probs - delta)).astype(BF)
                grad_query = grad_query + dot(kvar_turned[g, parity], grad_scores)
                gk[g, parity] += dot(grad_scores, query)
                gv[g, parity] += dot(probs.astype(BF), go)
            turned = grad_query.T * scale
            turned = turned * cosine - swap_halves(turned) * sine
            at = pl.multiple_of(p * LANES, LANES)
            gp[m * rows : (m + 1) * rows, pl.ds(at, LANES)] = turned.astype(BF)

            if m == 0:
                pl.when(p == 0)(fold_o.over_x)

            @pl.when(p == mid)
            def _():
                send_group(m, 0)
                if m == micro - 1:
                    columns(fold_a, 0, sizes[1])
                    fold_a.over_core()
                elif m == 0:
                    fold_o.over_y()

            if m == micro - 1:
                pl.when(p == mid + 1)(fold_a.over_x)

            @pl.when(p == pairs - 1)
            def _():
                send_group(m, 1)
                if m == micro - 1:
                    fold_a.over_y()

            if merged:
                step = m * pairs + p
                lax.fori_loop(
                    EARLY + RATE * step // 2, EARLY + RATE * (step + 1) // 2, sums.step, 0
                )
            return carry

        lax.fori_loop(0, pairs, pair, 0)
    ticks[0] = EARLY + RATE * micro * pairs // 2
    spare = max(0, PIECES - ticks[0])
    first = ticks[0]
    columns(fold_b, sizes[1], width)
    fold_b.over_core()
    advance(first + spare * 2 // 8)
    fold_b.over_x()
    advance(first + spare * 4 // 8)
    for m in range(micro):
        totals = []
        for g in range(KVH):
            total = part[m, g, c].astype(F32)
            for at, source in zip(arrivals[m][g], back):
                links.arrive(at, land.at[m, g, source])
                total = total + land[m, g, source].astype(F32)
            totals.append(total)
        lower = lax.broadcasted_iota(jnp.int32, (rows, LANES), 1) < HD
        cosine = cos_ref[m * rows : (m + 1) * rows, :]
        sine = sin_ref[m * rows : (m + 1) * rows, :]
        grad_keys = jnp.where(lower, totals[0], pltpu.roll(totals[1], HD, 1))
        grad_keys = grad_keys * cosine - swap_halves(grad_keys) * sine
        gp[m * rows : (m + 1) * rows, width : width + LANES] = grad_keys.astype(BF)
        grad_values = jnp.where(lower, pltpu.roll(totals[0], HD, 1), totals[1])
        gp[m * rows : (m + 1) * rows, width + LANES :] = grad_values.astype(BF)
    columns(fold_k, width, proj)
    fold_k.over_core()
    advance(first + spare * 5 // 8)
    fold_b.over_y()
    for m in range(micro):
        grad_project = gp[m * rows : (m + 1) * rows, :]
        stream = x[m].astype(F32)
        inverse = inverse_norm(stream)
        normed = stream * inverse
        term = jnp.sum(grad_project.astype(F32), axis=0, keepdims=True)
        vec_wide[:, :proj] = term if m == 0 else vec_wide[:, :proj] + term
        grad = dot_nt(grad_project, wq[...])
        term = jnp.sum(grad * normed, axis=0, keepdims=True)
        at = slice(proj, proj + width)
        vec_wide[:, at] = term if m == 0 else vec_wide[:, at] + term
        grad = grad * gain_attn[...]
        dx[m] = dx[m] + inverse * (
            grad - normed * jnp.mean(grad * normed, axis=1, keepdims=True)
        )
    vec = sums.vec.at[0] if merged else fin[4]
    vec[...] = jnp.zeros((VEC, LANES), F32)
    for k in range(vec_wide.shape[1] // LANES):
        vec[k : k + 1, :] = vec_wide[:, k * LANES : (k + 1) * LANES]
    fold_v.over_core()
    fold_k.over_x()
    advance(first + spare * 6 // 8)
    fold_v.over_x()
    fold_o.finish()
    fold_a.finish()
    advance(first + spare * 7 // 8)
    fold_k.over_y()
    fold_v.over_y()
    advance(first + spare)
    out_links.arrive(out_at, out_in)
    for m in range(micro):
        outputs[m] = (x2[m] + out[m] + out_in[m].astype(F32)).astype(BF)
    out_links.drain()
    fold_b.finish()
    advance(ALL_PIECES - 1)
    fold_k.finish()
    fold_v.finish()
    if merged:
        advance(sums.ticks)
        sums.close()
    links.drain()


def attention_backward(
    n, ctx, order, lens, gh2, x2, gy, x, wq, wo, gain_attn, gain_mlp, freq, qs, kv, lse, obt,
    out, out_par, grads,
):
    micro, rows, width = x.shape
    keys = rows * ctx
    proj = wq.shape[1]
    replicas = n // TP
    high, wide = grads.shape[2:]
    merged = ctx <= 4
    vmem = pl.BlockSpec(memory_space=pltpu.VMEM)
    smem = pl.BlockSpec(memory_space=pltpu.SMEM)
    anywhere = pl.BlockSpec(memory_space=pl.ANY)
    copies = micro * KVH * (ctx - 1)
    sizes, _ = fold_columns(width, proj)
    out_shape = [
        jax.ShapeDtypeStruct((micro, rows, width), F32),
        jax.ShapeDtypeStruct((micro, rows, width), BF),
    ]
    if merged:
        out_shape += [jax.ShapeDtypeStruct((ALL_PIECES, high, wide), BF)]
    else:
        out_shape += [
            jax.ShapeDtypeStruct((replicas, 2, 2, high, size), BF) for size in sizes
        ] + [jax.ShapeDtypeStruct((VEC, LANES), F32)]
    operands = (x2, gh2, gy, wo, x, obt, kv, qs, lse, wq, out)
    result = pl.pallas_call(
        functools.partial(backward_kernel, (n, micro, rows, ctx), merged),
        out_shape=out_shape,
        in_specs=[smem, smem] + [vmem] * 3 + [anywhere] * 13,
        out_specs=[vmem] * 2 + ([anywhere] if merged else [vmem] * 5),
        scratch_shapes=[pltpu.VMEM(one.shape, one.dtype) for one in operands]
        + [
            pltpu.SemaphoreType.DMA((len(operands),)),
            pltpu.VMEM((micro, rows, width), BF),
            pltpu.SemaphoreType.DMA((1,)),
            pltpu.SemaphoreType.DMA((1,)),
            pltpu.VMEM((micro * rows, LANES), F32),
            pltpu.VMEM((micro * rows, LANES), F32),
            pltpu.VMEM((keys, rows), F32),
            pltpu.VMEM((KVH, 2, keys, LANES), BF),
            pltpu.VMEM((KVH, 2, LANES, keys), BF),
            pltpu.VMEM((KVH, 2, keys, LANES), BF),
            pltpu.VMEM((micro, HQ // 2, rows, LANES), BF),
            pltpu.VMEM((micro * rows, proj), BF),
            pltpu.VMEM((width, micro * rows), BF),
            pltpu.VMEM((KVH, 2, keys, LANES), F32),
            pltpu.VMEM((KVH, 2, keys, LANES), F32),
            pltpu.VMEM((micro, KVH, ctx, rows, LANES), BF),
            pltpu.VMEM((micro, KVH, ctx, rows, LANES), BF),
            pltpu.VMEM((1, proj + 2 * width), F32),
            pltpu.SemaphoreType.DMA((copies,)),
            pltpu.SemaphoreType.DMA((copies,)),
        ]
        + (Sums.scratch(n, high, wide, sizes) if merged else []),
        compiler_params=pltpu.CompilerParams(
            collective_id=3, has_side_effects=True, vmem_limit_bytes=VMEM_LIMIT
        ),
        name="attention_backward",
    )(order, lens, gain_attn, gain_mlp, freq, *operands, out_par, grads)
    if merged:
        return result
    dx, outputs, *parts, vec = result
    return dx, outputs, reduce_grads(n, ctx, grads, parts, vec)


def reduce_kernel(n, ctx, grads, *rest):
    parts, vec, fin, scratch = rest[:4], rest[4], rest[5], rest[6:]
    sums = Sums(n, ctx, grads, fin, scratch)
    enter(sums.around())
    sums.start()
    sums.vec[0] = vec[...]
    for k in range(PIECES, ALL_PIECES):
        sums.total[k] = jnp.zeros(sums.total.shape[1:], BF)
    sums.own_copy().wait()
    sizes = [part.shape[-1] for part in parts]
    last = (ALL_PIECES - PIECES - 1) * sums.total.shape[-1]
    folds = [
        Fold(sums, k, start)
        for k, start in enumerate((0, sizes[0], sizes[0] + sizes[1], last))
    ] + [FoldVectors(sums, last + sizes[3])]
    for fold, part in zip(folds, parts):
        fold.own[...] = part[...]
    for stage in ("over_core", "over_x", "over_y", "finish"):
        for fold in folds:
            getattr(fold, stage)()
    lax.fori_loop(0, sums.ticks, sums.step, 0)
    sums.close()


def reduce_grads(n, ctx, grads, parts, vec):
    high, wide = grads.shape[2:]
    vmem = pl.BlockSpec(memory_space=pltpu.VMEM)
    anywhere = pl.BlockSpec(memory_space=pl.ANY)
    return pl.pallas_call(
        functools.partial(reduce_kernel, n, ctx),
        out_shape=jax.ShapeDtypeStruct((ALL_PIECES, high, wide), BF),
        in_specs=[anywhere] + [vmem] * 5,
        out_specs=anywhere,
        scratch_shapes=Sums.scratch(n, high, wide, [part.shape[-1] for part in parts]),
        compiler_params=pltpu.CompilerParams(
            collective_id=4, has_side_effects=True, vmem_limit_bytes=VMEM_LIMIT
        ),
        name="reduce_grads",
    )(grads, *parts, vec)


def finish_kernel(
    size, dx, outputs, fin, g_gu, g_down, g_qkv, g_out, g_qk, g_v, g_attn, g_mlp, dx_out, outputs_out,
    turn, vecs, dx_in, outputs_in, sems,
):
    n, units, padded, proj, width = size
    replicas = n // TP
    high = width // n
    through = [(dx, dx_in, dx_out), (outputs, outputs_in, outputs_out)]
    coming = [
        pltpu.make_async_copy(src, buf, sems.at[k]) for k, (src, buf, _) in enumerate(through)
    ]
    going = [
        pltpu.make_async_copy(buf, dst, sems.at[2 + k]) for k, (_, buf, dst) in enumerate(through)
    ]
    for copy in coming:
        copy.start()
    f = lax.axis_index("fsdp")
    vec = fin.at[ALL_PIECES - 1]
    lane = proj - width
    rows = vec[0:VEC, lane : lane + LANES].astype(F32)
    vecs[...] = rows
    for first, ref in ((0, g_qk), (width + LANES, g_v), (proj, g_attn), (proj + width, g_mlp)):
        count = ref.shape[-1]
        at = first + f * count
        row = at // LANES
        pair = jnp.concatenate(
            [vecs[pl.ds(row, 1), :], vecs[pl.ds(row + 1, 1), :]], axis=1
        )
        pair = jnp.broadcast_to(pair, (8, 2 * LANES))
        ref[...] = pltpu.roll(pair, 2 * LANES - (at - row * LANES), 1)[0:1, :count]
    for a, b in zip(coming, going):
        a.wait()
        b.start()
    wide = fin.shape[-1]
    for half in range(2):
        for k in range(TP):
            whole = jnp.concatenate(
                [fin[4 * k + 2 * half + q].astype(F32) for q in range(2)], axis=1
            )
            for q in range(replicas):
                at = ((half * replicas + q) * TP + k) * units
                g_gu[:, at : at + units] = whole[:, q * padded : q * padded + units]
    each = wide // padded
    for k in range(n):
        at = (k % each) * padded
        turn[k * high : (k + 1) * high, :] = fin[4 * TP + k // each, :, at : at + padded].astype(F32)
    g_down[...] = turn[...].T[:units, :]
    ahead = ALL_PIECES - PIECES - 1
    whole = jnp.concatenate([fin[PIECES + k] for k in range(ahead)], axis=1)
    g_out[...] = whole[:, :width].astype(F32)
    g_qkv[:, :width] = whole[:, width : 2 * width].astype(F32)
    g_qkv[:, width:] = fin[ALL_PIECES - 1, :, : proj - width].astype(F32)
    for copy in going:
        copy.wait()


def finish_grads(n, dx, outputs, fin, units, padded, proj, width):
    high = width // n
    vmem = pl.BlockSpec(memory_space=pltpu.VMEM)
    anywhere = pl.BlockSpec(memory_space=pl.ANY)
    one = lambda count: jax.ShapeDtypeStruct((1, count), F32)
    return pl.pallas_call(
        functools.partial(finish_kernel, (n, units, padded, proj, width)),
        out_shape=(
            jax.ShapeDtypeStruct((high, 2 * n * units), F32),
            jax.ShapeDtypeStruct((units, width), F32),
            jax.ShapeDtypeStruct((high, proj), F32),
            jax.ShapeDtypeStruct((high, width), F32),
            one((width + LANES) // n),
            one(LANES // n),
            one(high),
            one(high),
            jax.ShapeDtypeStruct(dx.shape, dx.dtype),
            jax.ShapeDtypeStruct(outputs.shape, outputs.dtype),
        ),
        in_specs=[anywhere, anywhere, vmem],
        out_specs=[vmem] * 8 + [anywhere] * 2,
        scratch_shapes=[
            pltpu.VMEM((width, padded), F32),
            pltpu.VMEM((VEC, LANES), F32),
            pltpu.VMEM(dx.shape, dx.dtype),
            pltpu.VMEM(outputs.shape, outputs.dtype),
            pltpu.SemaphoreType.DMA((4,)),
        ],
        compiler_params=pltpu.CompilerParams(vmem_limit_bytes=VMEM_LIMIT),
        name="finish_grads",
    )(dx, outputs, fin)


def pad_to(v, axis, size):
    pads = [(0, 0)] * v.ndim
    pads[axis] = (0, size - v.shape[axis])
    return jnp.pad(v, pads)


def local(
    inputs, cotangent, lengths, order, w_qkv, b_qkv, w_out, norm_attn, norm_mlp, w_gate_up, w_down
):
    n = lax.axis_size("fsdp")
    ctx = lax.axis_size("ctx")
    replicas = n // TP
    x, gy = inputs[0], cotangent[0]
    micro, rows, width = x.shape
    high = w_gate_up.shape[0]
    units = w_down.shape[0]
    padded = -(-units // LANES) * LANES
    quarter = replicas * padded
    proj = w_qkv.shape[1]

    small = jnp.concatenate(
        [
            pad_to(b_qkv, 0, 2 * LANES).reshape(2, LANES),
            pad_to(norm_attn, 0, LANES)[None],
            pad_to(norm_mlp, 0, LANES)[None],
            jnp.zeros((12, LANES), BF),
        ]
    )
    half = HD // 2
    freqs = np.power(np.float32(ROPE_BASE), -(np.arange(half, dtype=np.float32) * (2.0 / HD)))
    freq = jnp.asarray(np.tile(freqs.astype(np.float32), (8, LANES // half)))
    if ctx <= 4 and high % 16 == 0 and units % 32 == 0:
        (
            h2, x2, qs, kv, lse, obt, wq_all, wo_all, gain_attn, gain_mlp, wgu_t, wd_t, gd_all,
        ) = gather_and_attend(
            n, ctx, order[0], lengths[0], x, w_qkv, w_out, small, w_gate_up, w_down, gy, freq,
            padded,
        )
        wq_all = wq_all.reshape(width, proj)
        wo_all = wo_all.reshape(width, width)
    else:
        wgu = w_gate_up.reshape(high, 2, replicas, TP, units)
        wgu = pad_to(wgu.transpose(3, 1, 0, 2, 4), 4, padded).reshape(TP, 2, high, quarter)
        wq_all, wo_all, sm_all, wgu_t, wd_t, gd_all = gather_weights(
            n, w_qkv, w_out, small, wgu, pad_to(w_down, 0, padded), gy
        )
        wq_all = wq_all.reshape(width, proj)
        wo_all = wo_all.reshape(width, width)
        bias = sm_all[:, :2].reshape(n, 2 * LANES)[:, : b_qkv.shape[0]].reshape(1, proj)
        gain_attn = sm_all[:, 2, :high].reshape(1, width).astype(F32)
        gain_mlp = sm_all[:, 3, :high].reshape(1, width).astype(F32)
        h2, x2, qs, kv, lse, obt = attention_forward(
            ctx, order[0], lengths[0], x, wq_all, wo_all, bias.astype(F32), gain_attn, gain_mlp,
            freq,
        )
    wgu_t = wgu_t.reshape(2, width, quarter)
    wd_t = wd_t.reshape(quarter, width)
    out, out_par, gh2, grads = mlp(n, h2, gd_all, wgu_t, wd_t)
    dx, outputs, fin = attention_backward(
        n, ctx, order[0], lengths[0], gh2, x2, gy, x, wq_all, wo_all, gain_attn, gain_mlp, freq,
        qs, kv, lse, obt, out, out_par, grads,
    )
    g_gu, g_down, g_qkv, g_out, g_qk, g_v, g_attn, g_mlp, dx, outputs = finish_grads(
        n, dx, outputs, fin, units, padded, proj, width
    )
    return (
        outputs[None],
        dx[None],
        g_qkv,
        g_qk[0],
        g_v[0],
        g_out,
        g_attn[0],
        g_mlp[0],
        g_gu,
        g_down,
    )


def solution(mesh):
    return jax.shard_map(
        local,
        mesh=mesh,
        in_specs=(
            P("fsdp", None, "ctx", None),
            P("fsdp", None, "ctx", None),
            P("fsdp", None, None),
            P("fsdp", None, None),
            P("fsdp", None),
            P("fsdp"),
            P("fsdp", None),
            P("fsdp"),
            P("fsdp"),
            P("fsdp", None),
            P("fsdp", None),
        ),
        out_specs=(
            P("fsdp", None, "ctx", None),
            P("fsdp", None, "ctx", None),
            P("fsdp", None),
            P("fsdp"),
            P("fsdp"),
            P("fsdp", None),
            P("fsdp"),
            P("fsdp"),
            P("fsdp", None),
            P("fsdp", None),
        ),
        check_vma=False,
    )
```

```python
import functools
import math

import jax
import jax.numpy as jnp
import numpy as np
from jax import lax
from jax.experimental import pallas as pl
from jax.experimental.pallas import tpu as pltpu
from jax.sharding import PartitionSpec as P

HQ = 14
KVH = 2
HD = 64
EPSILON = 1e-06
ROPE_BASE = 1000000.0
NEGATIVE = -1e30
TP = 4
LANES = 128
PIECES = 6 * TP
EXTRA = 6
ALL_PIECES = PIECES + EXTRA
RING = 6
HOP = 3
RATE = 4
FIRST = 2
PACE = 4
FIRST_PIECES = 3 * TP
EARLY = 4
AHEAD = 4
SLOTS = 8
VEC = 32
BF = jnp.bfloat16
F32 = jnp.float32
MESH = pl.DeviceIdType.MESH
VMEM_LIMIT = 62 * 1024 * 1024


def flip1(v):
    return v + 1 - 2 * (v % 2)


def flip2(v):
    return v + 2 - 4 * ((v // 2) % 2)


def dot(a, b):
    return jnp.dot(a, b, preferred_element_type=F32)


def dot_nt(a, b):
    return lax.dot_general(a, b, (((1,), (1,)), ((), ())), preferred_element_type=F32)


class Links:
    def __init__(self, send_sems, recv_sems):
        self.send_sems, self.recv_sems = send_sems, recv_sems
        self.started, self.gone = [], set()

    def put(self, src, dst, device):
        at = len(self.started)
        copy = pltpu.make_async_remote_copy(
            src_ref=src,
            dst_ref=dst,
            send_sem=self.send_sems.at[at],
            recv_sem=self.recv_sems.at[at],
            device_id=device,
            device_id_type=MESH,
        )
        copy.start()
        self.started.append((src, device))
        return at

    def arrive(self, at, slot):
        pltpu.make_async_remote_copy(
            src_ref=slot,
            dst_ref=slot,
            send_sem=self.send_sems.at[at],
            recv_sem=self.recv_sems.at[at],
            device_id=self.started[at][1],
            device_id_type=MESH,
        ).wait_recv()

    def sent(self, at):
        if at in self.gone:
            return
        self.gone.add(at)
        src, device = self.started[at]
        pltpu.make_async_remote_copy(
            src_ref=src,
            dst_ref=src,
            send_sem=self.send_sems.at[at],
            recv_sem=self.recv_sems.at[at],
            device_id=device,
            device_id_type=MESH,
        ).wait_send()

    def drain(self):
        for at in range(len(self.started)):
            self.sent(at)


class Staged:
    def __init__(self, pairs, sems):
        self.copies = [
            pltpu.make_async_copy(src, dst, sems.at[at]) for at, (src, dst) in enumerate(pairs)
        ]
        self.waited = 0
        for copy in self.copies:
            copy.start()

    def need(self, count):
        for copy in self.copies[self.waited : count]:
            copy.wait()
        self.waited = max(self.waited, count)


def enter(devices):
    barrier = pltpu.get_barrier_semaphore()
    for device in devices:
        pl.semaphore_signal(barrier, inc=1, device_id=device, device_id_type=MESH)
    pl.semaphore_wait(barrier, len(devices))


def gather_kernel(
    n, wq, wo, sm, wgu, wd, gd, wq_all, wo_all, sm_all, wgu_t, wd_t, gd_all, send, recv, here
):
    replicas = n // TP
    f, c = lax.axis_index("fsdp"), lax.axis_index("ctx")
    t, r = f % TP, f // TP
    sib, par, cross = (flip1(f), c), (flip2(f), c), (flip2(flip1(f)), c)
    peers = [((f + TP * j) % n, c) for j in range(1, replicas)]
    back = [(f - TP * j + n) % n for j in range(1, replicas)]
    rback = [(r - j + replicas) % replicas for j in range(1, replicas)]
    enter([sib, par, cross] + peers)
    links = Links(send, recv)
    local = []

    def keep(src, dst):
        copy = pltpu.make_async_copy(src, dst, here.at[len(local)])
        copy.start()
        local.append(copy)

    pending = []
    both = []
    for own, every in ((wq, wq_all), (wo, wo_all), (sm, sm_all)):
        ys = [links.put(own, every.at[f], peer) for peer in peers]
        x = links.put(own, every.at[f], par)
        s = links.put(own, every.at[f], sib)
        keep(own, every.at[f])
        both.append((every, ys, x, s))
    gd_x = links.put(gd, gd_all.at[:, t], par)
    gd_s = links.put(gd, gd_all.at[:, t], sib)
    keep(gd, gd_all.at[:, t])
    arrivals = []
    for half in range(2):
        for other, device in ((flip1(t), sib), (flip2(t), par), (flip2(flip1(t)), cross)):
            at = links.put(wgu.at[other, half], wgu_t.at[half, r, t], device)
            arrivals.append((at, half, other))
        keep(wgu.at[t, half], wgu_t.at[half, r, t])
        for j, peer in enumerate(peers):
            at = links.put(wgu.at[t, half], wgu_t.at[half, r, t], peer)
            pending.append((at, wgu_t.at[half, rback[j], t]))
    for j, peer in enumerate(peers):
        at = links.put(wd, wd_t.at[r], peer)
        pending.append((at, wd_t.at[rback[j]]))
    keep(wd, wd_t.at[r])
    later = []
    for every, ys, x, s in both:
        pending.append((s, every.at[flip1(f)]))
        for j, at in enumerate(ys):
            links.arrive(at, every.at[back[j]])
            at_x = links.put(every.at[back[j]], every.at[back[j]], par)
            later.append((every, at_x, flip2(back[j])))
            at_s = links.put(every.at[back[j]], every.at[back[j]], sib)
            pending.append((at_s, every.at[flip1(back[j])]))
        links.arrive(x, every.at[flip2(f)])
        at_s = links.put(every.at[flip2(f)], every.at[flip2(f)], sib)
        pending.append((at_s, every.at[flip2(flip1(f))]))
    for at, half, other in arrivals:
        links.arrive(at, wgu_t.at[half, r, other])
        for j, peer in enumerate(peers):
            at_y = links.put(wgu_t.at[half, r, other], wgu_t.at[half, r, other], peer)
            pending.append((at_y, wgu_t.at[half, rback[j], other]))
    for every, at, slot in later:
        links.arrive(at, every.at[slot])
        at_s = links.put(every.at[slot], every.at[slot], sib)
        pending.append((at_s, every.at[flip1(slot)]))
    links.arrive(gd_x, gd_all.at[:, flip2(t)])
    at_s = links.put(gd_all.at[:, flip2(t)], gd_all.at[:, flip2(t)], sib)
    pending.append((at_s, gd_all.at[:, flip2(flip1(t))]))
    pending.append((gd_s, gd_all.at[:, flip1(t)]))
    for at, slot in pending:
        links.arrive(at, slot)
    links.drain()
    for copy in local:
        copy.wait()


def gather_weights(n, wq, wo, sm, wgu, wd, gd):
    replicas = n // TP
    peers = replicas - 1
    copies = 3 * (4 * peers + 3) + 3 + 2 * (3 + 4 * peers) + peers
    anywhere = pl.BlockSpec(memory_space=pl.ANY)
    high, quarter = wgu.shape[2:]
    shapes = (
        jax.ShapeDtypeStruct((n,) + wq.shape, BF),
        jax.ShapeDtypeStruct((n,) + wo.shape, BF),
        jax.ShapeDtypeStruct((n,) + sm.shape, BF),
        jax.ShapeDtypeStruct((2, replicas, TP, high, quarter), BF),
        jax.ShapeDtypeStruct((replicas,) + wd.shape, BF),
        jax.ShapeDtypeStruct((gd.shape[0], TP) + gd.shape[1:], BF),
    )
    return pl.pallas_call(
        functools.partial(gather_kernel, n),
        out_shape=shapes,
        in_specs=[anywhere] * 6,
        out_specs=[anywhere] * 6,
        scratch_shapes=[
            pltpu.SemaphoreType.DMA((copies,)),
            pltpu.SemaphoreType.DMA((copies,)),
            pltpu.SemaphoreType.DMA((7,)),
        ],
        compiler_params=pltpu.CompilerParams(collective_id=0, has_side_effects=True),
        name="gather_weights",
    )(wq, wo, sm, wgu, wd, gd)


def begin_of(natural, lens, m, count):
    begin = jnp.zeros_like(natural)
    end = jnp.int32(0)
    for j in range(count):
        piece = lens[m, j]
        end = end + piece
        begin = begin + jnp.where(end <= natural, piece, 0)
    return begin


def fill_tables(m, rows, c, freq, order, lens, cos_ref, sin_ref):
    block = rows // 2
    lane = lax.broadcasted_iota(jnp.int32, (block, LANES), 1)
    low = (lane % HD) < (HD // 2)
    for b in range(2):
        natural = order[m, c * 2 + b] * block + lax.broadcasted_iota(
            jnp.int32, (block, LANES), 0
        )
        position = natural - begin_of(natural, lens, m, lens.shape[1])
        angle = position.astype(F32) * freq[0:1, :]
        at = m * rows + b * block
        cos_ref[at : at + block, :] = jnp.cos(angle)
        sine = jnp.sin(angle)
        sin_ref[at : at + block, :] = jnp.where(low, -sine, sine)


def swap_halves(u):
    lane = lax.broadcasted_iota(jnp.int32, u.shape, 1)
    low = (lane % HD) < (HD // 2)
    return jnp.where(low, pltpu.roll(u, LANES - HD // 2, 1), pltpu.roll(u, HD // 2, 1))


def fill_bias(m, rows, c, order, lens, bias_ref):
    block = rows // 2
    lane = lax.broadcasted_iota(jnp.int32, (1, rows), 1)
    query = jnp.where(
        lane < block,
        order[m, c * 2] * block + lane,
        order[m, c * 2 + 1] * block + lane - block,
    )
    begin = begin_of(query, lens, m, lens.shape[1])

    def body(k, carry):
        key = order[m, k] * block + lax.broadcasted_iota(jnp.int32, (block, rows), 0)
        allowed = (key <= query) & (key >= begin)
        at = pl.multiple_of(k * block, block)
        bias_ref[pl.ds(at, block), :] = jnp.where(allowed, 0.0, NEGATIVE)
        return carry

    lax.fori_loop(0, order.shape[1], body, 0)


def fill_heads(whole, var_ref):
    rolled = pltpu.roll(whole, HD, 1)
    low = lax.broadcasted_iota(jnp.int32, whole.shape, 1) < HD
    var_ref[0, 0] = jnp.where(low, whole, 0.0).astype(BF)
    var_ref[0, 1] = jnp.where(low, 0.0, rolled).astype(BF)
    var_ref[1, 0] = jnp.where(low, rolled, 0.0).astype(BF)
    var_ref[1, 1] = jnp.where(low, 0.0, whole).astype(BF)


def fill_heads_turned(whole, var_ref):
    turned = whole.T
    rolled = jnp.concatenate([turned[HD:], turned[:HD]], axis=0)
    low = lax.broadcasted_iota(jnp.int32, turned.shape, 0) < HD
    var_ref[0, 0] = jnp.where(low, turned, 0.0).astype(BF)
    var_ref[0, 1] = jnp.where(low, 0.0, rolled).astype(BF)
    var_ref[1, 0] = jnp.where(low, rolled, 0.0).astype(BF)
    var_ref[1, 1] = jnp.where(low, 0.0, turned).astype(BF)


def inverse_norm(v):
    return lax.rsqrt(jnp.mean(v * v, axis=1, keepdims=True) + EPSILON)


class Forward:
    def __init__(self, size, order, lens, x, freq, outs, scratch):
        self.micro, self.rows, self.ctx = size
        self.order, self.lens, self.x, self.freq = order, lens, x, freq
        self.h2, self.x2, self.qs, self.kv, self.lse, self.obt = outs
        (
            self.cos_ref, self.sin_ref, self.bias_ref, self.kvar, self.vvar, self.ob, self.h1,
            self.land, send, recv, self.out_sem,
        ) = scratch
        f, c = lax.axis_index("fsdp"), lax.axis_index("ctx")
        self.c = c
        self.others = [(f, (c + j) % self.ctx) for j in range(1, self.ctx)]
        self.back = [(c - j + self.ctx) % self.ctx for j in range(1, self.ctx)]
        self.links = Links(send, recv)
        self.arrivals, self.out_copies = [], []

    @staticmethod
    def scratch(micro, rows, ctx, width):
        keys = rows * ctx
        copies = micro * (ctx - 1)
        return [
            pltpu.VMEM((micro * rows, LANES), F32),
            pltpu.VMEM((micro * rows, LANES), F32),
            pltpu.VMEM((keys, rows), F32),
            pltpu.VMEM((KVH, 2, keys, LANES), BF),
            pltpu.VMEM((KVH, 2, LANES, keys), BF),
            pltpu.VMEM((micro, rows, HQ * HD), BF),
            pltpu.VMEM((micro, rows, width), BF),
            pltpu.VMEM((micro, ctx, rows, 2 * LANES), BF),
            pltpu.SemaphoreType.DMA((copies,)),
            pltpu.SemaphoreType.DMA((copies,)),
            pltpu.SemaphoreType.DMA((micro,)),
        ]

    @staticmethod
    def shapes(micro, rows, ctx, width):
        return (
            jax.ShapeDtypeStruct((micro, rows, width), BF),
            jax.ShapeDtypeStruct((micro, rows, width), F32),
            jax.ShapeDtypeStruct((micro, HQ // 2, rows, LANES), BF),
            jax.ShapeDtypeStruct((micro, ctx, rows, 2 * LANES), BF),
            jax.ShapeDtypeStruct((micro, HQ, rows), F32),
            jax.ShapeDtypeStruct((micro, HQ * HD, rows), BF),
        )

    @staticmethod
    def specs():
        vmem = pl.BlockSpec(memory_space=pltpu.VMEM)
        return [vmem, vmem, vmem, pl.BlockSpec(memory_space=pl.ANY), vmem, vmem]

    def tables(self):
        for m in range(self.micro):
            fill_tables(
                m, self.rows, self.c, self.freq, self.order, self.lens, self.cos_ref, self.sin_ref
            )

    def norms(self, gain_attn):
        for m in range(self.micro):
            stream = self.x[m].astype(F32)
            self.h1[m] = (stream * inverse_norm(stream) * gain_attn).astype(BF)

    def project(self, m, wq, bias_qkv):
        rows, width = self.rows, HQ * HD
        project = dot(self.h1[m], wq) + bias_qkv
        cosine = self.cos_ref[m * rows : (m + 1) * rows, :]
        sine = self.sin_ref[m * rows : (m + 1) * rows, :]
        keys = project[:, width : width + LANES]
        keys = keys * cosine + swap_halves(keys) * sine
        self.land[m, self.c, :, :LANES] = keys.astype(BF)
        self.land[m, self.c, :, LANES:] = project[:, width + LANES :].astype(BF)
        own = self.land.at[m, self.c]
        self.arrivals.append([self.links.put(own, own, other) for other in self.others])
        for p in range(HQ // 2):
            query = project[:, p * LANES : (p + 1) * LANES]
            query = query * cosine + swap_halves(query) * sine
            self.qs[m, p] = (query.astype(BF).astype(F32) * (1.0 / math.sqrt(HD))).astype(BF)

    def attend(self, m, tick):
        rows, ctx, group, pairs = self.rows, self.ctx, HQ // KVH, HQ // 2
        fill_bias(m, rows, self.c, self.order, self.lens, self.bias_ref)
        for at, source in zip(self.arrivals[m], self.back):
            self.links.arrive(at, self.land.at[m, source])
        copy = pltpu.make_async_copy(self.land.at[m], self.kv.at[m], self.out_sem.at[m])
        copy.start()
        self.out_copies.append(copy)
        both = self.land[m].reshape(ctx * rows, 2 * LANES).astype(F32)
        fill_heads(both[:, :LANES], self.kvar)
        fill_heads_turned(both[:, LANES:], self.vvar)

        def pair(p, carry):
            query = self.qs[m, p]
            mixed = jnp.zeros((LANES, rows), F32)
            for parity in range(2):
                head = 2 * p + parity
                g = head // group
                scores = dot_nt(self.kvar[g, parity], query) + self.bias_ref[...]
                top = jnp.max(scores, axis=0, keepdims=True)
                probs = jnp.exp(scores - top)
                total = jnp.sum(probs, axis=0, keepdims=True)
                mixed = mixed + dot(self.vvar[g, parity], probs.astype(BF)) / total
                self.lse[m, pl.ds(head, 1), :] = top + jnp.log(total)
            at = pl.multiple_of(p * LANES, LANES)
            self.obt[m, pl.ds(at, LANES), :] = mixed.astype(BF)
            self.ob[m, :, pl.ds(at, LANES)] = mixed.T.astype(BF)
            tick(p)
            return carry

        lax.fori_loop(0, pairs, pair, 0)

    def close(self, m, wo, gain_mlp):
        middle = self.x[m].astype(F32) + dot(self.ob[m], wo)
        self.x2[m] = middle
        self.h2[m] = (middle * inverse_norm(middle) * gain_mlp).astype(BF)

    def drain(self):
        self.links.drain()
        for copy in self.out_copies:
            copy.wait()


def forward_kernel(size, order, lens, x, wq, wo, bias_qkv, gain_attn, gain_mlp, freq, *rest):
    work = Forward(size, order, lens, x, freq, rest[:6], rest[6:])
    enter(work.others)
    work.tables()
    work.norms(gain_attn[...])
    for m in range(work.micro):
        work.project(m, wq[...], bias_qkv[...])
    for m in range(work.micro):
        work.attend(m, lambda p: None)
        work.close(m, wo[...], gain_mlp[...])
    work.drain()


def attention_forward(ctx, order, lens, x, wq, wo, bias_qkv, gain_attn, gain_mlp, freq):
    micro, rows, width = x.shape
    vmem = pl.BlockSpec(memory_space=pltpu.VMEM)
    smem = pl.BlockSpec(memory_space=pltpu.SMEM)
    return pl.pallas_call(
        functools.partial(forward_kernel, (micro, rows, ctx)),
        out_shape=Forward.shapes(micro, rows, ctx, width),
        in_specs=[smem, smem] + [vmem] * 7,
        out_specs=Forward.specs(),
        scratch_shapes=Forward.scratch(micro, rows, ctx, width),
        compiler_params=pltpu.CompilerParams(
            collective_id=1, has_side_effects=True, vmem_limit_bytes=VMEM_LIMIT
        ),
        name="attention_forward",
    )(order, lens, x, wq, wo, bias_qkv, gain_attn, gain_mlp, freq)


def front_kernel(
    size, order, lens, x, wq, wo, sm, wgu_raw, wd, gy, freq,
    h2, x2, qs, kv, lse, obt, wq_out, wo_out, gain_attn, gain_mlp, wgu_t, wd_t, gd_all,
    wq_all, wo_all, sm_all, pieces, bias_qkv, zeros, wgu_in, wd_in, gy_in, staged_sems,
    send, recv, ys, yr, zs, zr, here, *scratch
):
    n, micro, rows, ctx = size
    replicas = n // TP
    peers_n = replicas - 1
    high = wgu_raw.shape[0]
    staged = Staged([(wgu_raw, wgu_in), (wd, wd_in), (gy, gy_in)], staged_sems)
    units, width = wd.shape
    padded = wd_t.shape[1]
    proj = wq.shape[1]
    work = Forward((micro, rows, ctx), order, lens, x, freq, (h2, x2, qs, kv, lse, obt), scratch)
    f, c = lax.axis_index("fsdp"), lax.axis_index("ctx")
    t, r = f % TP, f // TP
    even = c % 2 == 0
    odd = c % 2 == 1
    sib, par, cross = (flip1(f), c), (flip2(f), c), (flip2(flip1(f)), c)
    t_sib, t_par, t_cross = flip1(t), flip2(t), flip2(flip1(t))
    twin = (f, flip1(c))
    peers = [((f + TP * j) % n, c) for j in range(1, replicas)]
    back = [(f - TP * j + n) % n for j in range(1, replicas)]
    rback = [(r - j + replicas) % replicas for j in range(1, replicas)]
    enter([sib, par, cross] + peers + work.others)
    links = Links(send, recv)
    local = []

    def keep(src, dst):
        copy = pltpu.make_async_copy(src, dst, here.at[len(local)])
        copy.start()
        local.append(copy)
        return copy

    class Spread:
        def __init__(self, own, every):
            self.every = every
            self.ys = [links.put(own, every.at[f], peer) for peer in peers]
            self.mine = own
            self.pending = [(links.put(own, every.at[f], sib), every.at[flip1(f)])]
            self.own = keep(own, every.at[f])
            self.later = []
            self.slots = [
                tuple(every.at[k] for k in (p, flip1(p), flip2(p), flip1(flip2(p)))) for p in back
            ]
            self.across = (every.at[flip2(f)], every.at[flip1(flip2(f))])

        def start_x(self):
            self.x = links.put(self.mine, self.every.at[f], par)

        def on_y(self):
            for at, (p, p_sib, p_par, p_cross) in zip(self.ys, self.slots):
                links.arrive(at, p)
                self.later.append((links.put(p, p, par), p_par, p_cross))
                self.pending.append((links.put(p, p, sib), p_sib))

        def on_x(self):
            p, p_cross = self.across
            links.arrive(self.x, p)
            self.pending.append((links.put(p, p, sib), p_cross))

        def on_late(self):
            for at, p, p_cross in self.later:
                links.arrive(at, p)
                self.pending.append((links.put(p, p, sib), p_cross))

        def done(self):
            for at, p in self.pending:
                links.arrive(at, p)
            self.own.wait()

    first = [Spread(wq, wq_all), Spread(sm, sm_all)]
    for one in first:
        one.start_x()
    second = Spread(wo, wo_all)
    pieces[...] = jnp.zeros_like(pieces)
    zeros[...] = jnp.zeros_like(zeros)
    staged.need(3)
    for k in range(TP):
        for q in range(2 * replicas):
            at = (q * TP + k) * units
            to = (q % replicas) * padded
            pieces[k, q // replicas, :, to : to + units] = wgu_in[:, at : at + units]
    gu_s = [links.put(pieces.at[t_sib, k], wgu_t.at[k, r, t], sib) for k in range(2)]
    half = units // 2
    last = wd_in.at[pl.ds(half, half)], wd_t.at[r, pl.ds(half, half)]
    head = wd_in.at[pl.ds(0, half)], wd_t.at[r, pl.ds(0, half)]

    def y_copy(at, j, src, dst):
        at = at * peers_n + j
        return pltpu.make_async_remote_copy(
            src_ref=src, dst_ref=dst, send_sem=ys.at[at], recv_sem=yr.at[at],
            device_id=peers[j], device_id_type=MESH,
        )

    def z_copy(at, j, src):
        at = at * peers_n + j
        return pltpu.make_async_remote_copy(
            src_ref=src, dst_ref=src, send_sem=zs.at[at], recv_sem=zr.at[at],
            device_id=twin, device_id_type=MESH,
        )

    def down_put(at, pair):
        for j in range(peers_n):
            y_copy(at, j, *pair).start()

    kinds = ((t, t_sib), (t_par, t_cross))

    def piece(parity, item, replica):
        return wgu_t.at[item % 2, replica, kinds[parity][item // 2]]

    def y_put(parity, item):
        for j in range(peers_n):
            mine = piece(parity, item, r)
            src = pieces.at[t, item] if (parity, item // 2) == (0, 0) else mine
            y_copy(item, j, src, mine).start()

    def z_put(parity, item):
        for j in range(peers_n):
            got = piece(parity, item, rback[j])
            y_copy(item, j, got, got).wait_recv()
            z_copy(item, j, got).start()

    @pl.when(even)
    def _():
        y_put(0, 0)
        y_put(0, 1)

    @pl.when(odd)
    def _():
        down_put(4, head)

    for q in range(replicas):
        keep(zeros, wd_t.at[q, pl.ds(units, padded - units)])
    keep(wd_in, wd_t.at[r, pl.ds(0, units)])
    for k in range(2):
        keep(pieces.at[t, k], wgu_t.at[k, r, t])
    keep(gy_in, gd_all.at[:, t])
    gd_s = links.put(gy_in, gd_all.at[:, t], sib)
    for one in first:
        one.on_y()
    gu_x = [links.put(pieces.at[t_par, k], wgu_t.at[k, r, t], par) for k in range(2)]
    gu_c = [links.put(pieces.at[t_cross, k], wgu_t.at[k, r, t], cross) for k in range(2)]
    second.start_x()
    work.tables()
    for one in first:
        one.on_x()
    for k in range(2):
        links.arrive(gu_s[k], wgu_t.at[k, r, t_sib])

    @pl.when(even)
    def _():
        y_put(0, 2)
        y_put(0, 3)
        down_put(4, head)
        down_put(5, last)

    for one in first:
        one.on_late()
    for one in first:
        one.done()
    keep(wq_all, wq_out)
    share = proj // n
    for k in range(n):
        small = sm_all[k].astype(F32)
        bias_qkv[:, k * share : k * share + min(share, LANES)] = small[0:1, : min(share, LANES)]
        if share > LANES:
            bias_qkv[:, k * share + LANES : (k + 1) * share] = small[1:2, : share - LANES]
        gain_attn[:, k * high : (k + 1) * high] = small[2:3, :high]
        gain_mlp[:, k * high : (k + 1) * high] = small[3:4, :high]
    work.norms(gain_attn[...])
    for m in range(micro):
        work.project(m, wq_all[...].reshape(width, proj), bias_qkv[...])
    second.on_y()
    gd_x = [links.put(gy_in.at[m], gd_all.at[m, t], par) for m in range(micro)]
    gd_par = [gd_all.at[m, t_par] for m in range(micro)]
    gd_c = []

    def x_piece(k):
        links.arrive(gu_x[k], wgu_t.at[k, r, t_par])
        pl.when(odd)(lambda: y_put(1, k))

    def c_piece(k):
        links.arrive(gu_c[k], wgu_t.at[k, r, t_cross])

        @pl.when(odd)
        def _():
            y_put(1, 2 + k)
            if k == 1:
                down_put(5, last)

    def on_gd():
        links.arrive(gd_x[0], gd_par[0])
        gd_c.append(links.put(gd_par[0], gd_par[0], sib))

    x_piece(0)
    x_piece(1)
    steps = {
        (0, 0): [lambda: pl.when(even)(lambda: z_put(0, 0))],
        (0, 1): [lambda: pl.when(even)(lambda: z_put(0, 1)), lambda: c_piece(0)],
        (0, 2): [lambda: pl.when(even)(lambda: z_put(0, 2))],
        (0, 3): [lambda: c_piece(1), lambda: pl.when(odd)(lambda: z_put(1, 0))],
        (0, 4): [lambda: pl.when(even)(lambda: z_put(0, 3))],
        (0, 6): [lambda: pl.when(odd)(lambda: z_put(1, 1))],
        (1, 1): [lambda: pl.when(odd)(lambda: z_put(1, 2)), second.on_x],
        (1, 3): [lambda: pl.when(odd)(lambda: z_put(1, 3)), second.on_late],
        (1, 6): [on_gd],
    }
    for m in range(micro):

        def tick(p, m=m):
            for (at_m, at_p), todo in steps.items():
                if at_m == m:

                    @pl.when(p == at_p)
                    def _(todo=todo):
                        for one in todo:
                            one()

        work.attend(m, tick)
    second.done()
    keep(wo_all, wo_out)
    for m in range(micro):
        work.close(m, wo_all[...].reshape(width, width), gain_mlp[...])
    for m in range(1, micro):
        links.arrive(gd_x[m], gd_par[m])
        gd_c.append(links.put(gd_par[m], gd_par[m], sib))
    links.arrive(gd_s, gd_all.at[:, t_sib])
    for m in range(micro):
        links.arrive(gd_c[m], gd_all.at[m, t_cross])
    for parity in range(2):

        @pl.when(even if parity == 0 else odd)
        def _(parity=parity):
            for j in range(peers_n):
                for item in range(4):
                    z_copy(item, j, piece(1 - parity, item, rback[j])).wait_recv()
                    mine = piece(parity, item, r)
                    z_copy(item, j, mine).wait_send()
                    y_copy(item, j, mine, mine).wait_send()

    for j in range(peers_n):
        for at, pair in ((4, head), (5, last)):
            y_copy(at, j, *pair).wait_send()
            first_row = 0 if at == 4 else half
            y_copy(at, j, pair[0], wd_t.at[rback[j], pl.ds(first_row, half)]).wait_recv()
    for copy in local:
        if copy is not second.own and all(copy is not one.own for one in first):
            copy.wait()
    work.drain()
    links.drain()


def gather_and_attend(n, ctx, order, lens, x, wq, wo, sm, wgu, wd, gy, freq, padded):
    micro, rows, width = x.shape
    replicas = n // TP
    peers = replicas - 1
    high, proj = wq.shape
    quarter = replicas * padded
    vmem = pl.BlockSpec(memory_space=pltpu.VMEM)
    smem = pl.BlockSpec(memory_space=pltpu.SMEM)
    anywhere = pl.BlockSpec(memory_space=pl.ANY)
    sems = pltpu.SemaphoreType.DMA
    copies = 3 * (4 * peers + 3) + 6 + 1 + 2 * micro
    gain = jax.ShapeDtypeStruct((1, width), F32)
    return pl.pallas_call(
        functools.partial(front_kernel, (n, micro, rows, ctx)),
        out_shape=Forward.shapes(micro, rows, ctx, width) + (
            jax.ShapeDtypeStruct((n, high, proj), BF),
            jax.ShapeDtypeStruct((n, high, width), BF),
            gain,
            gain,
            jax.ShapeDtypeStruct((2, replicas, TP, high, quarter), BF),
            jax.ShapeDtypeStruct((replicas, padded, width), BF),
            jax.ShapeDtypeStruct((micro, TP, rows, width), BF),
        ),
        in_specs=[smem, smem, vmem] + [anywhere] * 6 + [vmem],
        out_specs=Forward.specs() + [anywhere, anywhere, vmem, vmem] + [anywhere] * 3,
        scratch_shapes=[
            pltpu.VMEM((n, high, proj), BF),
            pltpu.VMEM((n, high, width), BF),
            pltpu.VMEM((n,) + sm.shape, BF),
            pltpu.VMEM((TP, 2, high, quarter), BF),
            pltpu.VMEM((1, proj), F32),
            pltpu.VMEM((padded - wd.shape[0], width), BF),
            pltpu.VMEM(wgu.shape, BF),
            pltpu.VMEM(wd.shape, BF),
            pltpu.VMEM(gy.shape, BF),
            sems((3,)),
            sems((copies,)), sems((copies,)),
            sems((6 * peers,)), sems((6 * peers,)), sems((4 * peers,)), sems((4 * peers,)),
            sems((9 + replicas,)),
        ] + Forward.scratch(micro, rows, ctx, width),
        compiler_params=pltpu.CompilerParams(
            collective_id=5, has_side_effects=True, vmem_limit_bytes=VMEM_LIMIT
        ),
        name="gather_and_attend",
    )(order, lens, x, wq, wo, sm, wgu, wd, gy, freq)


def mlp_kernel(
    size, ctx, h2, gd_hbm, wgu_hbm, wd_hbm,
    out, out_par, gh2, grads, *rest
):
    micro, rows, width, replicas, padded = size
    n = replicas * TP
    columns = replicas * LANES
    tiles = padded // LANES
    split = ctx is not None
    if split:
        kept, fin_first, rest = rest[0], rest[1], rest[2:]
    (
        gd, wgu, wd, hbuf, turned_h, turned_g, acc_out, acc_gh, dgate, dup, ddown,
        sib_out, sib_in, par_out, par_in, keep_sum, stage, send, recv, out_sem, staged_sems,
    ), rest = rest[:21], rest[21:]
    both = 2 * rows
    f, c = lax.axis_index("fsdp"), lax.axis_index("ctx")
    t = f % TP
    core = t % 2
    mine, theirs = t - core, flip2(t) - core
    t_sib, t_par, t_cross = flip1(t), flip2(t), flip2(flip1(t))
    sib, par = (flip1(f), c), (flip2(f), c)
    staged = Staged(
        [(h2.at[m], hbuf.at[m, t]) for m in range(micro)]
        + [(gd_hbm.at[0], gd.at[0]), (wgu_hbm, wgu), (wd_hbm, wd)]
        + [(gd_hbm.at[m], gd.at[m]) for m in range(1, micro)],
        staged_sems,
    )
    if split:
        acc_stage, grads_first, kept_sem = rest[:3]
        first_sums = Sums(n, ctx, grads_first, fin_first, rest[3:], 2, 0, 2)
        enter(first_sums.around())
    else:
        enter([sib, par])
    links = Links(send, recv)
    from_sib, from_par, from_cross = [], [], [None] * micro
    for m in range(micro):
        from_par.append(links.put(h2.at[m], hbuf.at[m, t], par))
        from_sib.append(links.put(h2.at[m], hbuf.at[m, t], sib))

    def grad_of(m, side):
        return gd[m, pl.ds(side, 2)].reshape(both, width)

    def forward_on(m):
        buf = hbuf.at[m, t_par]
        links.arrive(from_par[m], buf)
        from_cross[m] = links.put(buf, buf, sib)

    def chunk(m, side, first, base, j):
        at = [pl.multiple_of(q * padded + j * LANES, LANES) for q in range(replicas)]
        to = pl.ds(pl.multiple_of((j - base) * columns, columns), columns)
        hidden_in = hbuf[m, pl.ds(side, 2)].reshape(both, width)
        grad_in = grad_of(m, side)
        w_gate = jnp.concatenate([wgu[0, :, pl.ds(k, LANES)] for k in at], axis=1)
        w_up = jnp.concatenate([wgu[1, :, pl.ds(k, LANES)] for k in at], axis=1)
        w_down = jnp.concatenate([wd[pl.ds(k, LANES), :] for k in at], axis=0)
        gate = dot(hidden_in, w_gate)
        up = dot(hidden_in, w_up)
        gm = dot_nt(grad_in, w_down)
        sg = 0.5 * jnp.tanh(0.5 * gate) + 0.5
        silu = gate * sg
        mb = (silu * up).astype(BF)
        ggate = (gm * up * (sg + silu * (1.0 - sg))).astype(BF)
        gup = (gm * silu).astype(BF)
        acc_out[...] += dot(mb, w_down)
        acc_gh[...] += dot_nt(ggate, w_gate) + dot_nt(gup, w_up)
        if first:
            dgate[:, to] = dot(turned_h[...], ggate)
            dup[:, to] = dot(turned_h[...], gup)
            ddown[:, to] = dot(turned_g[...], mb)
        else:
            dgate[:, to] += dot(turned_h[...], ggate)
            dup[:, to] += dot(turned_h[...], gup)
            ddown[:, to] += dot(turned_g[...], mb)

    def share(step):
        here = pl.multiple_of(core * rows, rows)
        there = pl.multiple_of(rows - core * rows, rows)
        ats = []
        for k, acc in enumerate((acc_gh, acc_out)):
            if step >= 2:
                links.sent(shared[step - 2][k])
            sib_out[step % 2, k] = acc[pl.ds(there, rows), :].astype(BF)
            ats.append(links.put(sib_out.at[step % 2, k], sib_in.at[step, k], sib))
            keep_sum[k] = acc[pl.ds(here, rows), :]
        shared.append(ats)

    shared = []
    passed = [None] * micro

    def settle(step, m, own):
        for k, at in enumerate(shared[step]):
            links.arrive(at, sib_in.at[step, k])
            whole = keep_sum[k] + sib_in[step, k].astype(F32)
            if own:
                (gh2, out)[k][m] = whole
            else:
                (par_out, out_par)[k][m] = whole.astype(BF)
        if not own:
            passed[m] = links.put(par_out.at[m], par_in.at[m], par)

    def piece_of(per, base, count, replica, k):
        high = width // n
        wide = columns * count * 2 // per
        if k < per * TP:
            at = (replica * TP + k // per) * high
            half, lane = divmod(k % per, per // 2)
            return (dgate, dup)[half][at : at + high, lane * wide : (lane + 1) * wide].astype(BF)
        blocks = 2 * replicas // per
        parts = []
        for q in range(blocks):
            at = ((k - per * TP) * blocks + q) * high
            for j in range(count):
                lane = (j * replicas + replica) * LANES
                parts.append(ddown[at : at + high, lane : lane + LANES])
        return jnp.concatenate(parts, axis=1).astype(BF)

    own_steps = [(m, True) for m in range(micro)]
    other_steps = [(m, False) for m in range(micro)]
    if split:
        passes = [(0, FIRST, own_steps + other_steps), (FIRST, tiles, other_steps + own_steps)]
    else:
        passes = [(0, tiles, own_steps[:1] + other_steps + own_steps[1:])]
    seen = set()
    writing = None
    ticks = 0
    for number, (base, end, plan) in enumerate(passes):
        final = number == len(passes) - 1
        second = split and final
        for step, (m, own) in enumerate(plan):
            if (m, own) not in seen:
                seen.add((m, own))
                if own:
                    links.arrive(from_sib[m], hbuf.at[m, t_sib])
                else:
                    if from_cross[m] is None:
                        forward_on(m)
                    links.arrive(from_cross[m], hbuf.at[m, t_cross])
            staged.need((micro + 3) if m == 0 else len(staged.copies))
            side = mine if own else theirs
            turned_h[...] = hbuf[m, pl.ds(side, 2)].reshape(both, width).T
            turned_g[...] = grad_of(m, side).T
            if second:
                index = passes[0][2].index((m, own))
                pltpu.make_async_copy(kept.at[index], acc_stage, kept_sem.at[1]).wait()
                acc_gh[...] = acc_stage[0].astype(F32)
                acc_out[...] = acc_stage[1].astype(F32)
                if step + 1 < len(plan):
                    index = passes[0][2].index(plan[step + 1])
                    pltpu.make_async_copy(kept.at[index], acc_stage, kept_sem.at[1]).start()
            else:
                acc_out[...] = jnp.zeros_like(acc_out)
                acc_gh[...] = jnp.zeros_like(acc_gh)

            def body(j, carry, m=m, side=side, step=step, second=second):
                chunk(m, side, step == 0, base, j)
                if second:
                    i = step * (end - base) + j - base
                    lax.fori_loop(
                        jnp.minimum(PACE * i // 4, first_sums.ticks),
                        jnp.minimum(PACE * (i + 1) // 4, first_sums.ticks),
                        first_sums.step, 0,
                    )
                return carry

            lax.fori_loop(base, end - 1, body, 0)
            if final and step > 0:
                settle(step - 1, *plan[step - 1])
            upcoming = plan[step + 1 : step + 2]
            if upcoming and not upcoming[0][1] and from_cross[upcoming[0][0]] is None:
                forward_on(upcoming[0][0])
            lax.fori_loop(end - 1, end, body, 0)
            if final:
                share(step)
            else:
                if writing is not None:
                    writing.wait()
                acc_stage[0] = acc_gh[...].astype(BF)
                acc_stage[1] = acc_out[...].astype(BF)
                writing = pltpu.make_async_copy(acc_stage, kept.at[step], kept_sem.at[0])
                writing.start()
        if not final:
            for k in range(FIRST_PIECES):
                for replica in range(replicas):
                    grads_first[replica, k] = piece_of(2, base, end - base, replica, k)
            first_sums.start()
            writing.wait()
            index = plan.index(passes[1][2][0])
            pltpu.make_async_copy(kept.at[index], acc_stage, kept_sem.at[1]).start()
            first_sums.own_copy().wait()
    ticks = min(PACE * len(plan) * (end - base) // 4, first_sums.ticks) if split else 0
    copies = []
    for k in range(PIECES):
        if split and k % 4 == 0 and ticks < first_sums.ticks:
            first_sums.tick(jnp.int32(ticks))
            ticks += 1
        for replica in range(replicas):
            slot = len(copies) % SLOTS
            if len(copies) >= SLOTS:
                copies[-SLOTS].wait()
            stage[slot] = piece_of(4, base, end - base, replica, k)
            copy = pltpu.make_async_copy(stage.at[slot], grads.at[replica, k], out_sem.at[slot])
            copy.start()
            copies.append(copy)
    settle(len(plan) - 1, *plan[-1])
    for m in range(micro):
        links.arrive(passed[m], par_in.at[m])
        gh2[m] = gh2[m] + par_in[m].astype(F32)
    if split:
        lax.fori_loop(ticks, max(ticks, first_sums.ticks), first_sums.step, 0)
        first_sums.close()
    for copy in copies[-SLOTS:]:
        copy.wait()
    links.drain()


def mlp(n, ctx, h2, gd, wgu, wd):
    micro, rows, width = h2.shape
    replicas = n // TP
    padded = wd.shape[0] // replicas
    high = width // n
    columns = replicas * LANES
    tiles = padded // LANES
    split = ctx <= 4 and tiles > FIRST
    count = tiles - FIRST if split else tiles
    vmem = pl.BlockSpec(memory_space=pltpu.VMEM)
    anywhere = pl.BlockSpec(memory_space=pl.ANY)
    sems = pltpu.SemaphoreType.DMA
    steps = 2 * micro
    copies = micro * 3 + steps * 2 + micro
    whole = jax.ShapeDtypeStruct((micro, rows, width), F32)
    most = columns * max(FIRST, count)
    out_shape = [
        whole,
        jax.ShapeDtypeStruct((micro, rows, width), BF),
        whole,
        jax.ShapeDtypeStruct((replicas, PIECES, high, columns * count // 2), BF),
    ]
    extra = []
    if split:
        out_shape += [
            jax.ShapeDtypeStruct((steps, 2, 2 * rows, width), BF),
            jax.ShapeDtypeStruct((FIRST_PIECES, high, columns * FIRST), BF),
        ]
        extra = [
            pltpu.VMEM((2, 2 * rows, width), BF),
            pltpu.VMEM((replicas, FIRST_PIECES, high, columns * FIRST), BF),
            sems((2,)),
        ] + Sums.scratch(n, high, columns * FIRST, (), 2, 0)
    result = pl.pallas_call(
        functools.partial(
            mlp_kernel, (micro, rows, width, replicas, padded), ctx if split else None
        ),
        out_shape=out_shape,
        in_specs=[anywhere] * 4,
        out_specs=[vmem, vmem, vmem] + [anywhere] * (len(out_shape) - 3),
        scratch_shapes=[
            pltpu.VMEM(gd.shape, BF),
            pltpu.VMEM(wgu.shape, BF),
            pltpu.VMEM(wd.shape, BF),
            pltpu.VMEM((micro, TP, rows, width), BF),
            pltpu.VMEM((width, 2 * rows), BF),
            pltpu.VMEM((width, 2 * rows), BF),
            pltpu.VMEM((2 * rows, width), F32),
            pltpu.VMEM((2 * rows, width), F32),
            pltpu.VMEM((width, most), F32),
            pltpu.VMEM((width, most), F32),
            pltpu.VMEM((width, most), F32),
            pltpu.VMEM((2, 2, rows, width), BF),
            pltpu.VMEM((steps, 2, rows, width), BF),
            pltpu.VMEM((micro, rows, width), BF),
            pltpu.VMEM((micro, rows, width), BF),
            pltpu.VMEM((2, rows, width), F32),
            pltpu.VMEM((SLOTS, high, columns * count // 2), BF),
            sems((copies,)),
            sems((copies,)),
            sems((SLOTS,)),
            sems((2 * micro + 2,)),
        ] + extra,
        compiler_params=pltpu.CompilerParams(
            collective_id=2, has_side_effects=True, vmem_limit_bytes=VMEM_LIMIT
        ),
        name="mlp",
    )(h2, gd, wgu, wd)
    out, out_par, gh2, grads = result[:4]
    fins = [(result[5], 2, FIRST)] if split else []
    return out, out_par, gh2, grads, fins, count


def add_into(dst, a, b):
    dst[...] = (a[...].astype(F32) + b[...].astype(F32)).astype(BF)


class Sums:
    def __init__(self, n, ctx, grads, fin, scratch, per=4, extra=EXTRA, hop=HOP):
        self.n, self.ctx, self.grads, self.fin = n, ctx, grads, fin
        self.per, self.hop = per, hop
        self.lots, self.pieces = per * TP, per * (TP + 2)
        self.all = self.pieces + extra
        (
            self.total, self.peer_in, self.pre, self.suf, self.suf_out, self.land,
            self.vec, self.vec_in,
            self.ys, self.yr, self.ps, self.pr, self.ss, self.sr, self.fs, self.fr,
            self.asend, self.arecv, self.own_sem, self.out_sem,
        ) = scratch[:20]
        self.fold_scratch = scratch[20:]
        self.replicas = n // TP
        self.f, self.c = lax.axis_index("fsdp"), lax.axis_index("ctx")
        f, c = self.f, self.c
        self.t, self.r = f % TP, f // TP
        self.core, self.side = self.t % 2, self.t // 2
        self.sib, self.par, self.cross = (flip1(f), c), (flip2(f), c), (flip2(flip1(f)), c)
        self.peers = [((f + TP * j) % n, c) for j in range(1, self.replicas)]
        self.left, self.right = (f, (c + ctx - 1) % ctx), (f, (c + 1) % ctx)
        self.links = Links(self.asend, self.arecv)

    @staticmethod
    def scratch(n, high, wide, columns, per=4, extra=EXTRA):
        replicas = n // TP
        lots, pieces = per * TP, per * (TP + 2)
        every = pieces + extra
        sems = pltpu.SemaphoreType.DMA
        peers = replicas - 1
        return [
            pltpu.VMEM((every, high, wide), BF),
            pltpu.VMEM((peers, pieces, high, wide), BF),
            pltpu.VMEM((every, high, wide), BF),
            pltpu.VMEM((every, high, wide), BF),
            pltpu.VMEM((RING, high, wide), BF),
            pltpu.VMEM((lots, high, wide), BF),
            pltpu.VMEM((3, VEC, LANES), F32),
            pltpu.VMEM((2 + peers, VEC, LANES), F32),
            sems((peers * pieces,)), sems((peers * pieces,)),
            sems((every,)), sems((every,)), sems((every,)), sems((every,)),
            sems((lots,)), sems((lots,)),
            sems(((len(columns) + 1) * (2 + peers),)), sems(((len(columns) + 1) * (2 + peers),)),
            sems((1,)), sems((every,)),
        ] + [
            one
            for wide_here in columns
            for one in (
                pltpu.VMEM((replicas, 2, 2, high, wide_here), BF),
                pltpu.VMEM((replicas, 2, high, wide_here), BF),
                pltpu.VMEM((replicas, high, wide_here), BF),
                pltpu.VMEM((peers, high, wide_here), BF),
            )
        ]

    def around(self):
        return [self.sib, self.par, self.cross] + self.peers + [self.left, self.right]

    def peer_copy(self, j, k):
        at = j * self.pieces + k
        return pltpu.make_async_remote_copy(
            src_ref=self.grads.at[(self.r + j + 1) % self.replicas, k],
            dst_ref=self.peer_in.at[j, k],
            send_sem=self.ys.at[at],
            recv_sem=self.yr.at[at],
            device_id=self.peers[j],
            device_id_type=MESH,
        )

    def own_copy(self):
        return pltpu.make_async_copy(
            self.grads.at[self.r], self.total.at[pl.ds(0, self.pieces)], self.own_sem.at[0]
        )

    def start(self):
        self.own_copy().start()
        for k in range(AHEAD):
            for j in range(self.replicas - 1):
                self.peer_copy(j, k).start()

    def pre_copy(self, k, src):
        return pltpu.make_async_remote_copy(
            src_ref=src.at[k], dst_ref=self.pre.at[k], send_sem=self.ps.at[k],
            recv_sem=self.pr.at[k], device_id=self.right, device_id_type=MESH,
        )

    def suf_copy(self, k, src):
        return pltpu.make_async_remote_copy(
            src_ref=src, dst_ref=self.suf.at[k], send_sem=self.ss.at[k],
            recv_sem=self.sr.at[k], device_id=self.left, device_id_type=MESH,
        )

    def out_copy(self, k, src):
        return pltpu.make_async_copy(src.at[k], self.fin.at[k], self.out_sem.at[k])

    def step(self, time, carry):
        self.tick(time)
        return carry

    def tick(self, time):
        c, ctx, total = self.c, self.ctx, self.total

        @pl.when(time + AHEAD < self.pieces)
        def _():
            for j in range(self.replicas - 1):
                self.peer_copy(j, time + AHEAD).start()

        @pl.when(time < self.pieces)
        def _():
            for j in range(self.replicas - 1):
                self.peer_copy(j, time).wait_recv()
                add_into(total.at[time], total.at[time], self.peer_in.at[j, time])

        k = time - self.hop * c

        @pl.when((k >= 0) & (k < self.all))
        def _():
            @pl.when(c > 0)
            def _():
                self.pre_copy(k, total).wait_recv()
                add_into(self.pre.at[k], self.pre.at[k], total.at[k])

                @pl.when(c < ctx - 1)
                def _():
                    self.pre_copy(k, self.pre).start()

            @pl.when(c == 0)
            def _():
                self.pre_copy(k, total).start()

        k2 = time - self.hop * (ctx - 1 - c)

        @pl.when((k2 >= 0) & (k2 < self.all))
        def _():
            @pl.when(c < ctx - 1)
            def _():
                self.suf_copy(k2, total.at[k2]).wait_recv()

            @pl.when((c > 0) & (c < ctx - 1))
            def _():
                @pl.when(k2 >= RING)
                def _():
                    self.suf_copy(k2 - RING, self.suf_out.at[(k2 - RING) % RING]).wait_send()

                add_into(self.suf_out.at[k2 % RING], self.suf.at[k2], total.at[k2])
                self.suf_copy(k2, self.suf_out.at[k2 % RING]).start()

            @pl.when(c == ctx - 1)
            def _():
                self.suf_copy(k2, total.at[k2]).start()

        k3 = time - self.hop * jnp.maximum(c, ctx - 1 - c)

        @pl.when((k3 >= 0) & (k3 < self.all))
        def _():
            @pl.when(c == 0)
            def _():
                add_into(self.suf.at[k3], self.suf.at[k3], total.at[k3])

            @pl.when((c > 0) & (c < ctx - 1))
            def _():
                add_into(self.suf.at[k3], self.suf.at[k3], self.pre.at[k3])

            @pl.when((k3 < self.lots) & (k3 // self.per != self.t))
            def _():
                @pl.when(c == ctx - 1)
                def _():
                    self.fin_copy_from(k3, self.pre).start()

                @pl.when(c < ctx - 1)
                def _():
                    self.fin_copy_from(k3, self.suf).start()

            @pl.when((k3 >= self.lots) | (k3 // self.per == self.t))
            def _():
                @pl.when(c == ctx - 1)
                def _():
                    self.out_copy(k3, self.pre).start()

                @pl.when(c < ctx - 1)
                def _():
                    self.out_copy(k3, self.suf).start()

    def fin_copy_from(self, k, src):
        return pltpu.make_async_remote_copy(
            src_ref=src.at[k], dst_ref=self.land.at[self.per * self.t + k % self.per], send_sem=self.fs.at[k],
            recv_sem=self.fr.at[self.per * self.t + k % self.per],
            device_id=(self.f - self.t + k // self.per, self.c), device_id_type=MESH,
        )

    @property
    def ticks(self):
        return self.all + self.hop * (self.ctx - 1)

    def close(self):
        c, ctx = self.c, self.ctx

        def arrive(k, carry):
            @pl.when(k // self.per != self.t)
            def _():
                pltpu.make_async_remote_copy(
                    src_ref=self.land.at[k], dst_ref=self.land.at[k], send_sem=self.fs.at[k],
                    recv_sem=self.fr.at[k], device_id=(self.f - self.t + k // self.per, c),
                    device_id_type=MESH,
                ).wait_recv()
                self.out_copy(k, self.land).start()
                self.fin_copy_from(k, self.suf).wait_send()

            return carry

        lax.fori_loop(0, self.lots, arrive, 0)

        def settle(k, carry):
            @pl.when(c < ctx - 1)
            def _():
                self.pre_copy(k, self.total).wait_send()

            @pl.when((c == ctx - 1) | ((c > 0) & (k >= self.all - RING)))
            def _():
                self.suf_copy(k, self.total.at[k]).wait_send()

            self.out_copy(k, self.suf).wait()
            return carry

        lax.fori_loop(0, self.all, settle, 0)

        def peers(k, carry):
            for j in range(self.replicas - 1):
                self.peer_copy(j, k).wait_send()
            return carry

        lax.fori_loop(0, self.pieces, peers, 0)
        self.links.drain()

    def place(self, column, value):
        wide = self.total.shape[-1]
        done = 0
        while done < value.shape[1]:
            piece, at = divmod(column + done, wide)
            count = min(wide - at, value.shape[1] - done)
            self.total[self.pieces + piece, : value.shape[0], at : at + count] = value[
                :, done : done + count
            ]
            done += count


class Fold:
    def __init__(self, sums, index, column):
        self.sums, self.column = sums, column
        self.own, self.got_core, self.got_par, self.got_ring = sums.fold_scratch[
            4 * index : 4 * index + 4
        ]
        replicas, r = sums.replicas, sums.r
        self.src_core = self.own.at[:, :, 1 - sums.core]
        self.mine_core = [
            [self.own.at[k, s, sums.core] for s in range(2)] for k in range(replicas)
        ]
        self.src_par = self.got_core.at[:, 1 - sums.side]
        self.mine_par = [self.got_core.at[k, sums.side] for k in range(replicas)]
        self.src_ring = [
            self.got_par.at[(r + j + 1) % replicas] for j in range(replicas - 1)
        ]
        self.mine = self.got_par.at[r]

    def set(self, k, value):
        self.own[k // TP, (k // 2) % 2, k % 2] = value.astype(BF)

    def over_core(self):
        self.at = self.sums.links.put(self.src_core, self.got_core, self.sums.sib)

    def over_x(self):
        links = self.sums.links
        links.arrive(self.at, self.got_core)
        for k, pair in enumerate(self.mine_core):
            for s, mine in enumerate(pair):
                add_into(self.got_core.at[k, s], self.got_core.at[k, s], mine)
        self.at = links.put(self.src_par, self.got_par, self.sums.par)

    def over_y(self):
        links = self.sums.links
        links.arrive(self.at, self.got_par)
        for k, mine in enumerate(self.mine_par):
            add_into(self.got_par.at[k], self.got_par.at[k], mine)
        self.ats = [
            links.put(src, self.got_ring.at[j], peer)
            for j, (src, peer) in enumerate(zip(self.src_ring, self.sums.peers))
        ]

    def finish(self):
        for j, at in enumerate(self.ats):
            self.sums.links.arrive(at, self.got_ring.at[j])
            add_into(self.mine, self.mine, self.got_ring.at[j])
        self.sums.place(self.column, self.mine[...])


class FoldVectors:
    def __init__(self, sums, column):
        self.sums, self.column = sums, column

    def over_core(self):
        sums = self.sums
        self.at = sums.links.put(sums.vec.at[0], sums.vec_in.at[0], sums.sib)

    def over_x(self):
        sums = self.sums
        sums.links.arrive(self.at, sums.vec_in.at[0])
        sums.vec[1] = sums.vec[0] + sums.vec_in[0]
        self.at = sums.links.put(sums.vec.at[1], sums.vec_in.at[1], sums.par)

    def over_y(self):
        sums = self.sums
        sums.links.arrive(self.at, sums.vec_in.at[1])
        sums.vec[2] = sums.vec[1] + sums.vec_in[1]
        self.ats = [
            sums.links.put(sums.vec.at[2], sums.vec_in.at[2 + j], peer)
            for j, peer in enumerate(sums.peers)
        ]

    def finish(self):
        sums = self.sums
        vec = sums.vec[2]
        for j, at in enumerate(self.ats):
            sums.links.arrive(at, sums.vec_in.at[2 + j])
            vec = vec + sums.vec_in[2 + j]
        sums.place(self.column, vec.astype(BF))


def fold_columns(width, proj):
    pairs = HQ // 2
    early = (pairs // 2 + 1) * LANES
    sizes = (width, early, HQ * HD - early, proj - HQ * HD)
    return sizes, (0, width, width + early)


class Plain:
    def __init__(self, own):
        self.own = own

    def set(self, k, value):
        self.own[k // TP, (k // 2) % 2, k % 2] = value.astype(BF)

    def over_core(self):
        pass

    over_x = over_y = finish = over_core


def backward_kernel(size, merged, order, lens, gain_attn, gain_mlp, freq, *rest):
    n, micro, rows, ctx = size
    hbm, rest = rest[:11], rest[11:]
    out_par, grads, dx, outputs = rest[:4]
    rest = rest[4:]
    outs = 1 if merged else 5
    fin, rest = rest[:outs], rest[outs:]
    (
        x2, gh2, gy, wo, x, obt, kv, qs, lse, wq, out, staged_sems,
        out_in, out_send, out_recv, cos_ref, sin_ref, bias_ref, kvar, kvar_turned, vvar,
        go_ref, gp, h1t, gk, gv, part, land, vec_wide, send, recv,
    ), rest = rest[:31], rest[31:]
    staged = Staged(
        list(zip(hbm, (x2, gh2, gy, wo, x, obt, kv, qs, lse, wq, out))), staged_sems
    )
    group = HQ // KVH
    pairs = HQ // 2
    width = HQ * HD
    high = width // n
    proj = wq.shape[1]
    scale = 1.0 / math.sqrt(HD)
    f, c = lax.axis_index("fsdp"), lax.axis_index("ctx")
    others = [(f, (c + j) % ctx) for j in range(1, ctx)]
    back = [(c - j + ctx) % ctx for j in range(1, ctx)]
    sizes, starts = fold_columns(width, proj)
    if merged:
        sums = Sums(n, ctx, grads, fin[0], rest)
        enter(others + sums.around())
        sums.start()
        last = (ALL_PIECES - PIECES - 1) * sums.total.shape[-1]
        folds = [Fold(sums, k, start) for k, start in enumerate(starts + (last,))]
        fold_v = FoldVectors(sums, last + sizes[3])
    else:
        enter(others + [(flip2(f), c)])
        folds = [Plain(own) for own in fin[:4]]
        fold_v = Plain(None)
    fold_o, fold_a, fold_b, fold_k = folds
    out_links = Links(out_send, out_recv)
    out_at = out_links.put(out_par, out_in, (flip2(f), c))
    links = Links(send, recv)
    ticks = [0]

    def advance(upto):
        if merged and upto > ticks[0]:
            lax.fori_loop(ticks[0], upto, sums.step, 0)
            ticks[0] = upto

    if merged:
        for k in range(PIECES, ALL_PIECES):
            sums.total[k] = jnp.zeros(sums.total.shape[1:], BF)
        sums.own_copy().wait()
    for m in range(micro):
        fill_tables(m, rows, c, freq, order, lens, cos_ref, sin_ref)
        advance(EARLY * (m + 1) // micro)
        staged.need(5)
        stream = x2[m]
        inverse = inverse_norm(stream)
        normed = stream * inverse
        grad = gh2[m]
        term = jnp.sum(grad * normed, axis=0, keepdims=True)
        at = proj + width
        vec_wide[:, at : at + width] = term if m == 0 else vec_wide[:, at : at + width] + term
        grad = grad * gain_mlp[...]
        grad = gy[m].astype(F32) + inverse * (
            grad - normed * jnp.mean(grad * normed, axis=1, keepdims=True)
        )
        dx[m] = grad
        spread = dot_nt(grad.astype(BF), wo[...]).astype(BF)
        for p in range(pairs):
            go_ref[m, p] = spread[:, p * LANES : (p + 1) * LANES]
        stream = x[m].astype(F32)
        h1t[:, m * rows : (m + 1) * rows] = (
            (stream * inverse_norm(stream) * gain_attn[...]).T.astype(BF)
        )
    staged.need(len(staged.copies))
    for k in range(n):
        term = dot(obt[0, k * high : (k + 1) * high, :], dx[0].astype(BF))
        for m in range(1, micro):
            term = term + dot(obt[m, k * high : (k + 1) * high, :], dx[m].astype(BF))
        fold_o.set(k, term)
    fold_o.over_core()

    def columns(fold, lo, hi):
        for k in range(n):
            fold.set(k, dot(h1t[k * high : (k + 1) * high, :], gp[:, lo:hi]))

    low = lax.broadcasted_iota(jnp.int32, (ctx * rows, LANES), 1) < HD
    mid = pairs // 2
    part_src = [
        [[part.at[m, g, other[1]] for other in others] for g in range(KVH)] for m in range(micro)
    ]
    part_dst = [[land.at[m, g, c] for g in range(KVH)] for m in range(micro)]
    arrivals = [[None] * KVH for _ in range(micro)]

    def send_group(m, g):
        keys = gk[g, 0] + pltpu.roll(gk[g, 1], HD, 1)
        values = pltpu.roll(gv[g, 0], HD, 1) + gv[g, 1]
        whole = jnp.where(low, keys, values).astype(BF)
        part[m, g] = whole.reshape(ctx, rows, LANES)
        arrivals[m][g] = [
            links.put(src, part_dst[m][g], other) for src, other in zip(part_src[m][g], others)
        ]

    for m in range(micro):
        fill_bias(m, rows, c, order, lens, bias_ref)
        both = kv[m].reshape(ctx * rows, 2 * LANES).astype(F32)
        fill_heads(both[:, :LANES], kvar)
        fill_heads_turned(both[:, :LANES], kvar_turned)
        fill_heads(both[:, LANES:], vvar)
        gk[...] = jnp.zeros_like(gk)
        gv[...] = jnp.zeros_like(gv)
        cosine = cos_ref[m * rows : (m + 1) * rows, :]
        sine = sin_ref[m * rows : (m + 1) * rows, :]

        def pair(p, carry):
            query = qs[m, p]
            go = go_ref[m, p]
            grad_query = jnp.zeros((LANES, rows), F32)
            for parity in range(2):
                head = 2 * p + parity
                g = head // group
                scores = dot_nt(kvar[g, parity], query) + bias_ref[...]
                probs = jnp.exp(scores - lse[m, pl.ds(head, 1), :])
                grad_probs = dot_nt(vvar[g, parity], go)
                delta = jnp.sum(probs * grad_probs, axis=0, keepdims=True)
                grad_scores = (probs * (grad_probs - delta)).astype(BF)
                grad_query = grad_query + dot(kvar_turned[g, parity], grad_scores)
                gk[g, parity] += dot(grad_scores, query)
                gv[g, parity] += dot(probs.astype(BF), go)
            turned = grad_query.T * scale
            turned = turned * cosine - swap_halves(turned) * sine
            at = pl.multiple_of(p * LANES, LANES)
            gp[m * rows : (m + 1) * rows, pl.ds(at, LANES)] = turned.astype(BF)

            if m == 0:
                pl.when(p == 0)(fold_o.over_x)

            @pl.when(p == mid)
            def _():
                send_group(m, 0)
                if m == micro - 1:
                    columns(fold_a, 0, sizes[1])
                    fold_a.over_core()
                elif m == 0:
                    fold_o.over_y()

            if m == micro - 1:
                pl.when(p == mid + 1)(fold_a.over_x)

            @pl.when(p == pairs - 1)
            def _():
                send_group(m, 1)
                if m == micro - 1:
                    fold_a.over_y()

            if merged:
                step = m * pairs + p
                lax.fori_loop(
                    EARLY + RATE * step // 4, EARLY + RATE * (step + 1) // 4, sums.step, 0
                )
            return carry

        lax.fori_loop(0, pairs, pair, 0)
    ticks[0] = EARLY + RATE * micro * pairs // 4
    spare = max(0, PIECES - ticks[0])
    first = ticks[0]
    columns(fold_b, sizes[1], width)
    fold_b.over_core()
    advance(first + spare * 2 // 8)
    fold_b.over_x()
    advance(first + spare * 4 // 8)
    for m in range(micro):
        totals = []
        for g in range(KVH):
            total = part[m, g, c].astype(F32)
            for at, source in zip(arrivals[m][g], back):
                links.arrive(at, land.at[m, g, source])
                total = total + land[m, g, source].astype(F32)
            totals.append(total)
        lower = lax.broadcasted_iota(jnp.int32, (rows, LANES), 1) < HD
        cosine = cos_ref[m * rows : (m + 1) * rows, :]
        sine = sin_ref[m * rows : (m + 1) * rows, :]
        grad_keys = jnp.where(lower, totals[0], pltpu.roll(totals[1], HD, 1))
        grad_keys = grad_keys * cosine - swap_halves(grad_keys) * sine
        gp[m * rows : (m + 1) * rows, width : width + LANES] = grad_keys.astype(BF)
        grad_values = jnp.where(lower, pltpu.roll(totals[0], HD, 1), totals[1])
        gp[m * rows : (m + 1) * rows, width + LANES :] = grad_values.astype(BF)
    columns(fold_k, width, proj)
    fold_k.over_core()
    advance(first + spare * 5 // 8)
    fold_b.over_y()
    for m in range(micro):
        grad_project = gp[m * rows : (m + 1) * rows, :]
        stream = x[m].astype(F32)
        inverse = inverse_norm(stream)
        normed = stream * inverse
        term = jnp.sum(grad_project.astype(F32), axis=0, keepdims=True)
        vec_wide[:, :proj] = term if m == 0 else vec_wide[:, :proj] + term
        grad = dot_nt(grad_project, wq[...])
        term = jnp.sum(grad * normed, axis=0, keepdims=True)
        at = slice(proj, proj + width)
        vec_wide[:, at] = term if m == 0 else vec_wide[:, at] + term
        grad = grad * gain_attn[...]
        dx[m] = dx[m] + inverse * (
            grad - normed * jnp.mean(grad * normed, axis=1, keepdims=True)
        )
    vec = sums.vec.at[0] if merged else fin[4]
    vec[...] = jnp.zeros((VEC, LANES), F32)
    for k in range(vec_wide.shape[1] // LANES):
        vec[k : k + 1, :] = vec_wide[:, k * LANES : (k + 1) * LANES]
    fold_v.over_core()
    fold_k.over_x()
    advance(first + spare * 6 // 8)
    fold_v.over_x()
    fold_o.finish()
    fold_a.finish()
    advance(first + spare * 7 // 8)
    fold_k.over_y()
    fold_v.over_y()
    advance(first + spare)
    out_links.arrive(out_at, out_in)
    for m in range(micro):
        outputs[m] = (x2[m] + out[m] + out_in[m].astype(F32)).astype(BF)
    out_links.drain()
    fold_b.finish()
    advance(ALL_PIECES - 1)
    fold_k.finish()
    fold_v.finish()
    if merged:
        advance(sums.ticks)
        sums.close()
    links.drain()


def attention_backward(
    n, ctx, order, lens, gh2, x2, gy, x, wq, wo, gain_attn, gain_mlp, freq, qs, kv, lse, obt,
    out, out_par, grads,
):
    micro, rows, width = x.shape
    keys = rows * ctx
    proj = wq.shape[1]
    replicas = n // TP
    high, wide = grads.shape[2:]
    merged = ctx <= 4
    vmem = pl.BlockSpec(memory_space=pltpu.VMEM)
    smem = pl.BlockSpec(memory_space=pltpu.SMEM)
    anywhere = pl.BlockSpec(memory_space=pl.ANY)
    copies = micro * KVH * (ctx - 1)
    sizes, _ = fold_columns(width, proj)
    out_shape = [
        jax.ShapeDtypeStruct((micro, rows, width), F32),
        jax.ShapeDtypeStruct((micro, rows, width), BF),
    ]
    if merged:
        out_shape += [jax.ShapeDtypeStruct((ALL_PIECES, high, wide), BF)]
    else:
        out_shape += [
            jax.ShapeDtypeStruct((replicas, 2, 2, high, size), BF) for size in sizes
        ] + [jax.ShapeDtypeStruct((VEC, LANES), F32)]
    operands = (x2, gh2, gy, wo, x, obt, kv, qs, lse, wq, out)
    result = pl.pallas_call(
        functools.partial(backward_kernel, (n, micro, rows, ctx), merged),
        out_shape=out_shape,
        in_specs=[smem, smem] + [vmem] * 3 + [anywhere] * 13,
        out_specs=[vmem] * 2 + ([anywhere] if merged else [vmem] * 5),
        scratch_shapes=[pltpu.VMEM(one.shape, one.dtype) for one in operands]
        + [
            pltpu.SemaphoreType.DMA((len(operands),)),
            pltpu.VMEM((micro, rows, width), BF),
            pltpu.SemaphoreType.DMA((1,)),
            pltpu.SemaphoreType.DMA((1,)),
            pltpu.VMEM((micro * rows, LANES), F32),
            pltpu.VMEM((micro * rows, LANES), F32),
            pltpu.VMEM((keys, rows), F32),
            pltpu.VMEM((KVH, 2, keys, LANES), BF),
            pltpu.VMEM((KVH, 2, LANES, keys), BF),
            pltpu.VMEM((KVH, 2, keys, LANES), BF),
            pltpu.VMEM((micro, HQ // 2, rows, LANES), BF),
            pltpu.VMEM((micro * rows, proj), BF),
            pltpu.VMEM((width, micro * rows), BF),
            pltpu.VMEM((KVH, 2, keys, LANES), F32),
            pltpu.VMEM((KVH, 2, keys, LANES), F32),
            pltpu.VMEM((micro, KVH, ctx, rows, LANES), BF),
            pltpu.VMEM((micro, KVH, ctx, rows, LANES), BF),
            pltpu.VMEM((1, proj + 2 * width), F32),
            pltpu.SemaphoreType.DMA((copies,)),
            pltpu.SemaphoreType.DMA((copies,)),
        ]
        + (Sums.scratch(n, high, wide, sizes) if merged else []),
        compiler_params=pltpu.CompilerParams(
            collective_id=3, has_side_effects=True, vmem_limit_bytes=VMEM_LIMIT
        ),
        name="attention_backward",
    )(order, lens, gain_attn, gain_mlp, freq, *operands, out_par, grads)
    if merged:
        return result
    dx, outputs, *parts, vec = result
    return dx, outputs, reduce_grads(n, ctx, grads, parts, vec)


def reduce_kernel(n, ctx, grads, *rest):
    parts, vec, fin, scratch = rest[:4], rest[4], rest[5], rest[6:]
    sums = Sums(n, ctx, grads, fin, scratch)
    enter(sums.around())
    sums.start()
    sums.vec[0] = vec[...]
    for k in range(PIECES, ALL_PIECES):
        sums.total[k] = jnp.zeros(sums.total.shape[1:], BF)
    sums.own_copy().wait()
    sizes = [part.shape[-1] for part in parts]
    last = (ALL_PIECES - PIECES - 1) * sums.total.shape[-1]
    folds = [
        Fold(sums, k, start)
        for k, start in enumerate((0, sizes[0], sizes[0] + sizes[1], last))
    ] + [FoldVectors(sums, last + sizes[3])]
    for fold, part in zip(folds, parts):
        fold.own[...] = part[...]
    for stage in ("over_core", "over_x", "over_y", "finish"):
        for fold in folds:
            getattr(fold, stage)()
    lax.fori_loop(0, sums.ticks, sums.step, 0)
    sums.close()


def reduce_grads(n, ctx, grads, parts, vec):
    high, wide = grads.shape[2:]
    vmem = pl.BlockSpec(memory_space=pltpu.VMEM)
    anywhere = pl.BlockSpec(memory_space=pl.ANY)
    return pl.pallas_call(
        functools.partial(reduce_kernel, n, ctx),
        out_shape=jax.ShapeDtypeStruct((ALL_PIECES, high, wide), BF),
        in_specs=[anywhere] + [vmem] * 5,
        out_specs=anywhere,
        scratch_shapes=Sums.scratch(n, high, wide, [part.shape[-1] for part in parts]),
        compiler_params=pltpu.CompilerParams(
            collective_id=4, has_side_effects=True, vmem_limit_bytes=VMEM_LIMIT
        ),
        name="reduce_grads",
    )(grads, *parts, vec)


def finish_kernel(
    size, sets, dx, outputs, *rest
):
    n, units, padded, proj, width = size
    fins, rest = rest[: len(sets)], rest[len(sets) :]
    (
        g_gu, g_down, g_qkv, g_out, g_qk, g_v, g_attn, g_mlp, dx_out, outputs_out,
        turn, vecs, dx_in, outputs_in, sems,
    ) = rest
    fin = fins[-1]
    replicas = n // TP
    high = width // n
    through = [(dx, dx_in, dx_out), (outputs, outputs_in, outputs_out)]
    coming = [
        pltpu.make_async_copy(src, buf, sems.at[k]) for k, (src, buf, _) in enumerate(through)
    ]
    going = [
        pltpu.make_async_copy(buf, dst, sems.at[2 + k]) for k, (_, buf, dst) in enumerate(through)
    ]
    for copy in coming:
        copy.start()
    f = lax.axis_index("fsdp")
    vec = fin.at[ALL_PIECES - 1]
    lane = proj - width
    rows = vec[0:VEC, lane : lane + LANES].astype(F32)
    vecs[...] = rows
    for first, ref in ((0, g_qk), (width + LANES, g_v), (proj, g_attn), (proj + width, g_mlp)):
        count = ref.shape[-1]
        at = first + f * count
        row = at // LANES
        pair = jnp.concatenate(
            [vecs[pl.ds(row, 1), :], vecs[pl.ds(row + 1, 1), :]], axis=1
        )
        pair = jnp.broadcast_to(pair, (8, 2 * LANES))
        ref[...] = pltpu.roll(pair, 2 * LANES - (at - row * LANES), 1)[0:1, :count]
    for a, b in zip(coming, going):
        a.wait()
        b.start()
    for half in range(2):
        for k in range(TP):
            wholes = []
            for ref, (per, count) in zip(fins, sets):
                first = per * k + half * (per // 2)
                whole = [ref[first + q].astype(F32) for q in range(per // 2)]
                wholes.append(whole[0] if len(whole) == 1 else jnp.concatenate(whole, axis=1))
            for q in range(replicas):
                tiles = []
                for whole, (per, count) in zip(wholes, sets):
                    for j in range(count):
                        lane = (j * replicas + q) * LANES
                        tiles.append(whole[:, lane : lane + LANES])
                at = ((half * replicas + q) * TP + k) * units
                g_gu[:, at : at + units] = jnp.concatenate(tiles, axis=1)[:, :units]
    done = 0
    for ref, (per, count) in zip(fins, sets):
        blocks = 2 * replicas // per
        for k in range(n):
            lane = (k % blocks) * count * LANES
            turn[k * high : (k + 1) * high, done : done + count * LANES] = ref[
                per * TP + k // blocks, :, lane : lane + count * LANES
            ].astype(F32)
        done += count * LANES
    g_down[...] = turn[...].T[:units, :]
    ahead = ALL_PIECES - PIECES - 1
    whole = jnp.concatenate([fin[PIECES + k] for k in range(ahead)], axis=1)
    g_out[...] = whole[:, :width].astype(F32)
    g_qkv[:, :width] = whole[:, width : 2 * width].astype(F32)
    g_qkv[:, width:] = fin[ALL_PIECES - 1, :, : proj - width].astype(F32)
    for copy in going:
        copy.wait()


def finish_grads(n, dx, outputs, fins, units, padded, proj, width):
    high = width // n
    vmem = pl.BlockSpec(memory_space=pltpu.VMEM)
    anywhere = pl.BlockSpec(memory_space=pl.ANY)
    one = lambda count: jax.ShapeDtypeStruct((1, count), F32)
    return pl.pallas_call(
        functools.partial(
            finish_kernel, (n, units, padded, proj, width), [one[1:] for one in fins]
        ),
        out_shape=(
            jax.ShapeDtypeStruct((high, 2 * n * units), F32),
            jax.ShapeDtypeStruct((units, width), F32),
            jax.ShapeDtypeStruct((high, proj), F32),
            jax.ShapeDtypeStruct((high, width), F32),
            one((width + LANES) // n),
            one(LANES // n),
            one(high),
            one(high),
            jax.ShapeDtypeStruct(dx.shape, dx.dtype),
            jax.ShapeDtypeStruct(outputs.shape, outputs.dtype),
        ),
        in_specs=[anywhere, anywhere] + [vmem] * len(fins),
        out_specs=[vmem] * 8 + [anywhere] * 2,
        scratch_shapes=[
            pltpu.VMEM((width, padded), F32),
            pltpu.VMEM((VEC, LANES), F32),
            pltpu.VMEM(dx.shape, dx.dtype),
            pltpu.VMEM(outputs.shape, outputs.dtype),
            pltpu.SemaphoreType.DMA((4,)),
        ],
        compiler_params=pltpu.CompilerParams(vmem_limit_bytes=VMEM_LIMIT),
        name="finish_grads",
    )(dx, outputs, *[one[0] for one in fins])


def pad_to(v, axis, size):
    pads = [(0, 0)] * v.ndim
    pads[axis] = (0, size - v.shape[axis])
    return jnp.pad(v, pads)


def local(
    inputs, cotangent, lengths, order, w_qkv, b_qkv, w_out, norm_attn, norm_mlp, w_gate_up, w_down
):
    n = lax.axis_size("fsdp")
    ctx = lax.axis_size("ctx")
    replicas = n // TP
    x, gy = inputs[0], cotangent[0]
    micro, rows, width = x.shape
    high = w_gate_up.shape[0]
    units = w_down.shape[0]
    padded = -(-units // LANES) * LANES
    quarter = replicas * padded
    proj = w_qkv.shape[1]

    small = jnp.concatenate(
        [
            pad_to(b_qkv, 0, 2 * LANES).reshape(2, LANES),
            pad_to(norm_attn, 0, LANES)[None],
            pad_to(norm_mlp, 0, LANES)[None],
            jnp.zeros((12, LANES), BF),
        ]
    )
    half = HD // 2
    freqs = np.power(np.float32(ROPE_BASE), -(np.arange(half, dtype=np.float32) * (2.0 / HD)))
    freq = jnp.asarray(np.tile(freqs.astype(np.float32), (8, LANES // half)))
    if ctx <= 4 and high % 16 == 0 and units % 32 == 0:
        (
            h2, x2, qs, kv, lse, obt, wq_all, wo_all, gain_attn, gain_mlp, wgu_t, wd_t, gd_all,
        ) = gather_and_attend(
            n, ctx, order[0], lengths[0], x, w_qkv, w_out, small, w_gate_up, w_down, gy, freq,
            padded,
        )
        wq_all = wq_all.reshape(width, proj)
        wo_all = wo_all.reshape(width, width)
    else:
        wgu = w_gate_up.reshape(high, 2, replicas, TP, units)
        wgu = pad_to(wgu.transpose(3, 1, 0, 2, 4), 4, padded).reshape(TP, 2, high, quarter)
        wq_all, wo_all, sm_all, wgu_t, wd_t, gd_all = gather_weights(
            n, w_qkv, w_out, small, wgu, pad_to(w_down, 0, padded), gy
        )
        wq_all = wq_all.reshape(width, proj)
        wo_all = wo_all.reshape(width, width)
        bias = sm_all[:, :2].reshape(n, 2 * LANES)[:, : b_qkv.shape[0]].reshape(1, proj)
        gain_attn = sm_all[:, 2, :high].reshape(1, width).astype(F32)
        gain_mlp = sm_all[:, 3, :high].reshape(1, width).astype(F32)
        h2, x2, qs, kv, lse, obt = attention_forward(
            ctx, order[0], lengths[0], x, wq_all, wo_all, bias.astype(F32), gain_attn, gain_mlp,
            freq,
        )
    wgu_t = wgu_t.reshape(2, width, quarter)
    wd_t = wd_t.reshape(quarter, width)
    out, out_par, gh2, grads, fins, count = mlp(n, ctx, h2, gd_all, wgu_t, wd_t)
    dx, outputs, fin = attention_backward(
        n, ctx, order[0], lengths[0], gh2, x2, gy, x, wq_all, wo_all, gain_attn, gain_mlp, freq,
        qs, kv, lse, obt, out, out_par, grads,
    )
    g_gu, g_down, g_qkv, g_out, g_qk, g_v, g_attn, g_mlp, dx, outputs = finish_grads(
        n, dx, outputs, fins + [(fin, 4, count)], units, padded, proj, width
    )
    return (
        outputs[None],
        dx[None],
        g_qkv,
        g_qk[0],
        g_v[0],
        g_out,
        g_attn[0],
        g_mlp[0],
        g_gu,
        g_down,
    )


def solution(mesh):
    return jax.shard_map(
        local,
        mesh=mesh,
        in_specs=(
            P("fsdp", None, "ctx", None),
            P("fsdp", None, "ctx", None),
            P("fsdp", None, None),
            P("fsdp", None, None),
            P("fsdp", None),
            P("fsdp"),
            P("fsdp", None),
            P("fsdp"),
            P("fsdp"),
            P("fsdp", None),
            P("fsdp", None),
        ),
        out_specs=(
            P("fsdp", None, "ctx", None),
            P("fsdp", None, "ctx", None),
            P("fsdp", None),
            P("fsdp"),
            P("fsdp"),
            P("fsdp", None),
            P("fsdp"),
            P("fsdp"),
            P("fsdp", None),
            P("fsdp", None),
        ),
        check_vma=False,
    )
```
